32 devices in a mesh: row: 8 (over y, x, core), col: 4 (over z).
Axes of the slice: x: 2, y: 2, z: 4, core: 2. Of those that a mesh axis runs over, the one named last changes fastest.
Arguments:
- object_field: float32 [2, 2048, 2048], P(None, 'row', 'col'), may hold values from -6 to 6
- probe: float32 [2, 4, 256, 256], replicated, may hold values from -3 to 3
- amplitudes: float32 [8, 4, 6, 256, 256], P('row', 'col'), may hold values from 0.25 to 4
- corners: int32 [8, 4, 6, 2], P('row', 'col'), may hold values from 0 to 1792, as said below
- counts: int32 [8, 4], replicated, may hold values from 1 to 6, as said below
Outputs:
- object_new: float32 [2, 2048, 2048], P(None, 'row', 'col')
- probe_new: float32 [2, 4, 256, 256], replicated
The draws below stay inside these ranges and needn't reach their ends.
Inputs may be any that keep to these rules, and one draw needn't show every extreme that they name: counts[i, j] live slots on the tile at row i, column j; the later slots of that tile hold unused data; some tile has exactly 6. `corners`: each slot's corner lies inside the tile of the slot; every patch of 256 x 256 cells lies inside the object.
All inputs are finite; a program needn't handle non-finite values.
Results may differ from the reference program's by a relative error of at most 0.0013.
Values sent between devices are 32-bit elements; how exact they have to be, the bound alone decides.
No kernel may reach another device: no remote copies, remote signals or barrier semaphores. Data moves between devices by JAX's collectives and lax.ppermute only.
A program may use at most 64 MiB of HBM per device.

```python
import math
import jax
import jax.numpy as jnp
from jax import lax

W = 256
MODES = 4
TR = 256
TC = 512
CAP = 6
NR = 2048
NC = 2048
N_ROW = 8
N_COL = 4


def draw_counts(key, part):
    key = jax.random.fold_in(key, 11)
    first, second, third, fourth = jax.random.split(key, 4)
    dense = jax.random.randint(first, (N_ROW, N_COL), CAP // 2, CAP + 1)
    sparse = jax.random.randint(second, (N_ROW, N_COL), 1, CAP // 2 + 1)
    light_tile = jax.random.randint(third, (N_ROW, N_COL), 0, 10) < 3
    chosen = jnp.where(light_tile, sparse, dense)
    picked = jax.random.randint(fourth, (), 0, N_ROW * N_COL)
    flat = jnp.arange(N_ROW * N_COL, dtype=jnp.int32).reshape(N_ROW, N_COL)
    return jnp.where(flat == picked, CAP, chosen).astype(jnp.int32)


def draw_corners(key, part):
    key = jax.random.fold_in(key, 23)
    first, second = jax.random.split(key)
    tile_row = jnp.arange(N_ROW, dtype=jnp.int32)[:, None, None]
    tile_col = jnp.arange(N_COL, dtype=jnp.int32)[None, :, None]
    row_span = jnp.where(tile_row == N_ROW - 1, TR - W + 1, TR)
    col_span = jnp.where(tile_col == N_COL - 1, TC - W + 1, TC)
    row_span = jnp.broadcast_to(row_span, (N_ROW, N_COL, CAP))
    col_span = jnp.broadcast_to(col_span, (N_ROW, N_COL, CAP))
    row_bits = jax.random.randint(first, (N_ROW, N_COL, CAP), 0, 2 ** 30)
    col_bits = jax.random.randint(second, (N_ROW, N_COL, CAP), 0, 2 ** 30)
    row_at = row_bits % row_span + tile_row * TR
    col_at = col_bits % col_span + tile_col * TC
    return jnp.stack([row_at, col_at], axis=-1).astype(jnp.int32)


def levels(rng, dims, shards, smallest, top_value):
    level = 1.0
    for position, parts in shards:
        heights = jax.random.uniform(jax.random.fold_in(jax.random.fold_in(rng, 6), position), (parts,), jnp.float32, smallest / len(shards), top_value / len(shards))
        level = level * jnp.repeat(jnp.exp(heights), dims[position] // parts).reshape((-1,) + (1,) * (len(dims) - 1 - position))
    return level


def scatter_about(rng, extent, width, limit, cuts=(), held_as=jnp.bfloat16):
    factor_of = levels(rng, extent, cuts, -0.22, 0.18) if cuts else 1.0
    entries = jax.random.normal(rng, extent, jnp.float32) * width * factor_of
    return jnp.minimum(jnp.maximum(entries, -limit), limit).astype(held_as)


def setup_inputs(seed: int = 0) -> dict:
    key_list = jax.random.split(jax.random.key(seed), 6)
    object_field = scatter_about(key_list[0], (2, NR, NC), 1.0, 6.0, ((1, 8), (2, 4)), jnp.float32)
    probe = scatter_about(key_list[1], (2, MODES, W, W), 0.5, 3.0, (), jnp.float32)
    amplitudes = jnp.clip(jnp.exp(math.log(4.0) - 2.7725887 * jax.random.uniform(key_list[2], (N_ROW, N_COL, CAP, W, W), jnp.float32) ** levels(key_list[2], (N_ROW, N_COL, CAP, W, W), ((0, 8), (1, 4)), -0.2, 0.2)), 0.25, 4.0)
    corners = draw_corners(jax.random.fold_in(key_list[5], 71), 0)
    counts = draw_counts(jax.random.fold_in(key_list[5], 71), 0)
    return dict(object_field=object_field, probe=probe, amplitudes=amplitudes, corners=corners, counts=counts)


def tables(pattern_side):
    index = jnp.arange(pattern_side, dtype=jnp.int32)
    product = index[:, None] * index[None, :] % pattern_side
    angle = product.astype(jnp.float32) * (2.0 * math.pi / pattern_side)
    scale = 1.0 / math.sqrt(pattern_side)
    return ((jnp.cos(angle) * scale).astype(jnp.bfloat16), (-jnp.sin(angle) * scale).astype(jnp.bfloat16))

def left_mul(table, values):
    return jnp.einsum('ab,mbc->mac', table.astype(jnp.float32), values.astype(jnp.float32), precision=lax.Precision.HIGHEST)

def right_mul(values, table):
    return jnp.einsum('mab,bc->mac', values.astype(jnp.float32), table.astype(jnp.float32), precision=lax.Precision.HIGHEST)

def transform(real_part, imag_part, table_re, table_im):
    rows_re = (left_mul(table_re, real_part) - left_mul(table_im, imag_part)).astype(jnp.bfloat16)
    rows_im = (left_mul(table_re, imag_part) + left_mul(table_im, real_part)).astype(jnp.bfloat16)
    out_re = right_mul(rows_re, table_re) - right_mul(rows_im, table_im)
    out_im = right_mul(rows_im, table_re) + right_mul(rows_re, table_im)
    return (out_re, out_im)

def process(window, amplitude, probe, table_re, table_im):
    probe_re, probe_im = (probe[0], probe[1])
    win_re, win_im = (window[0], window[1])
    psi_re = (probe_re * win_re - probe_im * win_im).astype(jnp.bfloat16)
    psi_im = (probe_re * win_im + probe_im * win_re).astype(jnp.bfloat16)
    wave_re, wave_im = transform(psi_re, psi_im, table_re, table_im)
    model = lax.optimization_barrier(jnp.sum(wave_re * wave_re + wave_im * wave_im, axis=0))
    factor = amplitude / jnp.sqrt(jnp.maximum(model, 1.0)) - 1.0
    target_re = (wave_re * factor).astype(jnp.bfloat16)
    target_im = (wave_im * factor).astype(jnp.bfloat16)
    chi_re, chi_im = transform(target_re, target_im, table_re, -table_im)
    grad_re = lax.optimization_barrier(jnp.sum(probe_re * chi_re + probe_im * chi_im, axis=0))
    grad_im = lax.optimization_barrier(jnp.sum(probe_re * chi_im - probe_im * chi_re, axis=0))
    pgrad_re = win_re * chi_re + win_im * chi_im
    pgrad_im = win_re * chi_im - win_im * chi_re
    return (jnp.stack([grad_re, grad_im]), jnp.stack([pgrad_re, pgrad_im]), win_re * win_re + win_im * win_im)

def reference(object_field, probe, amplitudes, corners, counts):
    pattern_side = probe.shape[-1]
    table_re, table_im = tables(pattern_side)
    slots = amplitudes.shape[2]
    measured = amplitudes.reshape(-1, pattern_side, pattern_side)
    spots = corners.reshape(-1, 2)
    live = (jnp.arange(slots, dtype=jnp.int32)[None, None, :] < counts[:, :, None]).reshape(-1)
    order = jnp.argsort(jnp.where(live, 0, 1).astype(jnp.int32), stable=True).astype(jnp.int32)
    total = jnp.sum(live.astype(jnp.int32)).astype(jnp.int32)
    lighting = lax.optimization_barrier(jnp.sum(probe[0] * probe[0] + probe[1] * probe[1], axis=0))
    zero_index = jnp.zeros((), jnp.int32)
    accumulated = jnp.zeros((3,) + object_field.shape[1:], jnp.float32)
    probe_grad = jnp.zeros(probe.shape, jnp.float32)
    probe_den = jnp.zeros((pattern_side, pattern_side), jnp.float32)

    def step(slot, state):
        accumulated, probe_grad, probe_den = state
        which = order[slot]
        row_at = spots[which, 0].astype(jnp.int32)
        col_at = spots[which, 1].astype(jnp.int32)
        window = lax.dynamic_slice(object_field, (zero_index, row_at, col_at), (2, pattern_side, pattern_side))
        grad, pgrad, pden = process(window, measured[which], probe, table_re, table_im)
        added = jnp.concatenate([grad, lighting[None]], axis=0)
        region = lax.dynamic_slice(accumulated, (zero_index, row_at, col_at), (3, pattern_side, pattern_side))
        accumulated = lax.dynamic_update_slice(accumulated, region + added, (zero_index, row_at, col_at))
        return (accumulated, probe_grad + pgrad, probe_den + pden)
    accumulated, probe_grad, probe_den = lax.fori_loop(zero_index, total, step, (accumulated, probe_grad, probe_den))
    light = accumulated[2]
    object_new = object_field + accumulated[:2] / (light + 0.1 * jnp.max(light))
    probe_new = probe + probe_grad / (probe_den + 0.1 * jnp.max(probe_den))
    return (object_new, probe_new)
```

```python
import functools
import math

import jax
import jax.numpy as jnp
import numpy as np
from jax import lax
from jax.experimental import pallas as pl
from jax.experimental.pallas import tpu as pltpu
from jax.sharding import PartitionSpec as P

LANES = 128
SUBLANES = 8
VMEM_LIMIT = 56 * 1024 * 1024


def shifted(value, d_row, d_col):
    rows, cols = lax.axis_size("row"), lax.axis_size("col")
    pairs = []
    for r in range(rows):
        for c in range(cols):
            if 0 <= r + d_row < rows and 0 <= c + d_col < cols:
                pairs.append((r * cols + c, (r + d_row) * cols + c + d_col))
    return lax.ppermute(value, ("row", "col"), pairs)


def tables(side):
    index = np.arange(side)
    angle = (index[:, None] * index[None, :] % side) * (2.0 * math.pi / side)
    scale = 1.0 / math.sqrt(side)
    re = (np.cos(angle) * scale).astype(np.float32)
    im = (-np.sin(angle) * scale).astype(np.float32)

    def left(im):
        return np.block([[re, -im], [im, re]])

    def right(im):
        return np.block([[re, im], [-im, re]])

    return [jnp.asarray(t, jnp.bfloat16) for t in (left(im), right(im), left(-im), right(-im))]


def corner_of(row, col):
    row_base = pl.multiple_of(row // SUBLANES * SUBLANES, SUBLANES)
    col_base = pl.multiple_of(col // LANES * LANES, LANES)
    return row_base, row - row_base, col_base, col - col_base


def window_at(ref, part, row, col, side):
    row_base, down, col_base, over = corner_of(row, col)
    groups = side // SUBLANES
    lane = lax.broadcasted_iota(jnp.int32, (side, LANES), 1)
    sub = lax.broadcasted_iota(jnp.int32, (groups, SUBLANES, LANES), 1)
    turned = []
    for j in range(side // LANES + 1):
        block = ref[part, pl.ds(row_base, side + SUBLANES), pl.ds(col_base + j * LANES, LANES)]
        block = block.reshape(groups + 1, SUBLANES, LANES)
        block = pltpu.roll(block, lax.rem(SUBLANES - down, SUBLANES), 1)
        block = jnp.where(sub < SUBLANES - down, block[:groups], block[1:]).reshape(side, LANES)
        turned.append(pltpu.roll(block, lax.rem(LANES - over, LANES), 1))
    parts = [jnp.where(lane < LANES - over, turned[j], turned[j + 1]) for j in range(side // LANES)]
    return jnp.concatenate(parts, axis=1)


def add_at(ref, part, row, col, value, side):
    row_base, down, col_base, over = corner_of(row, col)
    groups = side // SUBLANES
    blocks = side // LANES
    lane = lax.broadcasted_iota(jnp.int32, (side, LANES), 1)
    sub = lax.broadcasted_iota(jnp.int32, (groups + 1, SUBLANES, LANES), 1)
    turned = [pltpu.roll(value[:, j * LANES:(j + 1) * LANES], over, 1) for j in range(blocks)]
    none = jnp.zeros((side, LANES), value.dtype)
    gap = jnp.zeros((1, SUBLANES, LANES), value.dtype)
    for j in range(blocks + 1):
        block = jnp.where(lane >= over, turned[j] if j < blocks else none, turned[j - 1] if j else none)
        block = pltpu.roll(block.reshape(groups, SUBLANES, LANES), down, 1)
        block = jnp.where(
            sub >= down, jnp.concatenate([block, gap], axis=0), jnp.concatenate([gap, block], axis=0)
        )
        place = (part, pl.ds(row_base, side + SUBLANES), pl.ds(col_base + j * LANES, LANES))
        ref[place] += block.reshape(side + SUBLANES, LANES)


def main_kernel(
    count_ref, local_ref, tile_ref, below_ref, right_ref, corner_ref, amp_ref, probe_ref, lf_ref, rf_ref, lg_ref, rg_ref,
    g_tile, g_below, g_right, g_corner, pgrad_ref,
    ext, gacc, stage, turned, wave,
):
    modes, side = probe_ref.shape[1], probe_ref.shape[2]
    rows, cols = tile_ref.shape[1], tile_ref.shape[2]
    ext[:, :rows, :cols] = tile_ref[...]
    ext[:, rows:, :cols] = below_ref[...]
    ext[:, :rows, cols:] = right_ref[...]
    ext[:, rows:, cols:] = corner_ref[...]
    gacc[...] = jnp.zeros_like(gacc)
    pgrad_ref[...] = jnp.zeros_like(pgrad_ref)

    def dot(a, b):
        return jnp.dot(a, b, preferred_element_type=jnp.float32)

    def transform(left_ref, right_ref):
        for k in range(modes):
            got = dot(left_ref[...], stage[:, k * side:(k + 1) * side])
            turned[k * side:(k + 1) * side, :side] = got[:side].astype(jnp.bfloat16)
            turned[k * side:(k + 1) * side, side:] = got[side:].astype(jnp.bfloat16)
        wave[...] = dot(turned[...], right_ref[...])

    def step(p, carry):
        row, col = local_ref[p, 0], local_ref[p, 1]
        win_re = window_at(ext, 0, row, col, side)
        win_im = window_at(ext, 1, row, col, side)
        for k in range(modes):
            pr, pi = probe_ref[0, k], probe_ref[1, k]
            stage[:side, k * side:(k + 1) * side] = (pr * win_re - pi * win_im).astype(jnp.bfloat16)
            stage[side:, k * side:(k + 1) * side] = (pr * win_im + pi * win_re).astype(jnp.bfloat16)
        transform(lf_ref, rf_ref)
        model = jnp.zeros((side, side), jnp.float32)
        for k in range(modes):
            wr, wi = wave[k * side:(k + 1) * side, :side], wave[k * side:(k + 1) * side, side:]
            model += wr * wr + wi * wi
        factor = amp_ref[p] * lax.rsqrt(jnp.maximum(model, 1.0)) - 1.0
        for k in range(modes):
            wr, wi = wave[k * side:(k + 1) * side, :side], wave[k * side:(k + 1) * side, side:]
            stage[:side, k * side:(k + 1) * side] = (wr * factor).astype(jnp.bfloat16)
            stage[side:, k * side:(k + 1) * side] = (wi * factor).astype(jnp.bfloat16)
        transform(lg_ref, rg_ref)
        grad_re = jnp.zeros((side, side), jnp.float32)
        grad_im = jnp.zeros((side, side), jnp.float32)
        win_re = window_at(ext, 0, row, col, side)
        win_im = window_at(ext, 1, row, col, side)
        for k in range(modes):
            cr, ci = wave[k * side:(k + 1) * side, :side], wave[k * side:(k + 1) * side, side:]
            pr, pi = probe_ref[0, k], probe_ref[1, k]
            grad_re += pr * cr + pi * ci
            grad_im += pr * ci - pi * cr
            pgrad_ref[k] += win_re * cr + win_im * ci
            pgrad_ref[modes + k] += win_re * ci - win_im * cr
        pgrad_ref[2 * modes] += win_re * win_re + win_im * win_im
        add_at(gacc, 0, row, col, grad_re, side)
        add_at(gacc, 1, row, col, grad_im, side)
        return carry

    lax.fori_loop(0, count_ref[0], step, 0)
    g_tile[...] = gacc[:, :rows, :cols]
    g_below[...] = gacc[:, rows:, :cols]
    g_right[...] = gacc[:, :rows, cols:]
    g_corner[...] = gacc[:, rows:, cols:]


def light_kernel(total_ref, where_ref, probe_ref, light_ref, top_ref, lit, acc):
    side = probe_ref.shape[2]
    rows, cols = light_ref.shape
    lit[0] = jnp.sum(probe_ref[0] * probe_ref[0] + probe_ref[1] * probe_ref[1], axis=0)
    acc[...] = jnp.zeros_like(acc)

    def step(p, carry):
        add_at(acc, 0, where_ref[p, 0], where_ref[p, 1], lit[0], side)
        return carry

    lax.fori_loop(0, total_ref[0], step, 0)
    light = acc[0, side:side + rows, side:side + cols]
    light_ref[...] = light
    top = jnp.max(light, axis=0, keepdims=True)
    top = jnp.max(top, axis=1, keepdims=True)
    top_ref[...] = jnp.broadcast_to(top, top_ref.shape)


def finish_kernel(top_ref, tile_ref, light_ref, g_tile, g_up, g_left, g_diag, out_ref, total):
    side = g_left.shape[2]
    total[...] = g_tile[...] + g_up[...]
    total[:, :, :side] += g_left[...] + g_diag[...]
    scale = 1.0 / (light_ref[...] + 0.1 * top_ref[0, 0])
    out_ref[0] = tile_ref[0] + total[0] * scale
    out_ref[1] = tile_ref[1] + total[1] * scale


def probe_kernel(probe_ref, sums_ref, out_ref):
    modes = probe_ref.shape[1]
    den = sums_ref[2 * modes]
    top = jnp.max(jnp.max(den, axis=0, keepdims=True), axis=1, keepdims=True)
    scale = 1.0 / (den + 0.1 * top)
    for k in range(modes):
        out_ref[0, k] = probe_ref[0, k] + sums_ref[k] * scale
        out_ref[1, k] = probe_ref[1, k] + sums_ref[modes + k] * scale


def f32(*shape):
    return jax.ShapeDtypeStruct(shape, jnp.float32)


VM = pl.BlockSpec(memory_space=pltpu.VMEM)
SM = pl.BlockSpec(memory_space=pltpu.SMEM)
PARAMS = pltpu.CompilerParams(vmem_limit_bytes=VMEM_LIMIT)


def cost(flops, moved):
    return pl.CostEstimate(flops=flops, bytes_accessed=moved, transcendentals=0)


def body(object_field, probe, amplitudes, corners, counts):
    rows, cols = object_field.shape[1], object_field.shape[2]
    modes, side = probe.shape[1], probe.shape[2]
    slots = amplitudes.shape[2]
    my_row, my_col = lax.axis_index("row"), lax.axis_index("col")
    anchor = jnp.stack([my_row * rows, my_col * cols])
    spots = corners[0, 0]
    local = spots - anchor[None, :]

    from_up = shifted(spots, 1, 0)
    from_left = shifted(spots, 0, 1)
    from_diag = shifted(spots, 1, 1)
    below = shifted(object_field[:, :side, :], -1, 0)
    right = shifted(object_field[:, :, :side], 0, -1)
    corner = shifted(object_field[:, :side, :side], -1, -1)

    def live(d_row, d_col):
        inside = (my_row >= d_row) & (my_col >= d_col)
        number = counts[jnp.maximum(my_row - d_row, 0), jnp.maximum(my_col - d_col, 0)]
        return (jnp.arange(slots) < number) & inside

    where = jnp.concatenate([spots, from_up, from_left, from_diag], axis=0) - anchor[None, :] + side
    flags = jnp.concatenate([live(0, 0), live(1, 0), live(0, 1), live(1, 1)])
    flags = flags & (where[:, 0] > 0) & (where[:, 1] > 0)
    order = jnp.where(flags, jnp.cumsum(flags) - 1, 4 * slots)
    picked = jnp.arange(4 * slots)[:, None] == order[None, :]
    where = jnp.sum(jnp.where(picked[:, :, None], where[None, :, :], 0), axis=1).astype(jnp.int32)
    total = jnp.sum(flags).astype(jnp.int32).reshape(1)
    light, top = pl.pallas_call(
        light_kernel,
        out_shape=(f32(rows, cols), f32(8, LANES)),
        in_specs=[SM, SM, VM],
        out_specs=(VM, VM),
        scratch_shapes=[
            pltpu.VMEM((1, side, side), jnp.float32),
            pltpu.VMEM((1, rows + 2 * side, cols + 2 * side), jnp.float32),
        ],
        compiler_params=PARAMS,
        cost_estimate=cost(10**8, 10**7),
        name="lighting",
    )(total, where, probe)
    top = lax.pmax(top, ("row", "col"))

    count = counts[my_row, my_col].reshape(1)
    g_tile, g_below, g_right, g_corner, sums = pl.pallas_call(
        main_kernel,
        out_shape=(
            f32(2, rows, cols), f32(2, side, cols), f32(2, rows, side), f32(2, side, side),
            f32(2 * modes + 1, side, side),
        ),
        in_specs=[SM, SM] + [VM] * 10,
        out_specs=(VM,) * 5,
        scratch_shapes=[
            pltpu.VMEM((2, rows + side, cols + side), jnp.float32),
            pltpu.VMEM((2, rows + side, cols + side), jnp.float32),
            pltpu.VMEM((2 * side, modes * side), jnp.bfloat16),
            pltpu.VMEM((modes * side, 2 * side), jnp.bfloat16),
            pltpu.VMEM((modes * side, 2 * side), jnp.float32),
        ],
        compiler_params=PARAMS,
        cost_estimate=cost(13 * 10**9, 2 * 10**7),
        name="positions",
    )(count, local, object_field, below, right, corner, amplitudes[0, 0], probe, *tables(side))

    g_up = shifted(g_below, 1, 0)
    g_left = shifted(g_right, 0, 1)
    g_diag = shifted(g_corner, 1, 1)
    sums = lax.psum(sums, ("row", "col"))
    object_new = pl.pallas_call(
        finish_kernel,
        out_shape=f32(2, rows, cols),
        in_specs=[SM] + [VM] * 6,
        out_specs=VM,
        scratch_shapes=[pltpu.VMEM((2, rows, cols), jnp.float32)],
        compiler_params=PARAMS,
        cost_estimate=cost(10**6, 6 * 10**6),
        name="object_update",
    )(top, object_field, light, g_tile, g_up, g_left, g_diag)
    probe_new = pl.pallas_call(
        probe_kernel,
        out_shape=f32(*probe.shape),
        in_specs=[VM] * 2,
        out_specs=VM,
        compiler_params=PARAMS,
        cost_estimate=cost(10**6, 6 * 10**6),
        name="probe_update",
    )(probe, sums)
    return object_new, probe_new


def solution(mesh):
    in_specs = (
        P(None, "row", "col"),
        P(),
        P("row", "col", None, None, None),
        P("row", "col", None, None),
        P(),
    )
    out_specs = (P(None, "row", "col"), P())
    return jax.shard_map(body, mesh=mesh, in_specs=in_specs, out_specs=out_specs, check_vma=False)
```

```python
import functools
import math

import jax
import jax.numpy as jnp
import numpy as np
from jax import lax
from jax.experimental import pallas as pl
from jax.experimental.pallas import tpu as pltpu
from jax.sharding import PartitionSpec as P

LANES = 128
SUBLANES = 8
VMEM_LIMIT = 56 * 1024 * 1024


def shifted(value, d_row, d_col):
    rows, cols = lax.axis_size("row"), lax.axis_size("col")
    pairs = []
    for r in range(rows):
        for c in range(cols):
            if 0 <= r + d_row < rows and 0 <= c + d_col < cols:
                pairs.append((r * cols + c, (r + d_row) * cols + c + d_col))
    return lax.ppermute(value, ("row", "col"), pairs)


def swapped(value, flip_row, flip_col):
    rows, cols = lax.axis_size("row"), lax.axis_size("col")
    pairs = [(r * cols + c, (r ^ flip_row) * cols + (c ^ flip_col)) for r in range(rows) for c in range(cols)]
    return lax.ppermute(value, ("row", "col"), pairs)


def tables(side):
    index = np.arange(side)
    angle = (index[:, None] * index[None, :] % side) * (2.0 * math.pi / side)
    scale = 1.0 / math.sqrt(side)
    re = (np.cos(angle) * scale).astype(np.float32)
    im = (-np.sin(angle) * scale).astype(np.float32)

    def left(im):
        return np.block([[re, -im], [im, re]])

    def right(im):
        return np.block([[re, im], [-im, re]])

    return [jnp.asarray(t, jnp.bfloat16) for t in (left(im), right(im), left(-im), right(-im))]


def corner_of(row, col):
    row_base = pl.multiple_of(row // SUBLANES * SUBLANES, SUBLANES)
    col_base = pl.multiple_of(col // LANES * LANES, LANES)
    return row_base, row - row_base, col_base, col - col_base


def window_at(ref, part, row, col, side):
    row_base, down, col_base, over = corner_of(row, col)
    groups = side // SUBLANES
    lane = lax.broadcasted_iota(jnp.int32, (side, LANES), 1)
    sub = lax.broadcasted_iota(jnp.int32, (groups, SUBLANES, LANES), 1)
    turned = []
    for j in range(side // LANES + 1):
        block = ref[part, pl.ds(row_base, side + SUBLANES), pl.ds(col_base + j * LANES, LANES)]
        block = block.reshape(groups + 1, SUBLANES, LANES)
        block = pltpu.roll(block, lax.rem(SUBLANES - down, SUBLANES), 1)
        block = jnp.where(sub < SUBLANES - down, block[:groups], block[1:]).reshape(side, LANES)
        turned.append(pltpu.roll(block, lax.rem(LANES - over, LANES), 1))
    parts = [jnp.where(lane < LANES - over, turned[j], turned[j + 1]) for j in range(side // LANES)]
    return jnp.concatenate(parts, axis=1)


def add_at(ref, part, row, col, value, side):
    row_base, down, col_base, over = corner_of(row, col)
    groups = side // SUBLANES
    blocks = side // LANES
    lane = lax.broadcasted_iota(jnp.int32, (side, LANES), 1)
    sub = lax.broadcasted_iota(jnp.int32, (groups + 1, SUBLANES, LANES), 1)
    turned = [pltpu.roll(value[:, j * LANES:(j + 1) * LANES], over, 1) for j in range(blocks)]
    none = jnp.zeros((side, LANES), value.dtype)
    gap = jnp.zeros((1, SUBLANES, LANES), value.dtype)
    for j in range(blocks + 1):
        block = jnp.where(lane >= over, turned[j] if j < blocks else none, turned[j - 1] if j else none)
        block = pltpu.roll(block.reshape(groups, SUBLANES, LANES), down, 1)
        block = jnp.where(
            sub >= down, jnp.concatenate([block, gap], axis=0), jnp.concatenate([gap, block], axis=0)
        )
        place = (part, pl.ds(row_base, side + SUBLANES), pl.ds(col_base + j * LANES, LANES))
        ref[place] += block.reshape(side + SUBLANES, LANES)


def main_kernel(
    counts_ref, spots_ref, tile_ref, below_ref, right_ref, corner_ref, amp_ref, probe_ref, top_ref,
    lf_ref, rf_ref, lg_ref, rg_ref,
    g_tile, g_below, g_right, g_corner, mine_ref, other_ref,
    ext, gacc, stage, turned, wave, wins, sums,
):
    modes, side = probe_ref.shape[1], probe_ref.shape[2]
    rows, cols = tile_ref.shape[1], tile_ref.shape[2]
    my_row, my_col = lax.axis_index("row"), lax.axis_index("col")
    ext[:, :rows, :cols] = tile_ref[...]
    ext[:, rows:, :cols] = below_ref[...]
    ext[:, :rows, cols:] = right_ref[...]
    ext[:, rows:, cols:] = corner_ref[...]
    gacc[...] = jnp.zeros_like(gacc)
    sums[...] = jnp.zeros_like(sums)

    def dot(a, b):
        return jnp.dot(a, b, preferred_element_type=jnp.float32)

    def transform(left_ref, right_ref):
        for k in range(modes):
            got = dot(left_ref[...], stage[:, k * side:(k + 1) * side])
            turned[k * side:(k + 1) * side, :side] = got[:side].astype(jnp.bfloat16)
            turned[k * side:(k + 1) * side, side:] = got[side:].astype(jnp.bfloat16)
        wave[...] = dot(turned[...], right_ref[...])

    def plane(index):
        return slice(index * side, (index + 1) * side)

    def step(p, carry):
        row, col = spots_ref[p, 0] - my_row * rows, spots_ref[p, 1] - my_col * cols
        win_re = window_at(ext, 0, row, col, side)
        win_im = window_at(ext, 1, row, col, side)
        wins[0], wins[1] = win_re, win_im
        sums[plane(2 * modes)] += win_re * win_re + win_im * win_im
        for k in range(modes):
            pr, pi = probe_ref[0, k], probe_ref[1, k]
            stage[:side, plane(k)] = (pr * win_re - pi * win_im).astype(jnp.bfloat16)
            stage[side:, plane(k)] = (pr * win_im + pi * win_re).astype(jnp.bfloat16)
        transform(lf_ref, rf_ref)
        model = jnp.zeros((side, side), jnp.float32)
        for k in range(modes):
            wr, wi = wave[plane(k), :side], wave[plane(k), side:]
            model += wr * wr + wi * wi
        factor = amp_ref[p] * lax.rsqrt(jnp.maximum(model, 1.0)) - 1.0
        for k in range(modes):
            wr, wi = wave[plane(k), :side], wave[plane(k), side:]
            stage[:side, plane(k)] = (wr * factor).astype(jnp.bfloat16)
            stage[side:, plane(k)] = (wi * factor).astype(jnp.bfloat16)
        transform(lg_ref, rg_ref)
        grad_re = jnp.zeros((side, side), jnp.float32)
        grad_im = jnp.zeros((side, side), jnp.float32)
        for k in range(modes):
            cr, ci = wave[plane(k), :side], wave[plane(k), side:]
            pr, pi = probe_ref[0, k], probe_ref[1, k]
            grad_re += pr * cr + pi * ci
            grad_im += pr * ci - pi * cr
            sums[plane(k)] += wins[0] * cr + wins[1] * ci
            sums[plane(modes + k)] += wins[0] * ci - wins[1] * cr
        add_at(gacc, 0, row, col, grad_re, side)
        add_at(gacc, 1, row, col, grad_im, side)
        return carry

    lax.fori_loop(0, counts_ref[my_row, my_col], step, 0)
    g_tile[...] = gacc[:, :rows, :cols]
    g_below[...] = gacc[:, rows:, :cols]
    g_right[...] = gacc[:, :rows, cols:]
    g_corner[...] = gacc[:, rows:, cols:]
    half = mine_ref.shape[0]
    core = lax.rem(my_row, 2)
    mine_ref[...] = sums[pl.ds(pl.multiple_of(core * half, SUBLANES), half)]
    other_ref[:half] = sums[pl.ds(pl.multiple_of((1 - core) * half, SUBLANES), half)]
    other_ref[half:] = top_ref[...]


def light_kernel(counts_ref, spots_ref, up_ref, left_ref, diag_ref, probe_ref, light_ref, top_ref, lit, acc):
    side = probe_ref.shape[2]
    rows, cols = light_ref.shape
    my_row, my_col = lax.axis_index("row"), lax.axis_index("col")
    lit[...] = jnp.sum(probe_ref[0] * probe_ref[0] + probe_ref[1] * probe_ref[1], axis=0)
    acc[...] = jnp.zeros_like(acc)
    for ref, d_row, d_col in ((spots_ref, 0, 0), (up_ref, 1, 0), (left_ref, 0, 1), (diag_ref, 1, 1)):
        inside = (my_row >= d_row) & (my_col >= d_col)
        number = counts_ref[jnp.maximum(my_row - d_row, 0), jnp.maximum(my_col - d_col, 0)]

        def step(p, carry, ref=ref):
            row, col = ref[p, 0] - my_row * rows + side, ref[p, 1] - my_col * cols + side

            @pl.when((row > 0) & (col > 0))
            def _():
                add_at(acc, 0, row, col, lit[...], side)

            return carry

        lax.fori_loop(0, jnp.where(inside, number, 0), step, 0)
    light = acc[0, side:side + rows, side:side + cols]
    light_ref[...] = light
    top = jnp.max(light, axis=0, keepdims=True)
    top = jnp.max(top, axis=1, keepdims=True)
    top_ref[...] = jnp.broadcast_to(top, top_ref.shape)


def fold_kernel(group, rank_of, *refs):
    received, rest = refs[2:2 + group[0] - 1], refs[2 + group[0] - 1:]
    own_ref, top_ref = refs[:2]
    parts = group[1]
    out_own, out_top, out_other, total = rest[0], rest[1], rest[2:2 + parts - 1], rest[-1]
    rows = own_ref.shape[0]
    value, top = own_ref[...], top_ref[...]
    for ref in received:
        value += ref[:rows]
        top = jnp.maximum(top, ref[rows:])
    out_top[...] = top
    if parts == 1:
        out_own[...] = value
        return
    total[...] = value
    rank, share = rank_of(), rows // parts
    out_own[...] = total[pl.ds(pl.multiple_of(rank * share, SUBLANES), share)]
    for d, ref in enumerate(out_other, 1):
        ref[:share] = total[pl.ds(pl.multiple_of((rank ^ d) * share, SUBLANES), share)]
        ref[share:] = top


def fold(own, top, received, parts, rank_of, name):
    rows, width = own.shape
    share = rows // parts
    got = pl.pallas_call(
        functools.partial(fold_kernel, (len(received) + 1, parts), rank_of),
        out_shape=(f32(share, width), f32(*top.shape)) + (f32(share + SUBLANES, width),) * (parts - 1),
        in_specs=[VM] * (2 + len(received)),
        out_specs=(VM,) * (parts + 1),
        scratch_shapes=[pltpu.VMEM((rows, width), jnp.float32)],
        compiler_params=PARAMS,
        cost_estimate=cost(10**6, 4 * rows * width * (len(received) + 2)),
        name=name,
    )(own, top, *received)
    return got[0], got[1], got[2:]


def unfold_kernel(rank_of, *refs):
    out_ref = refs[-1]
    share, rank = refs[0].shape[0], rank_of()
    for d, ref in enumerate(refs[:-1]):
        out_ref[pl.ds(pl.multiple_of((rank ^ d) * share, SUBLANES), share)] = ref[...]


def unfold(parts, rank_of, name):
    share, width = parts[0].shape
    return pl.pallas_call(
        functools.partial(unfold_kernel, rank_of),
        out_shape=f32(share * len(parts), width),
        in_specs=[VM] * len(parts),
        out_specs=VM,
        compiler_params=PARAMS,
        cost_estimate=cost(10**6, 8 * share * width * len(parts)),
        name=name,
    )(*parts)


def pair_rank():
    return lax.axis_index("row") // 2


def col_rank():
    return lax.axis_index("col")


def finish_kernel(top_ref, tile_ref, light_ref, g_tile, g_up, g_left, g_diag, out_ref, total):
    side = g_left.shape[2]
    total[...] = g_tile[...] + g_up[...]
    total[:, :, :side] += g_left[...] + g_diag[...]
    scale = 1.0 / (light_ref[...] + 0.1 * top_ref[0, 0])
    out_ref[0] = tile_ref[0] + total[0] * scale
    out_ref[1] = tile_ref[1] + total[1] * scale


def probe_kernel(probe_ref, mine_ref, other_ref, out_ref, sums):
    modes, side = probe_ref.shape[1], probe_ref.shape[2]
    half = mine_ref.shape[0]
    core = lax.rem(lax.axis_index("row"), 2)
    sums[pl.ds(pl.multiple_of(core * half, SUBLANES), half)] = mine_ref[...]
    sums[pl.ds(pl.multiple_of((1 - core) * half, SUBLANES), half)] = other_ref[...]
    den = sums[2 * modes * side:(2 * modes + 1) * side]
    top = jnp.max(jnp.max(den, axis=0, keepdims=True), axis=1, keepdims=True)
    scale = 1.0 / (den + 0.1 * top)
    for k in range(modes):
        out_ref[0, k] = probe_ref[0, k] + sums[k * side:(k + 1) * side] * scale
        out_ref[1, k] = probe_ref[1, k] + sums[(modes + k) * side:(modes + k + 1) * side] * scale


def f32(*shape):
    return jax.ShapeDtypeStruct(shape, jnp.float32)


VM = pl.BlockSpec(memory_space=pltpu.VMEM)
SM = pl.BlockSpec(memory_space=pltpu.SMEM)
PARAMS = pltpu.CompilerParams(vmem_limit_bytes=VMEM_LIMIT)


def cost(flops, moved):
    return pl.CostEstimate(flops=flops, bytes_accessed=moved, transcendentals=0)


def body(object_field, probe, amplitudes, corners, counts):
    rows, cols = object_field.shape[1], object_field.shape[2]
    modes, side = probe.shape[1], probe.shape[2]
    pairs, n_col = lax.axis_size("row") // 2, lax.axis_size("col")
    step = SUBLANES * 2 * pairs * n_col
    total_rows = -(-(2 * modes + 1) * side // step) * step
    half = total_rows // 2
    spots = corners[0, 0]

    from_up = shifted(spots, 1, 0)
    from_left = shifted(spots, 0, 1)
    from_diag = shifted(spots, 1, 1)
    below = shifted(object_field[:, :side, :], -1, 0)
    right = shifted(object_field[:, :, :side], 0, -1)
    corner = shifted(object_field[:, :side, :side], -1, -1)

    light, top = pl.pallas_call(
        light_kernel,
        out_shape=(f32(rows, cols), f32(SUBLANES, side)),
        in_specs=[SM] * 5 + [VM],
        out_specs=(VM, VM),
        scratch_shapes=[
            pltpu.VMEM((side, side), jnp.float32),
            pltpu.VMEM((1, rows + 2 * side, cols + 2 * side), jnp.float32),
        ],
        compiler_params=PARAMS,
        cost_estimate=cost(10**8, 10**7),
        name="lighting",
    )(counts, spots, from_up, from_left, from_diag, probe)

    g_tile, g_below, g_right, g_corner, mine, other = pl.pallas_call(
        main_kernel,
        out_shape=(
            f32(2, rows, cols), f32(2, side, cols), f32(2, rows, side), f32(2, side, side),
            f32(half, side), f32(half + SUBLANES, side),
        ),
        in_specs=[SM] * 2 + [VM] * 11,
        out_specs=(VM,) * 6,
        scratch_shapes=[
            pltpu.VMEM((2, rows + side, cols + side), jnp.float32),
            pltpu.VMEM((2, rows + side, cols + side), jnp.float32),
            pltpu.VMEM((2 * side, modes * side), jnp.bfloat16),
            pltpu.VMEM((modes * side, 2 * side), jnp.bfloat16),
            pltpu.VMEM((modes * side, 2 * side), jnp.float32),
            pltpu.VMEM((2, side, side), jnp.float32),
            pltpu.VMEM((total_rows, side), jnp.float32),
        ],
        compiler_params=PARAMS,
        cost_estimate=cost(13 * 10**9, 2 * 10**7),
        name="positions",
    )(counts, spots, object_field, below, right, corner, amplitudes[0, 0], probe, top, *tables(side))

    received = [swapped(other, 1, 0)]
    g_up = shifted(g_below, 1, 0)
    g_left = shifted(g_right, 0, 1)
    g_diag = shifted(g_corner, 1, 1)
    own, top, others = fold(mine, top, received, pairs, pair_rank, "fold_chip")
    received = [swapped(value, 2 * d, 0) for d, value in enumerate(others, 1)]
    own, top, others = fold(own, top, received, n_col, col_rank, "fold_plane")
    received = [swapped(value, 0, d) for d, value in enumerate(others, 1)]
    own, top, _ = fold(own, top, received, 1, None, "fold_all")
    own = unfold([own] + [swapped(own, 0, d) for d in range(1, n_col)], col_rank, "unfold_col")
    own = unfold([own] + [swapped(own, 2 * d, 0) for d in range(1, pairs)], pair_rank, "unfold_pairs")
    other = swapped(own, 1, 0)

    object_new = pl.pallas_call(
        finish_kernel,
        out_shape=f32(2, rows, cols),
        in_specs=[SM] + [VM] * 6,
        out_specs=VM,
        scratch_shapes=[pltpu.VMEM((2, rows, cols), jnp.float32)],
        compiler_params=PARAMS,
        cost_estimate=cost(10**6, 6 * 10**6),
        name="object_update",
    )(top, object_field, light, g_tile, g_up, g_left, g_diag)
    probe_new = pl.pallas_call(
        probe_kernel,
        out_shape=f32(*probe.shape),
        in_specs=[VM] * 3,
        out_specs=VM,
        scratch_shapes=[pltpu.VMEM((total_rows, side), jnp.float32)],
        compiler_params=PARAMS,
        cost_estimate=cost(10**6, 6 * 10**6),
        name="probe_update",
    )(probe, own, other)
    return object_new, probe_new


def solution(mesh):
    in_specs = (
        P(None, "row", "col"),
        P(),
        P("row", "col", None, None, None),
        P("row", "col", None, None),
        P(),
    )
    out_specs = (P(None, "row", "col"), P())
    return jax.shard_map(body, mesh=mesh, in_specs=in_specs, out_specs=out_specs, check_vma=False)
```

```python
import functools
import math

import jax
import jax.numpy as jnp
import numpy as np
from jax import lax
from jax.experimental import pallas as pl
from jax.experimental.pallas import tpu as pltpu
from jax.sharding import PartitionSpec as P

LANES = 128
SUBLANES = 8
VMEM_LIMIT = 56 * 1024 * 1024


def shifted(value, d_row, d_col):
    rows, cols = lax.axis_size("row"), lax.axis_size("col")
    pairs = []
    for r in range(rows):
        for c in range(cols):
            if 0 <= r + d_row < rows and 0 <= c + d_col < cols:
                pairs.append((r * cols + c, (r + d_row) * cols + c + d_col))
    return lax.ppermute(value, ("row", "col"), pairs)


def swapped(value, flip_row, flip_col):
    rows, cols = lax.axis_size("row"), lax.axis_size("col")
    pairs = [(r * cols + c, (r ^ flip_row) * cols + (c ^ flip_col)) for r in range(rows) for c in range(cols)]
    return lax.ppermute(value, ("row", "col"), pairs)


def tables(side):
    index = np.arange(side)
    angle = (index[:, None] * index[None, :] % side) * (2.0 * math.pi / side)
    scale = 1.0 / math.sqrt(side)
    re = (np.cos(angle) * scale).astype(np.float32)
    im = (-np.sin(angle) * scale).astype(np.float32)

    def left(im):
        return np.block([[re, -im], [im, re]])

    def right(im):
        return np.block([[re, im], [-im, re]])

    return [jnp.asarray(t, jnp.bfloat16) for t in (left(im), right(im), left(-im), right(-im))]


def corner_of(row, col):
    row_base = pl.multiple_of(row // SUBLANES * SUBLANES, SUBLANES)
    col_base = pl.multiple_of(col // LANES * LANES, LANES)
    return row_base, row - row_base, col_base, col - col_base


def window_at(ref, part, row, col, side):
    row_base, down, col_base, over = corner_of(row, col)
    groups = side // SUBLANES
    lane = lax.broadcasted_iota(jnp.int32, (side, LANES), 1)
    sub = lax.broadcasted_iota(jnp.int32, (groups, SUBLANES, LANES), 1)
    turned = []
    for j in range(side // LANES + 1):
        block = ref[part, pl.ds(row_base, side + SUBLANES), pl.ds(col_base + j * LANES, LANES)]
        block = block.reshape(groups + 1, SUBLANES, LANES)
        block = pltpu.roll(block, lax.rem(SUBLANES - down, SUBLANES), 1)
        block = jnp.where(sub < SUBLANES - down, block[:groups], block[1:]).reshape(side, LANES)
        turned.append(pltpu.roll(block, lax.rem(LANES - over, LANES), 1))
    parts = [jnp.where(lane < LANES - over, turned[j], turned[j + 1]) for j in range(side // LANES)]
    return jnp.concatenate(parts, axis=1)


def add_at(ref, part, row, col, value, side):
    row_base, down, col_base, over = corner_of(row, col)
    groups = side // SUBLANES
    blocks = side // LANES
    lane = lax.broadcasted_iota(jnp.int32, (side, LANES), 1)
    sub = lax.broadcasted_iota(jnp.int32, (groups + 1, SUBLANES, LANES), 1)
    turned = [pltpu.roll(value[:, j * LANES:(j + 1) * LANES], over, 1) for j in range(blocks)]
    none = jnp.zeros((side, LANES), value.dtype)
    gap = jnp.zeros((1, SUBLANES, LANES), value.dtype)
    for j in range(blocks + 1):
        block = jnp.where(lane >= over, turned[j] if j < blocks else none, turned[j - 1] if j else none)
        block = pltpu.roll(block.reshape(groups, SUBLANES, LANES), down, 1)
        block = jnp.where(
            sub >= down, jnp.concatenate([block, gap], axis=0), jnp.concatenate([gap, block], axis=0)
        )
        place = (part, pl.ds(row_base, side + SUBLANES), pl.ds(col_base + j * LANES, LANES))
        ref[place] += block.reshape(side + SUBLANES, LANES)


def main_kernel(
    counts_ref, spots_ref, tile_ref, below_ref, right_ref, corner_ref, amp_ref, probe_ref, top_ref,
    lf_ref, rf_ref, lg_ref, rg_ref,
    g_tile, g_below, g_side, mine_ref, other_ref,
    ext, gacc, stage, turned, wave, wins, sums,
):
    modes, side = probe_ref.shape[1], probe_ref.shape[2]
    rows, cols = tile_ref.shape[1], tile_ref.shape[2]
    my_row, my_col = lax.axis_index("row"), lax.axis_index("col")
    ext[:, :rows, :cols] = tile_ref[...]
    ext[:, rows:, :cols] = below_ref[...]
    ext[:, :rows, cols:] = right_ref[...]
    ext[:, rows:, cols:] = corner_ref[...]
    gacc[...] = jnp.zeros_like(gacc)
    sums[...] = jnp.zeros_like(sums)

    def dot(a, b):
        return jnp.dot(a, b, preferred_element_type=jnp.float32)

    def transform(left_ref, right_ref):
        for k in range(modes):
            got = dot(left_ref[...], stage[:, k * side:(k + 1) * side])
            turned[k * side:(k + 1) * side, :side] = got[:side].astype(jnp.bfloat16)
            turned[k * side:(k + 1) * side, side:] = got[side:].astype(jnp.bfloat16)
        wave[...] = dot(turned[...], right_ref[...])

    def plane(index):
        return slice(index * side, (index + 1) * side)

    def step(p, carry):
        row, col = spots_ref[p, 0] - my_row * rows, spots_ref[p, 1] - my_col * cols
        win_re = window_at(ext, 0, row, col, side)
        win_im = window_at(ext, 1, row, col, side)
        wins[0], wins[1] = win_re, win_im
        sums[plane(2 * modes)] += win_re * win_re + win_im * win_im
        for k in range(modes):
            pr, pi = probe_ref[0, k], probe_ref[1, k]
            stage[:side, plane(k)] = (pr * win_re - pi * win_im).astype(jnp.bfloat16)
            stage[side:, plane(k)] = (pr * win_im + pi * win_re).astype(jnp.bfloat16)
        transform(lf_ref, rf_ref)
        model = jnp.zeros((side, side), jnp.float32)
        for k in range(modes):
            wr, wi = wave[plane(k), :side], wave[plane(k), side:]
            model += wr * wr + wi * wi
        factor = amp_ref[p] * lax.rsqrt(jnp.maximum(model, 1.0)) - 1.0
        for k in range(modes):
            wr, wi = wave[plane(k), :side], wave[plane(k), side:]
            stage[:side, plane(k)] = (wr * factor).astype(jnp.bfloat16)
            stage[side:, plane(k)] = (wi * factor).astype(jnp.bfloat16)
        transform(lg_ref, rg_ref)
        grad_re = jnp.zeros((side, side), jnp.float32)
        grad_im = jnp.zeros((side, side), jnp.float32)
        for k in range(modes):
            cr, ci = wave[plane(k), :side], wave[plane(k), side:]
            pr, pi = probe_ref[0, k], probe_ref[1, k]
            grad_re += pr * cr + pi * ci
            grad_im += pr * ci - pi * cr
            sums[plane(k)] += wins[0] * cr + wins[1] * ci
            sums[plane(modes + k)] += wins[0] * ci - wins[1] * cr
        add_at(gacc, 0, row, col, grad_re, side)
        add_at(gacc, 1, row, col, grad_im, side)
        return carry

    lax.fori_loop(0, counts_ref[my_row, my_col], step, 0)
    g_tile[...] = gacc[:, :rows, :cols]
    g_below[...] = gacc[:, rows:, :cols]
    g_side[...] = gacc[:, :, cols:]
    pairs = lax.axis_size("row") // 2
    share = mine_ref.shape[0] // pairs - SUBLANES
    half = share * pairs
    core = lax.rem(my_row, 2)
    for ref, base in ((mine_ref, core * half), (other_ref, (1 - core) * half)):
        base = pl.multiple_of(base, SUBLANES)
        for j in range(pairs):
            at = j * (share + SUBLANES)
            ref[at:at + share] = sums[pl.ds(base + j * share, share)]
            ref[at + share:at + share + SUBLANES] = top_ref[...]


def light_kernel(counts_ref, spots_ref, up_ref, left_ref, diag_ref, probe_ref, light_ref, top_ref, lit, acc):
    side = probe_ref.shape[2]
    rows, cols = light_ref.shape
    my_row, my_col = lax.axis_index("row"), lax.axis_index("col")
    lit[...] = jnp.sum(probe_ref[0] * probe_ref[0] + probe_ref[1] * probe_ref[1], axis=0)
    acc[...] = jnp.zeros_like(acc)
    for ref, d_row, d_col in ((spots_ref, 0, 0), (up_ref, 1, 0), (left_ref, 0, 1), (diag_ref, 1, 1)):
        inside = (my_row >= d_row) & (my_col >= d_col)
        number = counts_ref[jnp.maximum(my_row - d_row, 0), jnp.maximum(my_col - d_col, 0)]

        def step(p, carry, ref=ref):
            row, col = ref[p, 0] - my_row * rows + side, ref[p, 1] - my_col * cols + side

            @pl.when((row > 0) & (col > 0))
            def _():
                add_at(acc, 0, row, col, lit[...], side)

            return carry

        lax.fori_loop(0, jnp.where(inside, number, 0), step, 0)
    light = acc[0, side:side + rows, side:side + cols]
    light_ref[...] = light
    top = jnp.max(light, axis=0, keepdims=True)
    top = jnp.max(top, axis=1, keepdims=True)
    top_ref[...] = jnp.broadcast_to(top, top_ref.shape)


def merge(share, values):
    summed = jnp.arange(values[0].shape[0])[:, None] < share
    return functools.reduce(lambda a, b: jnp.where(summed, a + b, jnp.maximum(a, b)), values)


def finish_kernel(tile_ref, light_ref, top_ref, g_tile, g_left, g_up, out_ref):
    side = g_left.shape[2]
    rows, cols = light_ref.shape
    top = top_ref[0:1, 0:1]
    for at in range(0, cols, side):
        part = slice(at, at + side)
        scale = 1.0 / (light_ref[:, part] + 0.1 * top)
        for i in range(2):
            total = g_tile[i, :, part] + g_up[i, :, part]
            if at == 0:
                total += g_left[i, :rows]
            out_ref[i, :, part] = tile_ref[i, :, part] + total * scale


def probe_kernel(parts, probe_ref, *refs):
    pairs, n_col = parts
    block_refs, out_ref, sums = refs[:-2], refs[-2], refs[-1]
    modes, side = probe_ref.shape[1], probe_ref.shape[2]
    share = block_refs[0].shape[0]
    piece = share // n_col
    my_row, my_col = lax.axis_index("row"), lax.axis_index("col")
    core, pair = lax.rem(my_row, 2), my_row // 2
    for i, ref in enumerate(block_refs):
        flip, d = i // pairs, i % pairs
        base = ((core ^ flip) * pairs + (pair ^ d)) * share
        for e in range(n_col):
            to = pl.multiple_of(base + (my_col ^ e) * piece, SUBLANES)
            sums[pl.ds(to, piece)] = ref[e * piece:(e + 1) * piece]
    den = sums[2 * modes * side:(2 * modes + 1) * side]
    top = jnp.max(jnp.max(den, axis=0, keepdims=True), axis=1, keepdims=True)
    scale = 1.0 / (den + 0.1 * top)
    for k in range(modes):
        out_ref[0, k] = probe_ref[0, k] + sums[k * side:(k + 1) * side] * scale
        out_ref[1, k] = probe_ref[1, k] + sums[(modes + k) * side:(modes + k + 1) * side] * scale


def f32(*shape):
    return jax.ShapeDtypeStruct(shape, jnp.float32)


VM = pl.BlockSpec(memory_space=pltpu.VMEM)
SM = pl.BlockSpec(memory_space=pltpu.SMEM)
PARAMS = pltpu.CompilerParams(vmem_limit_bytes=VMEM_LIMIT)


def cost(flops, moved):
    return pl.CostEstimate(flops=flops, bytes_accessed=moved, transcendentals=0)


def body(object_field, probe, amplitudes, corners, counts):
    rows, cols = object_field.shape[1], object_field.shape[2]
    modes, side = probe.shape[1], probe.shape[2]
    pairs, n_col = lax.axis_size("row") // 2, lax.axis_size("col")
    step = SUBLANES * 2 * pairs * n_col
    total_rows = -(-(2 * modes + 1) * side // step) * step
    share = total_rows // (2 * pairs)
    piece = share // n_col
    pair, my_col = lax.axis_index("row") // 2, lax.axis_index("col")
    spots = corners[0, 0]

    right = shifted(object_field[:, :, :side], 0, -1)
    from_up = shifted(spots, 1, 0)
    from_left = shifted(spots, 0, 1)
    from_diag = shifted(spots, 1, 1)
    below = shifted(object_field[:, :side, :], -1, 0)
    corner = shifted(right[:, :side, :], -1, 0)

    light, top = pl.pallas_call(
        light_kernel,
        out_shape=(f32(rows, cols), f32(SUBLANES, side)),
        in_specs=[SM] * 5 + [VM],
        out_specs=(VM, VM),
        scratch_shapes=[
            pltpu.VMEM((side, side), jnp.float32),
            pltpu.VMEM((1, rows + 2 * side, cols + 2 * side), jnp.float32),
        ],
        compiler_params=PARAMS,
        cost_estimate=cost(10**8, 10**7),
        name="lighting",
    )(counts, spots, from_up, from_left, from_diag, probe)

    g_tile, g_below, g_side, mine, other = pl.pallas_call(
        main_kernel,
        out_shape=(
            f32(2, rows, cols), f32(2, side, cols), f32(2, rows + side, side),
            f32(pairs * (share + SUBLANES), side), f32(pairs * (share + SUBLANES), side),
        ),
        in_specs=[SM] * 2 + [VM] * 11,
        out_specs=(VM,) * 5,
        scratch_shapes=[
            pltpu.VMEM((2, rows + side, cols + side), jnp.float32),
            pltpu.VMEM((2, rows + side, cols + side), jnp.float32),
            pltpu.VMEM((2 * side, modes * side), jnp.bfloat16),
            pltpu.VMEM((modes * side, 2 * side), jnp.bfloat16),
            pltpu.VMEM((modes * side, 2 * side), jnp.float32),
            pltpu.VMEM((2, side, side), jnp.float32),
            pltpu.VMEM((total_rows, side), jnp.float32),
        ],
        compiler_params=PARAMS,
        cost_estimate=cost(13 * 10**9, 2 * 10**7),
        name="positions",
    )(counts, spots, object_field, below, right, corner, amplitudes[0, 0], probe, top, *tables(side))

    g_left = shifted(g_side, 0, 1)
    arrived = swapped(other, 1, 0)

    def cut(value, start, size):
        return lax.dynamic_slice_in_dim(value, start, size, 0)

    def chip_sum(d):
        start = (pair ^ d) * (share + SUBLANES)
        return merge(share, [cut(mine, start, share + SUBLANES), cut(arrived, start, share + SUBLANES)])

    plane_sum = merge(share, [chip_sum(0)] + [swapped(chip_sum(d), 2 * d, 0) for d in range(1, pairs)])
    lower = jnp.concatenate([g_below[:, :, :side] + g_left[:, rows:], g_below[:, :, side:]], axis=2)
    plane_sum, lower = lax.optimization_barrier((plane_sum, lower))
    g_up = shifted(lower, 1, 0)

    def col_part(e):
        return jnp.concatenate([cut(plane_sum, (my_col ^ e) * piece, piece), plane_sum[share:]], axis=0)

    own = merge(piece, [col_part(0)] + [swapped(col_part(e), 0, e) for e in range(1, n_col)])
    top = own[piece:]
    own = own[:piece]
    own = jnp.concatenate([own] + [swapped(own, 0, e) for e in range(1, n_col)], axis=0)
    object_new = pl.pallas_call(
        finish_kernel,
        out_shape=f32(2, rows, cols),
        in_specs=[VM] * 6,
        out_specs=VM,
        compiler_params=PARAMS,
        cost_estimate=cost(10**6, 6 * 10**6),
        name="object_update",
    )(object_field, light, top, g_tile, g_left, g_up)
    own, object_new = lax.optimization_barrier((own, object_new))
    blocks = [own] + [swapped(own, 2 * d, 0) for d in range(1, pairs)]
    blocks = blocks + [swapped(block, 1, 0) for block in blocks]
    probe_new = pl.pallas_call(
        functools.partial(probe_kernel, (pairs, n_col)),
        out_shape=f32(*probe.shape),
        in_specs=[VM] * (1 + len(blocks)),
        out_specs=VM,
        scratch_shapes=[pltpu.VMEM((total_rows, side), jnp.float32)],
        compiler_params=PARAMS,
        cost_estimate=cost(10**6, 6 * 10**6),
        name="probe_update",
    )(probe, *blocks)
    return object_new, probe_new


def solution(mesh):
    in_specs = (
        P(None, "row", "col"),
        P(),
        P("row", "col", None, None, None),
        P("row", "col", None, None),
        P(),
    )
    out_specs = (P(None, "row", "col"), P())
    return jax.shard_map(body, mesh=mesh, in_specs=in_specs, out_specs=out_specs, check_vma=False)
```

```python
import functools
import math

import jax
import jax.numpy as jnp
import numpy as np
from jax import lax
from jax.experimental import pallas as pl
from jax.experimental.pallas import tpu as pltpu
from jax.sharding import PartitionSpec as P

LANES = 128
SUBLANES = 8
MIB = 1024 * 1024


def shifted(value, d_row, d_col):
    rows, cols = lax.axis_size("row"), lax.axis_size("col")
    pairs = []
    for r in range(rows):
        for c in range(cols):
            if 0 <= r + d_row < rows and 0 <= c + d_col < cols:
                pairs.append((r * cols + c, (r + d_row) * cols + c + d_col))
    return lax.ppermute(value, ("row", "col"), pairs)


def swapped(value, flip_row, flip_col):
    rows, cols = lax.axis_size("row"), lax.axis_size("col")
    pairs = [(r * cols + c, (r ^ flip_row) * cols + (c ^ flip_col)) for r in range(rows) for c in range(cols)]
    return lax.ppermute(value, ("row", "col"), pairs)


def tables(side):
    index = np.arange(side)
    angle = (index[:, None] * index[None, :] % side) * (2.0 * math.pi / side)
    scale = 1.0 / math.sqrt(side)
    re = (np.cos(angle) * scale).astype(np.float32)
    im = (-np.sin(angle) * scale).astype(np.float32)
    blocks = []
    for first in (0, 1):
        a, b = re[first::2, :side // 2], im[first::2, :side // 2]
        blocks.append(np.block([[a, -b], [b, a]]))
    return jnp.asarray(np.stack(blocks + [block.T for block in blocks]), jnp.bfloat16)


def evens_first(amplitudes):
    side = amplitudes.shape[-1]
    order = np.concatenate([np.arange(0, side, 2), np.arange(1, side, 2)])
    pick = jnp.asarray(np.eye(side)[order], jnp.float32)
    rows = jnp.einsum("ab,sbc->sac", pick, amplitudes, precision=lax.Precision.HIGHEST)
    return jnp.einsum("sac,dc->sad", rows, pick, precision=lax.Precision.HIGHEST)


def corner_of(row, col):
    row_base = pl.multiple_of(row // SUBLANES * SUBLANES, SUBLANES)
    col_base = pl.multiple_of(col // LANES * LANES, LANES)
    return row_base, row - row_base, col_base, col - col_base


def window_at(ref, part, row, col, side):
    row_base, down, col_base, over = corner_of(row, col)
    groups = side // SUBLANES
    lane = lax.broadcasted_iota(jnp.int32, (side, LANES), 1)
    sub = lax.broadcasted_iota(jnp.int32, (groups, SUBLANES, LANES), 1)
    turned = []
    for j in range(side // LANES + 1):
        block = ref[part, pl.ds(row_base, side + SUBLANES), pl.ds(col_base + j * LANES, LANES)]
        block = block.reshape(groups + 1, SUBLANES, LANES)
        block = pltpu.roll(block, lax.rem(SUBLANES - down, SUBLANES), 1)
        block = jnp.where(sub < SUBLANES - down, block[:groups], block[1:]).reshape(side, LANES)
        turned.append(pltpu.roll(block, lax.rem(LANES - over, LANES), 1))
    parts = [jnp.where(lane < LANES - over, turned[j], turned[j + 1]) for j in range(side // LANES)]
    return jnp.concatenate(parts, axis=1)


def add_at(ref, part, row, col, value, side):
    row_base, down, col_base, over = corner_of(row, col)
    groups = side // SUBLANES
    blocks = side // LANES
    lane = lax.broadcasted_iota(jnp.int32, (side, LANES), 1)
    sub = lax.broadcasted_iota(jnp.int32, (groups + 1, SUBLANES, LANES), 1)
    turned = [pltpu.roll(value[:, j * LANES:(j + 1) * LANES], over, 1) for j in range(blocks)]
    none = jnp.zeros((side, LANES), value.dtype)
    gap = jnp.zeros((1, SUBLANES, LANES), value.dtype)
    for j in range(blocks + 1):
        block = jnp.where(lane >= over, turned[j] if j < blocks else none, turned[j - 1] if j else none)
        block = pltpu.roll(block.reshape(groups, SUBLANES, LANES), down, 1)
        block = jnp.where(
            sub >= down, jnp.concatenate([block, gap], axis=0), jnp.concatenate([gap, block], axis=0)
        )
        place = (part, pl.ds(row_base, side + SUBLANES), pl.ds(col_base + j * LANES, LANES))
        ref[place] += block.reshape(side + SUBLANES, LANES)


def main_kernel(
    counts_ref, spots_ref, tile_ref, below_ref, right_ref, corner_ref, amp_ref, probe_ref, top_ref, table_ref,
    g_tile, g_below, g_side, mine_ref, other_ref,
    ext, gacc, stage, turned, wave, wins, sums, in_sem, out_sem,
):
    modes, side = probe_ref.shape[1], probe_ref.shape[2]
    rows, cols = tile_ref.shape[1], tile_ref.shape[2]
    low = side // 2
    my_row, my_col = lax.axis_index("row"), lax.axis_index("col")
    loads = [
        pltpu.make_async_copy(ref, ext.at[:, pl.ds(r, ref.shape[1]), pl.ds(c, ref.shape[2])], in_sem.at[i])
        for i, (ref, r, c) in enumerate(
            ((tile_ref, 0, 0), (below_ref, rows, 0), (right_ref, 0, cols), (corner_ref, rows, cols))
        )
    ]
    for load in loads:
        load.start()
    gacc[...] = jnp.zeros_like(gacc)
    sums[...] = jnp.zeros_like(sums)
    for load in loads:
        load.wait()

    def dot(a, b):
        return jnp.dot(a, b, preferred_element_type=jnp.float32)

    def plane(index):
        return slice(index * side, (index + 1) * side)

    def bf16(value):
        return value.astype(jnp.bfloat16)

    def step(p, carry):
        row, col = spots_ref[p, 0] - my_row * rows, spots_ref[p, 1] - my_col * cols
        win_re = window_at(ext, 0, row, col, side)
        win_im = window_at(ext, 1, row, col, side)
        wins[0], wins[1] = win_re, win_im
        sums[plane(2 * modes)] += win_re * win_re + win_im * win_im
        for k in range(modes):
            pr, pi = probe_ref[0, k], probe_ref[1, k]
            for i, psi in enumerate((pr * win_re - pi * win_im, pr * win_im + pi * win_re)):
                stage[0, i * low:(i + 1) * low, plane(k)] = bf16(psi[:low] + psi[low:])
                stage[1, i * low:(i + 1) * low, plane(k)] = bf16(psi[:low] - psi[low:])
        for k in range(modes):
            for parity in range(2):
                half = dot(table_ref[parity], stage[parity, :, plane(k)])
                at = k * side + parity * low
                for i in range(2):
                    left, right = half[i * low:(i + 1) * low, :low], half[i * low:(i + 1) * low, low:]
                    turned[0, at:at + low, i * low:(i + 1) * low] = bf16(left + right)
                    turned[1, at:at + low, i * low:(i + 1) * low] = bf16(left - right)
        for parity in range(2):
            wave[parity] = dot(turned[parity], table_ref[2 + parity])
        for parity in range(2):
            model = jnp.zeros((side, low), jnp.float32)
            for k in range(modes):
                wr, wi = wave[parity, plane(k), :low], wave[parity, plane(k), low:]
                model += wr * wr + wi * wi
            factor = amp_ref[p, :, parity * low:(parity + 1) * low] * lax.rsqrt(jnp.maximum(model, 1.0)) - 1.0
            for k in range(modes):
                at = k * side + parity * low
                for i in range(2):
                    target = bf16(wave[parity, plane(k), i * low:(i + 1) * low] * factor)
                    stage[0, i * low:(i + 1) * low, at:at + low] = target[:low]
                    stage[1, i * low:(i + 1) * low, at:at + low] = target[low:]
        for k in range(modes):
            even = dot(table_ref[2], stage[0, :, plane(k)])
            odd = dot(table_ref[3], stage[1, :, plane(k)])
            for lower, back in enumerate((bf16(even + odd), bf16(even - odd))):
                at = k * side + lower * low
                for i in range(2):
                    for parity in range(2):
                        turned[parity, at:at + low, i * low:(i + 1) * low] = (
                            back[i * low:(i + 1) * low, parity * low:(parity + 1) * low]
                        )
        for parity in range(2):
            wave[parity] = dot(turned[parity], table_ref[parity])
        grads = []
        for lower in range(2):
            part = slice(lower * low, (lower + 1) * low)
            grad_re = jnp.zeros((side, low), jnp.float32)
            grad_im = jnp.zeros((side, low), jnp.float32)
            win_re, win_im = wins[0, :, part], wins[1, :, part]
            for k in range(modes):
                even_re, even_im = wave[0, plane(k), :low], wave[0, plane(k), low:]
                odd_re, odd_im = wave[1, plane(k), :low], wave[1, plane(k), low:]
                if lower:
                    cr, ci = even_re - odd_re, even_im - odd_im
                else:
                    cr, ci = even_re + odd_re, even_im + odd_im
                pr, pi = probe_ref[0, k, :, part], probe_ref[1, k, :, part]
                grad_re += pr * cr + pi * ci
                grad_im += pr * ci - pi * cr
                sums[plane(k), part] += win_re * cr + win_im * ci
                sums[plane(modes + k), part] += win_re * ci - win_im * cr
            grads.append((grad_re, grad_im))
        for i in range(2):
            add_at(gacc, i, row, col, jnp.concatenate([grads[0][i], grads[1][i]], axis=1), side)
        return carry

    lax.fori_loop(0, counts_ref[my_row, my_col], step, 0)

    pairs = lax.axis_size("row") // 2
    share = mine_ref.shape[0] // pairs - SUBLANES
    core = lax.rem(my_row, 2)
    stores = []
    for ref, base in ((other_ref, (1 - core) * (share * pairs)), (mine_ref, core * (share * pairs))):
        base = pl.multiple_of(base, SUBLANES)
        for j in range(pairs):
            at = j * (share + SUBLANES)
            stores.append((sums.at[pl.ds(base + j * share, share)], ref.at[pl.ds(at, share)]))
            stores.append((top_ref, ref.at[pl.ds(at + share, SUBLANES)]))
    stores.append((gacc.at[:, :, pl.ds(cols, side)], g_side))
    stores.append((gacc.at[:, pl.ds(0, rows), pl.ds(0, cols)], g_tile))
    stores.append((gacc.at[:, pl.ds(rows, side), pl.ds(0, cols)], g_below))
    stores = [pltpu.make_async_copy(a, b, out_sem.at[i]) for i, (a, b) in enumerate(stores)]
    for store in stores:
        store.start()
    for store in stores:
        store.wait()


def light_kernel(counts_ref, spots_ref, up_ref, left_ref, diag_ref, probe_ref, light_ref, top_ref, lit, acc):
    side = probe_ref.shape[2]
    rows, cols = light_ref.shape
    my_row, my_col = lax.axis_index("row"), lax.axis_index("col")
    lit[...] = jnp.sum(probe_ref[0] * probe_ref[0] + probe_ref[1] * probe_ref[1], axis=0)
    acc[...] = jnp.zeros_like(acc)
    for ref, d_row, d_col in ((spots_ref, 0, 0), (up_ref, 1, 0), (left_ref, 0, 1), (diag_ref, 1, 1)):
        inside = (my_row >= d_row) & (my_col >= d_col)
        number = counts_ref[jnp.maximum(my_row - d_row, 0), jnp.maximum(my_col - d_col, 0)]

        def step(p, carry, ref=ref):
            row, col = ref[p, 0] - my_row * rows + side, ref[p, 1] - my_col * cols + side

            @pl.when((row > 0) & (col > 0))
            def _():
                add_at(acc, 0, row, col, lit[...], side)

            return carry

        lax.fori_loop(0, jnp.where(inside, number, 0), step, 0)
    light = acc[0, side:side + rows, side:side + cols]
    light_ref[...] = light
    top = jnp.max(light, axis=0, keepdims=True)
    top = jnp.max(top, axis=1, keepdims=True)
    top_ref[...] = jnp.broadcast_to(top, top_ref.shape)


def merge(share, values):
    summed = jnp.arange(values[0].shape[0])[:, None] < share
    return functools.reduce(lambda a, b: jnp.where(summed, a + b, jnp.maximum(a, b)), values)


def finish_kernel(tile_ref, light_ref, top_ref, g_tile, g_left, g_up, out_ref):
    side = g_left.shape[2]
    rows, cols = light_ref.shape
    top = top_ref[0:1, 0:1]
    for at in range(0, cols, side):
        part = slice(at, at + side)
        scale = 1.0 / (light_ref[:, part] + 0.1 * top)
        for i in range(2):
            total = g_tile[i, :, part] + g_up[i, :, part]
            if at == 0:
                total += g_left[i, :rows]
            out_ref[i, :, part] = tile_ref[i, :, part] + total * scale


def probe_kernel(parts, probe_ref, *refs):
    pairs, n_col = parts
    block_refs, out_ref, sums = refs[:-2], refs[-2], refs[-1]
    modes, side = probe_ref.shape[1], probe_ref.shape[2]
    share = block_refs[0].shape[0]
    piece = share // n_col
    my_row, my_col = lax.axis_index("row"), lax.axis_index("col")
    core, pair = lax.rem(my_row, 2), my_row // 2
    for i, ref in enumerate(block_refs):
        flip, d = i // pairs, i % pairs
        base = ((core ^ flip) * pairs + (pair ^ d)) * share
        for e in range(n_col):
            to = pl.multiple_of(base + (my_col ^ e) * piece, SUBLANES)
            sums[pl.ds(to, piece)] = ref[e * piece:(e + 1) * piece]
    den = sums[2 * modes * side:(2 * modes + 1) * side]
    top = jnp.max(jnp.max(den, axis=0, keepdims=True), axis=1, keepdims=True)
    scale = 1.0 / (den + 0.1 * top)
    for k in range(modes):
        out_ref[0, k] = probe_ref[0, k] + sums[k * side:(k + 1) * side] * scale
        out_ref[1, k] = probe_ref[1, k] + sums[(modes + k) * side:(modes + k + 1) * side] * scale


def f32(*shape):
    return jax.ShapeDtypeStruct(shape, jnp.float32)


VM = pl.BlockSpec(memory_space=pltpu.VMEM)
SM = pl.BlockSpec(memory_space=pltpu.SMEM)
ANY = pl.BlockSpec(memory_space=pl.ANY)


def params(mib):
    return pltpu.CompilerParams(vmem_limit_bytes=mib * MIB)


def cost(flops, moved):
    return pl.CostEstimate(flops=flops, bytes_accessed=moved, transcendentals=0)


def body(object_field, probe, amplitudes, corners, counts):
    rows, cols = object_field.shape[1], object_field.shape[2]
    modes, side = probe.shape[1], probe.shape[2]
    pairs, n_col = lax.axis_size("row") // 2, lax.axis_size("col")
    step = SUBLANES * 2 * pairs * n_col
    total_rows = -(-(2 * modes + 1) * side // step) * step
    share = total_rows // (2 * pairs)
    piece = share // n_col
    pair, my_col = lax.axis_index("row") // 2, lax.axis_index("col")
    spots = corners[0, 0]

    right = shifted(object_field[:, :, :side], 0, -1)
    from_up = shifted(spots, 1, 0)
    from_left = shifted(spots, 0, 1)
    from_diag = shifted(spots, 1, 1)
    below = shifted(object_field[:, :side, :], -1, 0)
    light, top = pl.pallas_call(
        light_kernel,
        out_shape=(f32(rows, cols), f32(SUBLANES, side)),
        in_specs=[SM] * 5 + [VM],
        out_specs=(VM, VM),
        scratch_shapes=[
            pltpu.VMEM((side, side), jnp.float32),
            pltpu.VMEM((1, rows + 2 * side, cols + 2 * side), jnp.float32),
        ],
        compiler_params=params(12),
        cost_estimate=cost(10**8, 10**7),
        name="lighting",
    )(counts, spots, from_up, from_left, from_diag, probe)

    right, light = lax.optimization_barrier((right, light))
    corner = shifted(right[:, :side, :], -1, 0)
    g_tile, g_below, g_side, mine, other = pl.pallas_call(
        main_kernel,
        out_shape=(
            f32(2, rows, cols), f32(2, side, cols), f32(2, rows + side, side),
            f32(pairs * (share + SUBLANES), side), f32(pairs * (share + SUBLANES), side),
        ),
        in_specs=[SM] * 2 + [ANY] * 4 + [VM] * 4,
        out_specs=(ANY,) * 5,
        scratch_shapes=[
            pltpu.VMEM((2, rows + side, cols + side), jnp.float32),
            pltpu.VMEM((2, rows + side, cols + side), jnp.float32),
            pltpu.VMEM((2, side, modes * side), jnp.bfloat16),
            pltpu.VMEM((2, modes * side, side), jnp.bfloat16),
            pltpu.VMEM((2, modes * side, side), jnp.float32),
            pltpu.VMEM((2, side, side), jnp.float32),
            pltpu.VMEM((total_rows, side), jnp.float32),
            pltpu.SemaphoreType.DMA((4,)),
            pltpu.SemaphoreType.DMA((4 * pairs + 3,)),
        ],
        compiler_params=params(28),
        cost_estimate=cost(7 * 10**9, 2 * 10**7),
        name="positions",
    )(counts, spots, object_field, below, right, corner, evens_first(amplitudes[0, 0]), probe, top, tables(side))

    g_left = shifted(g_side, 0, 1)
    arrived = swapped(other, 1, 0)

    def cut(value, start, size):
        return lax.dynamic_slice_in_dim(value, start, size, 0)

    def chip_sum(d):
        start = (pair ^ d) * (share + SUBLANES)
        return merge(share, [cut(mine, start, share + SUBLANES), cut(arrived, start, share + SUBLANES)])

    plane_sum = merge(share, [chip_sum(0)] + [swapped(chip_sum(d), 2 * d, 0) for d in range(1, pairs)])
    lower = jnp.concatenate([g_below[:, :, :side] + g_left[:, rows:], g_below[:, :, side:]], axis=2)
    plane_sum, lower = lax.optimization_barrier((plane_sum, lower))
    g_up = shifted(lower, 1, 0)

    def col_part(e):
        return jnp.concatenate([cut(plane_sum, (my_col ^ e) * piece, piece), plane_sum[share:]], axis=0)

    own = merge(piece, [col_part(0)] + [swapped(col_part(e), 0, e) for e in range(1, n_col)])
    top = own[piece:]
    own = own[:piece]
    own = jnp.concatenate([own] + [swapped(own, 0, e) for e in range(1, n_col)], axis=0)
    object_new = pl.pallas_call(
        finish_kernel,
        out_shape=f32(2, rows, cols),
        in_specs=[VM] * 6,
        out_specs=VM,
        compiler_params=params(10),
        cost_estimate=cost(10**6, 6 * 10**6),
        name="object_update",
    )(object_field, light, top, g_tile, g_left, g_up)
    own, object_new = lax.optimization_barrier((own, object_new))
    blocks = [own] + [swapped(own, 2 * d, 0) for d in range(1, pairs)]
    blocks = blocks + [swapped(block, 1, 0) for block in blocks]
    probe_new = pl.pallas_call(
        functools.partial(probe_kernel, (pairs, n_col)),
        out_shape=f32(*probe.shape),
        in_specs=[VM] * (1 + len(blocks)),
        out_specs=VM,
        scratch_shapes=[pltpu.VMEM((total_rows, side), jnp.float32)],
        compiler_params=params(14),
        cost_estimate=cost(10**6, 6 * 10**6),
        name="probe_update",
    )(probe, *blocks)
    return object_new, probe_new


def solution(mesh):
    in_specs = (
        P(None, "row", "col"),
        P(),
        P("row", "col", None, None, None),
        P("row", "col", None, None),
        P(),
    )
    out_specs = (P(None, "row", "col"), P())
    return jax.shard_map(body, mesh=mesh, in_specs=in_specs, out_specs=out_specs, check_vma=False)
```

```python
import functools
import math

import jax
import jax.numpy as jnp
import numpy as np
from jax import lax
from jax.experimental import pallas as pl
from jax.experimental.pallas import tpu as pltpu
from jax.sharding import PartitionSpec as P

LANES = 128
SUBLANES = 8
MIB = 1024 * 1024


def shifted(value, d_row, d_col):
    rows, cols = lax.axis_size("row"), lax.axis_size("col")
    pairs = []
    for r in range(rows):
        for c in range(cols):
            if 0 <= r + d_row < rows and 0 <= c + d_col < cols:
                pairs.append((r * cols + c, (r + d_row) * cols + c + d_col))
    return lax.ppermute(value, ("row", "col"), pairs)


def swapped(value, flip_row, flip_col):
    rows, cols = lax.axis_size("row"), lax.axis_size("col")
    pairs = [(r * cols + c, (r ^ flip_row) * cols + (c ^ flip_col)) for r in range(rows) for c in range(cols)]
    return lax.ppermute(value, ("row", "col"), pairs)


def tables(side):
    index = np.arange(side)
    angle = (index[:, None] * index[None, :] % side) * (2.0 * math.pi / side)
    scale = 1.0 / math.sqrt(side)
    re = (np.cos(angle) * scale).astype(np.float32)
    im = (-np.sin(angle) * scale).astype(np.float32)
    blocks = []
    for first in (0, 1):
        a, b = re[first::2, :side // 2], im[first::2, :side // 2]
        blocks.append(np.block([[a, -b], [b, a]]))
    return jnp.asarray(np.stack(blocks + [block.T for block in blocks]), jnp.bfloat16)


def evens_first(amplitudes):
    side = amplitudes.shape[-1]
    order = np.concatenate([np.arange(0, side, 2), np.arange(1, side, 2)])
    pick = jnp.asarray(np.eye(side)[order], jnp.float32)
    rows = jnp.einsum("ab,sbc->sac", pick, amplitudes, precision=lax.Precision.HIGHEST)
    return jnp.einsum("sac,dc->sad", rows, pick, precision=lax.Precision.HIGHEST)


def corner_of(row, col):
    row_base = pl.multiple_of(row // SUBLANES * SUBLANES, SUBLANES)
    col_base = pl.multiple_of(col // LANES * LANES, LANES)
    return row_base, row - row_base, col_base, col - col_base


def window_at(ref, part, row, col, side):
    row_base, down, col_base, over = corner_of(row, col)
    groups = side // SUBLANES
    lane = lax.broadcasted_iota(jnp.int32, (side, LANES), 1)
    sub = lax.broadcasted_iota(jnp.int32, (groups, SUBLANES, LANES), 1)
    turned = []
    for j in range(side // LANES + 1):
        block = ref[part, pl.ds(row_base, side + SUBLANES), pl.ds(col_base + j * LANES, LANES)]
        block = block.reshape(groups + 1, SUBLANES, LANES)
        block = pltpu.roll(block, lax.rem(SUBLANES - down, SUBLANES), 1)
        block = jnp.where(sub < SUBLANES - down, block[:groups], block[1:]).reshape(side, LANES)
        turned.append(pltpu.roll(block, lax.rem(LANES - over, LANES), 1))
    parts = [jnp.where(lane < LANES - over, turned[j], turned[j + 1]) for j in range(side // LANES)]
    return jnp.concatenate(parts, axis=1)


def add_at(ref, part, row, col, value, side):
    row_base, down, col_base, over = corner_of(row, col)
    groups = side // SUBLANES
    blocks = side // LANES
    lane = lax.broadcasted_iota(jnp.int32, (side, LANES), 1)
    sub = lax.broadcasted_iota(jnp.int32, (groups + 1, SUBLANES, LANES), 1)
    turned = [pltpu.roll(value[:, j * LANES:(j + 1) * LANES], over, 1) for j in range(blocks)]
    none = jnp.zeros((side, LANES), value.dtype)
    gap = jnp.zeros((1, SUBLANES, LANES), value.dtype)
    for j in range(blocks + 1):
        block = jnp.where(lane >= over, turned[j] if j < blocks else none, turned[j - 1] if j else none)
        block = pltpu.roll(block.reshape(groups, SUBLANES, LANES), down, 1)
        block = jnp.where(
            sub >= down, jnp.concatenate([block, gap], axis=0), jnp.concatenate([gap, block], axis=0)
        )
        place = (part, pl.ds(row_base, side + SUBLANES), pl.ds(col_base + j * LANES, LANES))
        ref[place] += block.reshape(side + SUBLANES, LANES)


def main_kernel(
    counts_ref, spots_ref, tile_ref, below_ref, right_ref, corner_ref, amp_ref, probe_ref, top_ref, table_ref,
    g_tile, g_lower, g_right, mine_ref, other_ref,
    ext, gacc, stage, turned, wave, wins, sums, in_sem, out_sem,
):
    modes, side = probe_ref.shape[1], probe_ref.shape[2]
    rows, cols = tile_ref.shape[1], tile_ref.shape[2]
    low = side // 2
    my_row, my_col = lax.axis_index("row"), lax.axis_index("col")
    loads = [
        pltpu.make_async_copy(ref, ext.at[:, pl.ds(r, ref.shape[1]), pl.ds(c, ref.shape[2])], in_sem.at[i])
        for i, (ref, r, c) in enumerate(
            ((tile_ref, 0, 0), (below_ref, rows, 0), (right_ref, 0, cols), (corner_ref, rows, cols))
        )
    ]
    for load in loads:
        load.start()
    gacc[...] = jnp.zeros_like(gacc)
    sums[...] = jnp.zeros_like(sums)
    for load in loads:
        load.wait()

    def dot(a, b):
        return jnp.dot(a, b, preferred_element_type=jnp.float32)

    def plane(index):
        return slice(index * side, (index + 1) * side)

    def bf16(value):
        return value.astype(jnp.bfloat16)

    def step(p, carry):
        row, col = spots_ref[p, 0] - my_row * rows, spots_ref[p, 1] - my_col * cols
        win_re = window_at(ext, 0, row, col, side)
        win_im = window_at(ext, 1, row, col, side)
        wins[0], wins[1] = win_re, win_im
        sums[plane(2 * modes)] += win_re * win_re + win_im * win_im
        for k in range(modes):
            pr, pi = probe_ref[0, k], probe_ref[1, k]
            for i, psi in enumerate((pr * win_re - pi * win_im, pr * win_im + pi * win_re)):
                stage[0, i * low:(i + 1) * low, plane(k)] = bf16(psi[:low] + psi[low:])
                stage[1, i * low:(i + 1) * low, plane(k)] = bf16(psi[:low] - psi[low:])
        for k in range(modes):
            for parity in range(2):
                half = dot(table_ref[parity], stage[parity, :, plane(k)])
                at = k * side + parity * low
                for i in range(2):
                    left, right = half[i * low:(i + 1) * low, :low], half[i * low:(i + 1) * low, low:]
                    turned[0, at:at + low, i * low:(i + 1) * low] = bf16(left + right)
                    turned[1, at:at + low, i * low:(i + 1) * low] = bf16(left - right)
        for parity in range(2):
            wave[parity] = dot(turned[parity], table_ref[2 + parity])
        for parity in range(2):
            model = jnp.zeros((side, low), jnp.float32)
            for k in range(modes):
                wr, wi = wave[parity, plane(k), :low], wave[parity, plane(k), low:]
                model += wr * wr + wi * wi
            factor = amp_ref[p, :, parity * low:(parity + 1) * low] * lax.rsqrt(jnp.maximum(model, 1.0)) - 1.0
            for k in range(modes):
                at = k * side + parity * low
                for i in range(2):
                    target = bf16(wave[parity, plane(k), i * low:(i + 1) * low] * factor)
                    stage[0, i * low:(i + 1) * low, at:at + low] = target[:low]
                    stage[1, i * low:(i + 1) * low, at:at + low] = target[low:]
        for k in range(modes):
            even = dot(table_ref[2], stage[0, :, plane(k)])
            odd = dot(table_ref[3], stage[1, :, plane(k)])
            for lower, back in enumerate((bf16(even + odd), bf16(even - odd))):
                at = k * side + lower * low
                for i in range(2):
                    for parity in range(2):
                        turned[parity, at:at + low, i * low:(i + 1) * low] = (
                            back[i * low:(i + 1) * low, parity * low:(parity + 1) * low]
                        )
        for parity in range(2):
            wave[parity] = dot(turned[parity], table_ref[parity])
        grads = []
        for lower in range(2):
            part = slice(lower * low, (lower + 1) * low)
            grad_re = jnp.zeros((side, low), jnp.float32)
            grad_im = jnp.zeros((side, low), jnp.float32)
            win_re, win_im = wins[0, :, part], wins[1, :, part]
            for k in range(modes):
                even_re, even_im = wave[0, plane(k), :low], wave[0, plane(k), low:]
                odd_re, odd_im = wave[1, plane(k), :low], wave[1, plane(k), low:]
                if lower:
                    cr, ci = even_re - odd_re, even_im - odd_im
                else:
                    cr, ci = even_re + odd_re, even_im + odd_im
                pr, pi = probe_ref[0, k, :, part], probe_ref[1, k, :, part]
                grad_re += pr * cr + pi * ci
                grad_im += pr * ci - pi * cr
                sums[plane(k), part] += win_re * cr + win_im * ci
                sums[plane(modes + k), part] += win_re * ci - win_im * cr
            grads.append((grad_re, grad_im))
        for i in range(2):
            add_at(gacc, i, row, col, jnp.concatenate([grads[0][i], grads[1][i]], axis=1), side)
        return carry

    lax.fori_loop(0, counts_ref[my_row, my_col], step, 0)

    pairs = lax.axis_size("row") // 2
    share = mine_ref.shape[0] // pairs - SUBLANES
    core = lax.rem(my_row, 2)
    stores = []
    for ref, base in ((other_ref, (1 - core) * (share * pairs)), (mine_ref, core * (share * pairs))):
        base = pl.multiple_of(base, SUBLANES)
        for j in range(pairs):
            at = j * (share + SUBLANES)
            stores.append((sums.at[pl.ds(base + j * share, share)], ref.at[pl.ds(at, share)]))
            stores.append((top_ref, ref.at[pl.ds(at + share, SUBLANES)]))
    stores.append((gacc.at[:, pl.ds(0, rows), pl.ds(cols, side)], g_right))
    stores.append((gacc.at[:, pl.ds(0, rows), pl.ds(0, cols)], g_tile))
    stores.append((gacc.at[:, pl.ds(rows, side)], g_lower))
    stores = [pltpu.make_async_copy(a, b, out_sem.at[i]) for i, (a, b) in enumerate(stores)]
    for store in stores:
        store.start()
    for store in stores:
        store.wait()


def light_kernel(counts_ref, spots_ref, up_ref, left_ref, diag_ref, probe_ref, light_ref, top_ref, lit, acc):
    side = probe_ref.shape[2]
    rows, cols = light_ref.shape
    my_row, my_col = lax.axis_index("row"), lax.axis_index("col")
    lit[...] = jnp.sum(probe_ref[0] * probe_ref[0] + probe_ref[1] * probe_ref[1], axis=0)
    acc[...] = jnp.zeros_like(acc)
    for ref, d_row, d_col in ((spots_ref, 0, 0), (up_ref, 1, 0), (left_ref, 0, 1), (diag_ref, 1, 1)):
        inside = (my_row >= d_row) & (my_col >= d_col)
        number = counts_ref[jnp.maximum(my_row - d_row, 0), jnp.maximum(my_col - d_col, 0)]

        def step(p, carry, ref=ref):
            row, col = ref[p, 0] - my_row * rows + side, ref[p, 1] - my_col * cols + side

            @pl.when((row > 0) & (col > 0))
            def _():
                add_at(acc, 0, row, col, lit[...], side)

            return carry

        lax.fori_loop(0, jnp.where(inside, number, 0), step, 0)
    light = acc[0, side:side + rows, side:side + cols]
    light_ref[...] = light
    top = jnp.max(light, axis=0, keepdims=True)
    top = jnp.max(top, axis=1, keepdims=True)
    top_ref[...] = jnp.broadcast_to(top, top_ref.shape)


def merge(share, values):
    summed = jnp.arange(values[0].shape[0])[:, None] < share
    return functools.reduce(lambda a, b: jnp.where(summed, a + b, jnp.maximum(a, b)), values)


def finish_kernel(tile_ref, light_ref, top_ref, g_tile, g_left, g_up, g_diag, out_ref):
    side = g_left.shape[2]
    rows, cols = light_ref.shape
    top = top_ref[0:1, 0:1]
    for at in range(0, cols, side):
        part = slice(at, at + side)
        scale = 1.0 / (light_ref[:, part] + 0.1 * top)
        for i in range(2):
            total = g_tile[i, :, part] + g_up[i, :, part]
            if at == 0:
                total += g_left[i] + g_diag[i]
            out_ref[i, :, part] = tile_ref[i, :, part] + total * scale


def probe_kernel(parts, probe_ref, *refs):
    pairs, n_col = parts
    block_refs, out_ref, sums = refs[:-2], refs[-2], refs[-1]
    modes, side = probe_ref.shape[1], probe_ref.shape[2]
    share = block_refs[0].shape[0]
    piece = share // n_col
    my_row, my_col = lax.axis_index("row"), lax.axis_index("col")
    core, pair = lax.rem(my_row, 2), my_row // 2
    for i, ref in enumerate(block_refs):
        flip, d = i // pairs, i % pairs
        base = ((core ^ flip) * pairs + (pair ^ d)) * share
        for e in range(n_col):
            to = pl.multiple_of(base + (my_col ^ e) * piece, SUBLANES)
            sums[pl.ds(to, piece)] = ref[e * piece:(e + 1) * piece]
    den = sums[2 * modes * side:(2 * modes + 1) * side]
    top = jnp.max(jnp.max(den, axis=0, keepdims=True), axis=1, keepdims=True)
    scale = 1.0 / (den + 0.1 * top)
    for k in range(modes):
        out_ref[0, k] = probe_ref[0, k] + sums[k * side:(k + 1) * side] * scale
        out_ref[1, k] = probe_ref[1, k] + sums[(modes + k) * side:(modes + k + 1) * side] * scale


def f32(*shape):
    return jax.ShapeDtypeStruct(shape, jnp.float32)


VM = pl.BlockSpec(memory_space=pltpu.VMEM)
SM = pl.BlockSpec(memory_space=pltpu.SMEM)
ANY = pl.BlockSpec(memory_space=pl.ANY)
HBM = pl.BlockSpec(memory_space=pltpu.HBM)


def params(mib):
    return pltpu.CompilerParams(vmem_limit_bytes=mib * MIB)


def cost(flops, moved):
    return pl.CostEstimate(flops=flops, bytes_accessed=moved, transcendentals=0)


def body(object_field, probe, amplitudes, corners, counts):
    rows, cols = object_field.shape[1], object_field.shape[2]
    modes, side = probe.shape[1], probe.shape[2]
    pairs, n_col = lax.axis_size("row") // 2, lax.axis_size("col")
    step = SUBLANES * 2 * pairs * n_col
    total_rows = -(-(2 * modes + 1) * side // step) * step
    share = total_rows // (2 * pairs)
    piece = share // n_col
    pair, my_col = lax.axis_index("row") // 2, lax.axis_index("col")
    spots = corners[0, 0]

    right = shifted(object_field[:, :, :side], 0, -1)
    from_up = shifted(spots, 1, 0)
    from_left = shifted(spots, 0, 1)
    from_diag = shifted(spots, 1, 1)
    below = shifted(object_field[:, :side, :], -1, 0)
    right, from_up, from_left, from_diag = lax.optimization_barrier((right, from_up, from_left, from_diag))
    corner = shifted(right[:, :side, :], -1, 0)
    light, top = pl.pallas_call(
        light_kernel,
        out_shape=(f32(rows, cols), f32(SUBLANES, side)),
        in_specs=[SM] * 5 + [VM],
        out_specs=(VM, VM),
        scratch_shapes=[
            pltpu.VMEM((side, side), jnp.float32),
            pltpu.VMEM((1, rows + 2 * side, cols + 2 * side), jnp.float32),
        ],
        compiler_params=params(12),
        cost_estimate=cost(10**8, 10**7),
        name="lighting",
    )(counts, spots, from_up, from_left, from_diag, probe)

    g_tile, g_lower, g_right, mine, other = pl.pallas_call(
        main_kernel,
        out_shape=(
            f32(2, rows, cols), f32(2, side, cols + side), f32(2, rows, side),
            f32(pairs * (share + SUBLANES), side), f32(pairs * (share + SUBLANES), side),
        ),
        in_specs=[SM] * 2 + [ANY] * 4 + [VM] * 4,
        out_specs=(HBM,) * 5,
        scratch_shapes=[
            pltpu.VMEM((2, rows + side, cols + side), jnp.float32),
            pltpu.VMEM((2, rows + side, cols + side), jnp.float32),
            pltpu.VMEM((2, side, modes * side), jnp.bfloat16),
            pltpu.VMEM((2, modes * side, side), jnp.bfloat16),
            pltpu.VMEM((2, modes * side, side), jnp.float32),
            pltpu.VMEM((2, side, side), jnp.float32),
            pltpu.VMEM((total_rows, side), jnp.float32),
            pltpu.SemaphoreType.DMA((4,)),
            pltpu.SemaphoreType.DMA((4 * pairs + 3,)),
        ],
        compiler_params=params(28),
        cost_estimate=cost(7 * 10**9, 2 * 10**7),
        name="positions",
    )(counts, spots, object_field, below, right, corner, evens_first(amplitudes[0, 0]), probe, top, tables(side))

    arrived = swapped(other, 1, 0)
    g_left = shifted(g_right, 0, 1)

    def cut(value, start, size):
        return lax.dynamic_slice_in_dim(value, start, size, 0)

    def chip_sum(d):
        start = (pair ^ d) * (share + SUBLANES)
        return merge(share, [cut(mine, start, share + SUBLANES), cut(arrived, start, share + SUBLANES)])

    plane_sum = merge(share, [chip_sum(0)] + [swapped(chip_sum(d), 2 * d, 0) for d in range(1, pairs)])
    plane_sum, g_lower, g_left = lax.optimization_barrier((plane_sum, g_lower, g_left))
    g_up = shifted(g_lower, 1, 0)

    def col_part(e):
        return jnp.concatenate([cut(plane_sum, (my_col ^ e) * piece, piece), plane_sum[share:]], axis=0)

    own = merge(piece, [col_part(0)] + [swapped(col_part(e), 0, e) for e in range(1, n_col)])
    top = own[piece:]
    own = own[:piece]
    own = jnp.concatenate([own] + [swapped(own, 0, e) for e in range(1, n_col)], axis=0)
    own, g_up = lax.optimization_barrier((own, g_up))
    g_diag = shifted(g_up[:, :, cols:], 0, 1)
    object_new = pl.pallas_call(
        finish_kernel,
        out_shape=f32(2, rows, cols),
        in_specs=[VM] * 7,
        out_specs=VM,
        compiler_params=params(10),
        cost_estimate=cost(10**6, 6 * 10**6),
        name="object_update",
    )(object_field, light, top, g_tile, g_left, g_up, g_diag)
    blocks = [own] + [swapped(own, 2 * d, 0) for d in range(1, pairs)]
    blocks = blocks + [swapped(block, 1, 0) for block in blocks]
    probe_new = pl.pallas_call(
        functools.partial(probe_kernel, (pairs, n_col)),
        out_shape=f32(*probe.shape),
        in_specs=[VM] * (1 + len(blocks)),
        out_specs=VM,
        scratch_shapes=[pltpu.VMEM((total_rows, side), jnp.float32)],
        compiler_params=params(14),
        cost_estimate=cost(10**6, 6 * 10**6),
        name="probe_update",
    )(probe, *blocks)
    return object_new, probe_new


def solution(mesh):
    in_specs = (
        P(None, "row", "col"),
        P(),
        P("row", "col", None, None, None),
        P("row", "col", None, None),
        P(),
    )
    out_specs = (P(None, "row", "col"), P())
    return jax.shard_map(body, mesh=mesh, in_specs=in_specs, out_specs=out_specs, check_vma=False)
```

```python
import functools
import math

import jax
import jax.numpy as jnp
import numpy as np
from jax import lax
from jax.experimental import pallas as pl
from jax.experimental.pallas import tpu as pltpu
from jax.sharding import PartitionSpec as P

LANES = 128
SUBLANES = 8
MIB = 1024 * 1024


def shifted(value, d_row, d_col):
    rows, cols = lax.axis_size("row"), lax.axis_size("col")
    pairs = []
    for r in range(rows):
        for c in range(cols):
            if 0 <= r + d_row < rows and 0 <= c + d_col < cols:
                pairs.append((r * cols + c, (r + d_row) * cols + c + d_col))
    return lax.ppermute(value, ("row", "col"), pairs)


def swapped(value, flip_row, flip_col):
    rows, cols = lax.axis_size("row"), lax.axis_size("col")
    pairs = [(r * cols + c, (r ^ flip_row) * cols + (c ^ flip_col)) for r in range(rows) for c in range(cols)]
    return lax.ppermute(value, ("row", "col"), pairs)


def tables(side):
    index = np.arange(side)
    angle = (index[:, None] * index[None, :] % side) * (2.0 * math.pi / side)
    scale = 1.0 / math.sqrt(side)
    re = (np.cos(angle) * scale).astype(np.float32)
    im = (-np.sin(angle) * scale).astype(np.float32)
    blocks = []
    for first in (0, 1):
        a, b = re[first::2, :side // 2], im[first::2, :side // 2]
        blocks.append(np.block([[a, -b], [b, a]]))
    return jnp.asarray(np.stack(blocks + [block.T for block in blocks]), jnp.bfloat16)


def evens_first(amplitudes):
    side = amplitudes.shape[-1]
    order = np.concatenate([np.arange(0, side, 2), np.arange(1, side, 2)])
    pick = jnp.asarray(np.eye(side)[order], jnp.float32)
    rows = jnp.einsum("ab,sbc->sac", pick, amplitudes, precision=lax.Precision.HIGHEST)
    return jnp.einsum("sac,dc->sad", rows, pick, precision=lax.Precision.HIGHEST)


def corner_of(row, col):
    row_base = pl.multiple_of(row // SUBLANES * SUBLANES, SUBLANES)
    col_base = pl.multiple_of(col // LANES * LANES, LANES)
    return row_base, row - row_base, col_base, col - col_base


def window_at(ref, part, row, col, side):
    row_base, down, col_base, over = corner_of(row, col)
    groups = side // SUBLANES
    lane = lax.broadcasted_iota(jnp.int32, (side, LANES), 1)
    sub = lax.broadcasted_iota(jnp.int32, (groups, SUBLANES, LANES), 1)
    turned = []
    for j in range(side // LANES + 1):
        block = ref[part, pl.ds(row_base, side + SUBLANES), pl.ds(col_base + j * LANES, LANES)]
        block = block.reshape(groups + 1, SUBLANES, LANES)
        block = pltpu.roll(block, lax.rem(SUBLANES - down, SUBLANES), 1)
        block = jnp.where(sub < SUBLANES - down, block[:groups], block[1:]).reshape(side, LANES)
        turned.append(pltpu.roll(block, lax.rem(LANES - over, LANES), 1))
    parts = [jnp.where(lane < LANES - over, turned[j], turned[j + 1]) for j in range(side // LANES)]
    return jnp.concatenate(parts, axis=1)


def add_at(ref, part, row, col, value, side):
    row_base, down, col_base, over = corner_of(row, col)
    groups = side // SUBLANES
    blocks = side // LANES
    lane = lax.broadcasted_iota(jnp.int32, (side, LANES), 1)
    sub = lax.broadcasted_iota(jnp.int32, (groups + 1, SUBLANES, LANES), 1)
    turned = [pltpu.roll(value[:, j * LANES:(j + 1) * LANES], over, 1) for j in range(blocks)]
    none = jnp.zeros((side, LANES), value.dtype)
    gap = jnp.zeros((1, SUBLANES, LANES), value.dtype)
    for j in range(blocks + 1):
        block = jnp.where(lane >= over, turned[j] if j < blocks else none, turned[j - 1] if j else none)
        block = pltpu.roll(block.reshape(groups, SUBLANES, LANES), down, 1)
        block = jnp.where(
            sub >= down, jnp.concatenate([block, gap], axis=0), jnp.concatenate([gap, block], axis=0)
        )
        place = (part, pl.ds(row_base, side + SUBLANES), pl.ds(col_base + j * LANES, LANES))
        ref[place] += block.reshape(side + SUBLANES, LANES)


def main_kernel(
    counts_ref, spots_ref, tile_ref, below_ref, right_ref, corner_ref, amp_ref, probe_ref, table_ref,
    g_tile, g_lower, g_right, mine_ref, other_ref,
    ext, gacc, stage, turned, wave, wins, sums, in_sem, out_sem,
):
    modes, side = probe_ref.shape[1], probe_ref.shape[2]
    rows, cols = tile_ref.shape[1], tile_ref.shape[2]
    low = side // 2
    my_row, my_col = lax.axis_index("row"), lax.axis_index("col")
    loads = [
        pltpu.make_async_copy(ref, ext.at[:, pl.ds(r, ref.shape[1]), pl.ds(c, ref.shape[2])], in_sem.at[i])
        for i, (ref, r, c) in enumerate(
            ((tile_ref, 0, 0), (below_ref, rows, 0), (right_ref, 0, cols), (corner_ref, rows, cols))
        )
    ]
    for load in loads:
        load.start()
    gacc[...] = jnp.zeros_like(gacc)
    sums[...] = jnp.zeros_like(sums)
    for load in loads:
        load.wait()

    def dot(a, b):
        return jnp.dot(a, b, preferred_element_type=jnp.float32)

    def plane(index):
        return slice(index * side, (index + 1) * side)

    def bf16(value):
        return value.astype(jnp.bfloat16)

    def step(p, carry):
        row, col = spots_ref[p, 0] - my_row * rows, spots_ref[p, 1] - my_col * cols
        win_re = window_at(ext, 0, row, col, side)
        win_im = window_at(ext, 1, row, col, side)
        wins[0], wins[1] = win_re, win_im
        sums[plane(2 * modes)] += win_re * win_re + win_im * win_im
        for k in range(modes):
            pr, pi = probe_ref[0, k], probe_ref[1, k]
            for i, psi in enumerate((pr * win_re - pi * win_im, pr * win_im + pi * win_re)):
                stage[0, i * low:(i + 1) * low, plane(k)] = bf16(psi[:low] + psi[low:])
                stage[1, i * low:(i + 1) * low, plane(k)] = bf16(psi[:low] - psi[low:])
        for k in range(modes):
            for parity in range(2):
                half = dot(table_ref[parity], stage[parity, :, plane(k)])
                at = k * side + parity * low
                for i in range(2):
                    left, right = half[i * low:(i + 1) * low, :low], half[i * low:(i + 1) * low, low:]
                    turned[0, at:at + low, i * low:(i + 1) * low] = bf16(left + right)
                    turned[1, at:at + low, i * low:(i + 1) * low] = bf16(left - right)
        for parity in range(2):
            wave[parity] = dot(turned[parity], table_ref[2 + parity])
        for parity in range(2):
            model = jnp.zeros((side, low), jnp.float32)
            for k in range(modes):
                wr, wi = wave[parity, plane(k), :low], wave[parity, plane(k), low:]
                model += wr * wr + wi * wi
            factor = amp_ref[p, :, parity * low:(parity + 1) * low] * lax.rsqrt(jnp.maximum(model, 1.0)) - 1.0
            for k in range(modes):
                at = k * side + parity * low
                for i in range(2):
                    target = bf16(wave[parity, plane(k), i * low:(i + 1) * low] * factor)
                    stage[0, i * low:(i + 1) * low, at:at + low] = target[:low]
                    stage[1, i * low:(i + 1) * low, at:at + low] = target[low:]
        for k in range(modes):
            even = dot(table_ref[2], stage[0, :, plane(k)])
            odd = dot(table_ref[3], stage[1, :, plane(k)])
            for lower, back in enumerate((bf16(even + odd), bf16(even - odd))):
                at = k * side + lower * low
                for i in range(2):
                    for parity in range(2):
                        turned[parity, at:at + low, i * low:(i + 1) * low] = (
                            back[i * low:(i + 1) * low, parity * low:(parity + 1) * low]
                        )
        for parity in range(2):
            wave[parity] = dot(turned[parity], table_ref[parity])
        grads = []
        for lower in range(2):
            part = slice(lower * low, (lower + 1) * low)
            grad_re = jnp.zeros((side, low), jnp.float32)
            grad_im = jnp.zeros((side, low), jnp.float32)
            win_re, win_im = wins[0, :, part], wins[1, :, part]
            for k in range(modes):
                even_re, even_im = wave[0, plane(k), :low], wave[0, plane(k), low:]
                odd_re, odd_im = wave[1, plane(k), :low], wave[1, plane(k), low:]
                if lower:
                    cr, ci = even_re - odd_re, even_im - odd_im
                else:
                    cr, ci = even_re + odd_re, even_im + odd_im
                pr, pi = probe_ref[0, k, :, part], probe_ref[1, k, :, part]
                grad_re += pr * cr + pi * ci
                grad_im += pr * ci - pi * cr
                sums[plane(k), part] += win_re * cr + win_im * ci
                sums[plane(modes + k), part] += win_re * ci - win_im * cr
            grads.append((grad_re, grad_im))
        for i in range(2):
            add_at(gacc, i, row, col, jnp.concatenate([grads[0][i], grads[1][i]], axis=1), side)
        return carry

    lax.fori_loop(0, counts_ref[my_row, my_col], step, 0)

    pairs = lax.axis_size("row") // 2
    share = mine_ref.shape[1]
    core = lax.rem(my_row, 2)
    stores = []
    for ref, base in ((other_ref, (1 - core) * (share * pairs)), (mine_ref, core * (share * pairs))):
        base = pl.multiple_of(base, SUBLANES)
        for j in range(pairs):
            stores.append((sums.at[pl.ds(base + j * share, share)], ref.at[j]))
    stores.append((gacc.at[:, pl.ds(0, rows), pl.ds(cols, side)], g_right))
    stores.append((gacc.at[:, pl.ds(0, rows), pl.ds(0, cols)], g_tile))
    stores.append((gacc.at[:, pl.ds(rows, side)], g_lower))
    stores = [pltpu.make_async_copy(a, b, out_sem.at[i]) for i, (a, b) in enumerate(stores)]
    for store in stores:
        store.start()
    for store in stores:
        store.wait()


def light_kernel(counts_ref, spots_ref, up_ref, left_ref, diag_ref, probe_ref, light_ref, top_ref, lit, acc):
    side = probe_ref.shape[2]
    rows, cols = light_ref.shape
    my_row, my_col = lax.axis_index("row"), lax.axis_index("col")
    lit[...] = jnp.sum(probe_ref[0] * probe_ref[0] + probe_ref[1] * probe_ref[1], axis=0)
    acc[...] = jnp.zeros_like(acc)
    for ref, d_row, d_col in ((spots_ref, 0, 0), (up_ref, 1, 0), (left_ref, 0, 1), (diag_ref, 1, 1)):
        inside = (my_row >= d_row) & (my_col >= d_col)
        number = counts_ref[jnp.maximum(my_row - d_row, 0), jnp.maximum(my_col - d_col, 0)]

        def step(p, carry, ref=ref):
            row, col = ref[p, 0] - my_row * rows + side, ref[p, 1] - my_col * cols + side

            @pl.when((row > 0) & (col > 0))
            def _():
                add_at(acc, 0, row, col, lit[...], side)

            return carry

        lax.fori_loop(0, jnp.where(inside, number, 0), step, 0)
    light = acc[0, side:side + rows, side:side + cols]
    light_ref[...] = light
    top = jnp.max(light, axis=0, keepdims=True)
    top = jnp.max(top, axis=1, keepdims=True)
    top_ref[...] = jnp.broadcast_to(top, top_ref.shape)


def finish_kernel(tile_ref, light_ref, top_ref, g_tile, g_left, g_up, g_diag, out_ref):
    side = g_left.shape[2]
    rows, cols = light_ref.shape
    top = top_ref[0:1, 0:1]
    for at in range(0, cols, side):
        part = slice(at, at + side)
        scale = 1.0 / (light_ref[:, part] + 0.1 * top)
        for i in range(2):
            total = g_tile[i, :, part] + g_up[i, :, part]
            if at == 0:
                total += g_left[i] + g_diag[i]
            out_ref[i, :, part] = tile_ref[i, :, part] + total * scale


def probe_kernel(parts, probe_ref, *refs):
    pairs, n_col = parts
    block_refs, out_ref, sums = refs[:-2], refs[-2], refs[-1]
    modes, side = probe_ref.shape[1], probe_ref.shape[2]
    share = block_refs[0].shape[0] - SUBLANES
    piece = share // n_col
    my_row, my_col = lax.axis_index("row"), lax.axis_index("col")
    core, pair = lax.rem(my_row, 2), my_row // 2
    for i, ref in enumerate(block_refs):
        flip, d = i // pairs, i % pairs
        base = ((core ^ flip) * pairs + (pair ^ d)) * share
        for e in range(n_col):
            to = pl.multiple_of(base + (my_col ^ e) * piece, SUBLANES)
            sums[pl.ds(to, piece)] = ref[e * piece:(e + 1) * piece]
    den = sums[2 * modes * side:(2 * modes + 1) * side]
    top = jnp.max(jnp.max(den, axis=0, keepdims=True), axis=1, keepdims=True)
    scale = 1.0 / (den + 0.1 * top)
    for k in range(modes):
        out_ref[0, k] = probe_ref[0, k] + sums[k * side:(k + 1) * side] * scale
        out_ref[1, k] = probe_ref[1, k] + sums[(modes + k) * side:(modes + k + 1) * side] * scale


def f32(*shape):
    return jax.ShapeDtypeStruct(shape, jnp.float32)


VM = pl.BlockSpec(memory_space=pltpu.VMEM)
SM = pl.BlockSpec(memory_space=pltpu.SMEM)
ANY = pl.BlockSpec(memory_space=pl.ANY)
HBM = pl.BlockSpec(memory_space=pltpu.HBM)


def params(mib):
    return pltpu.CompilerParams(vmem_limit_bytes=mib * MIB)


def cost(flops, moved):
    return pl.CostEstimate(flops=flops, bytes_accessed=moved, transcendentals=0)


def body(object_field, probe, amplitudes, corners, counts):
    rows, cols = object_field.shape[1], object_field.shape[2]
    modes, side = probe.shape[1], probe.shape[2]
    pairs, n_col = lax.axis_size("row") // 2, lax.axis_size("col")
    step = SUBLANES * 2 * pairs * n_col
    total_rows = -(-(2 * modes + 1) * side // step) * step
    share = total_rows // (2 * pairs)
    piece = share // n_col
    pair, my_col = lax.axis_index("row") // 2, lax.axis_index("col")
    spots = corners[0, 0]

    right = shifted(object_field[:, :, :side], 0, -1)
    measured = evens_first(amplitudes[0, 0])
    tile, measured = lax.optimization_barrier((object_field, measured))
    below = shifted(tile[:, :side, :], -1, 0)
    from_up = shifted(spots, 1, 0)
    from_left = shifted(spots, 0, 1)
    from_diag = shifted(spots, 1, 1)
    right, measured = lax.optimization_barrier((right, measured))
    corner = shifted(right[:, :side, :], -1, 0)
    corner, from_up, from_left, from_diag = lax.optimization_barrier((corner, from_up, from_left, from_diag))
    g_tile, g_lower, g_right, mine, other = pl.pallas_call(
        main_kernel,
        out_shape=(
            f32(2, rows, cols), f32(2, side, cols + side), f32(2, rows, side),
            f32(pairs, share, side), f32(pairs, share, side),
        ),
        in_specs=[SM] * 2 + [HBM] * 4 + [VM] * 3,
        out_specs=(HBM,) * 5,
        scratch_shapes=[
            pltpu.VMEM((2, rows + side, cols + side), jnp.float32),
            pltpu.VMEM((2, rows + side, cols + side), jnp.float32),
            pltpu.VMEM((2, side, modes * side), jnp.bfloat16),
            pltpu.VMEM((2, modes * side, side), jnp.bfloat16),
            pltpu.VMEM((2, modes * side, side), jnp.float32),
            pltpu.VMEM((2, side, side), jnp.float32),
            pltpu.VMEM((total_rows, side), jnp.float32),
            pltpu.SemaphoreType.DMA((4,)),
            pltpu.SemaphoreType.DMA((2 * pairs + 3,)),
        ],
        compiler_params=params(28),
        cost_estimate=cost(7 * 10**9, 2 * 10**7),
        name="positions",
    )(counts, spots, object_field, below, right, corner, measured, probe, tables(side))

    arrived = swapped(other, 1, 0)
    arrived, from_up, from_left, from_diag = lax.optimization_barrier((arrived, from_up, from_left, from_diag))
    light, top = pl.pallas_call(
        light_kernel,
        out_shape=(f32(rows, cols), f32(SUBLANES, side)),
        in_specs=[SM] * 5 + [VM],
        out_specs=(VM, VM),
        scratch_shapes=[
            pltpu.VMEM((side, side), jnp.float32),
            pltpu.VMEM((1, rows + 2 * side, cols + 2 * side), jnp.float32),
        ],
        compiler_params=params(12),
        cost_estimate=cost(10**8, 10**7),
        name="lighting",
    )(counts, spots, from_up, from_left, from_diag, probe)

    g_left = shifted(g_right, 0, 1)

    def chip_sum(d):
        return mine[pair ^ d] + arrived[pair ^ d]

    plane_sum = sum([swapped(chip_sum(d), 2 * d, 0) for d in range(1, pairs)], chip_sum(0))
    plane_sum, g_lower, g_left, top = lax.optimization_barrier((plane_sum, g_lower, g_left, top))
    g_up = shifted(g_lower, 1, 0)

    plane_sum = plane_sum.reshape(n_col, piece, side)

    def col_part(e):
        return jnp.concatenate([plane_sum[my_col ^ e], top], axis=0)

    received = [swapped(col_part(e), 0, e) for e in range(1, n_col)]
    own = sum([value[:piece] for value in received], plane_sum[my_col])
    top = functools.reduce(jnp.maximum, [value[piece:] for value in received], top)
    own = jnp.concatenate([own] + [swapped(own, 0, e) for e in range(1, n_col)] + [top], axis=0)
    own, g_up, g_corner = lax.optimization_barrier((own, g_up, g_up[:, :, cols:]))
    g_diag = shifted(g_corner, 0, 1)
    blocks = [own] + [swapped(own, 2 * d, 0) for d in range(1, pairs)]
    blocks[-1], g_diag = lax.optimization_barrier((blocks[-1], g_diag))
    blocks = blocks + [swapped(block, 1, 0) for block in blocks]
    top = functools.reduce(jnp.maximum, [block[share:] for block in blocks])
    object_new = pl.pallas_call(
        finish_kernel,
        out_shape=f32(2, rows, cols),
        in_specs=[VM] * 7,
        out_specs=VM,
        compiler_params=params(10),
        cost_estimate=cost(10**6, 6 * 10**6),
        name="object_update",
    )(object_field, light, top, g_tile, g_left, g_up, g_diag)
    probe_new = pl.pallas_call(
        functools.partial(probe_kernel, (pairs, n_col)),
        out_shape=f32(*probe.shape),
        in_specs=[VM] * (1 + len(blocks)),
        out_specs=VM,
        scratch_shapes=[pltpu.VMEM((total_rows, side), jnp.float32)],
        compiler_params=params(14),
        cost_estimate=cost(10**6, 6 * 10**6),
        name="probe_update",
    )(probe, *blocks)
    return object_new, probe_new


def solution(mesh):
    in_specs = (
        P(None, "row", "col"),
        P(),
        P("row", "col", None, None, None),
        P("row", "col", None, None),
        P(),
    )
    out_specs = (P(None, "row", "col"), P())
    return jax.shard_map(body, mesh=mesh, in_specs=in_specs, out_specs=out_specs, check_vma=False)
```

```python
import functools
import math

import jax
import jax.numpy as jnp
import numpy as np
from jax import lax
from jax.experimental import pallas as pl
from jax.experimental.pallas import tpu as pltpu
from jax.sharding import PartitionSpec as P

LANES = 128
SUBLANES = 8
MIB = 1024 * 1024


def shifted(value, d_row, d_col):
    rows, cols = lax.axis_size("row"), lax.axis_size("col")
    pairs = []
    for r in range(rows):
        for c in range(cols):
            if 0 <= r + d_row < rows and 0 <= c + d_col < cols:
                pairs.append((r * cols + c, (r + d_row) * cols + c + d_col))
    return lax.ppermute(value, ("row", "col"), pairs)


def swapped(value, flip_row, flip_col):
    rows, cols = lax.axis_size("row"), lax.axis_size("col")
    pairs = [(r * cols + c, (r ^ flip_row) * cols + (c ^ flip_col)) for r in range(rows) for c in range(cols)]
    return lax.ppermute(value, ("row", "col"), pairs)


def plane_bits():
    return (lax.axis_size("row") // 2).bit_length() - 1


def plane_bit(core, step):
    return step if core == 0 else plane_bits() - 1 - step


def plane_rank(core, pair):
    ranks = []
    for c in range(2):
        rank = 0
        for step in range(plane_bits()):
            rank = rank * 2 + ((pair >> plane_bit(c, step)) & 1)
        ranks.append(rank)
    return jnp.where(core == 0, ranks[0], ranks[1])


def flipped(value, step):
    rows, cols = lax.axis_size("row"), lax.axis_size("col")
    pairs = [
        (r * cols + c, (r ^ (2 << plane_bit(r % 2, step))) * cols + c) for r in range(rows) for c in range(cols)
    ]
    return lax.ppermute(value, ("row", "col"), pairs)


def tables(side):
    index = np.arange(side)
    angle = (index[:, None] * index[None, :] % side) * (2.0 * math.pi / side)
    scale = 1.0 / math.sqrt(side)
    re = (np.cos(angle) * scale).astype(np.float32)
    im = (-np.sin(angle) * scale).astype(np.float32)
    blocks = []
    for first in (0, 1):
        a, b = re[first::2, :side // 2], im[first::2, :side // 2]
        blocks.append(np.block([[a, -b], [b, a]]))
    return jnp.asarray(np.stack(blocks + [block.T for block in blocks]), jnp.bfloat16)


def evens_first(amplitudes):
    side = amplitudes.shape[-1]
    order = np.concatenate([np.arange(0, side, 2), np.arange(1, side, 2)])
    pick = jnp.asarray(np.eye(side)[order], jnp.float32)
    rows = jnp.einsum("ab,sbc->sac", pick, amplitudes, precision=lax.Precision.HIGHEST)
    return jnp.einsum("sac,dc->sad", rows, pick, precision=lax.Precision.HIGHEST)


def corner_of(row, col):
    row_base = pl.multiple_of(row // SUBLANES * SUBLANES, SUBLANES)
    col_base = pl.multiple_of(col // LANES * LANES, LANES)
    return row_base, row - row_base, col_base, col - col_base


def window_at(ref, part, row, col, side):
    row_base, down, col_base, over = corner_of(row, col)
    groups = side // SUBLANES
    lane = lax.broadcasted_iota(jnp.int32, (side, LANES), 1)
    sub = lax.broadcasted_iota(jnp.int32, (groups, SUBLANES, LANES), 1)
    turned = []
    for j in range(side // LANES + 1):
        block = ref[part, pl.ds(row_base, side + SUBLANES), pl.ds(col_base + j * LANES, LANES)]
        block = block.reshape(groups + 1, SUBLANES, LANES)
        block = pltpu.roll(block, lax.rem(SUBLANES - down, SUBLANES), 1)
        block = jnp.where(sub < SUBLANES - down, block[:groups], block[1:]).reshape(side, LANES)
        turned.append(pltpu.roll(block, lax.rem(LANES - over, LANES), 1))
    parts = [jnp.where(lane < LANES - over, turned[j], turned[j + 1]) for j in range(side // LANES)]
    return jnp.concatenate(parts, axis=1)


def add_at(ref, part, row, col, value, side):
    row_base, down, col_base, over = corner_of(row, col)
    groups = side // SUBLANES
    blocks = side // LANES
    lane = lax.broadcasted_iota(jnp.int32, (side, LANES), 1)
    sub = lax.broadcasted_iota(jnp.int32, (groups + 1, SUBLANES, LANES), 1)
    turned = [pltpu.roll(value[:, j * LANES:(j + 1) * LANES], over, 1) for j in range(blocks)]
    none = jnp.zeros((side, LANES), value.dtype)
    gap = jnp.zeros((1, SUBLANES, LANES), value.dtype)
    for j in range(blocks + 1):
        block = jnp.where(lane >= over, turned[j] if j < blocks else none, turned[j - 1] if j else none)
        block = pltpu.roll(block.reshape(groups, SUBLANES, LANES), down, 1)
        block = jnp.where(
            sub >= down, jnp.concatenate([block, gap], axis=0), jnp.concatenate([gap, block], axis=0)
        )
        place = (part, pl.ds(row_base, side + SUBLANES), pl.ds(col_base + j * LANES, LANES))
        ref[place] += block.reshape(side + SUBLANES, LANES)


def main_kernel(
    counts_ref, spots_ref, tile_hbm, below_hbm, right_hbm, corner_hbm, amp_hbm, probe_hbm, table_hbm,
    g_tile, g_lower, g_right, mine_ref, other_ref,
    ext, gacc, stage, turned, wave, wins, sums, amp_ref, probe_ref, table_ref, in_sem, amp_sem, out_sem,
):
    modes, side = probe_ref.shape[1], probe_ref.shape[2]
    rows, cols = tile_hbm.shape[1], tile_hbm.shape[2]
    low = side // 2
    my_row, my_col = lax.axis_index("row"), lax.axis_index("col")
    count = counts_ref[my_row, my_col]
    loads = [(probe_hbm, probe_ref), (table_hbm, table_ref)]
    for ref, r, c in ((tile_hbm, 0, 0), (below_hbm, rows, 0), (right_hbm, 0, cols), (corner_hbm, rows, cols)):
        loads.append((ref, ext.at[:, pl.ds(r, ref.shape[1]), pl.ds(c, ref.shape[2])]))
    loads = [pltpu.make_async_copy(a, b, in_sem.at[i]) for i, (a, b) in enumerate(loads)]

    def amp_load(p, slot):
        return pltpu.make_async_copy(amp_hbm.at[p], amp_ref.at[slot], amp_sem.at[slot])

    for load in loads:
        load.start()
    amp_load(0, 0).start()
    gacc[...] = jnp.zeros_like(gacc)
    sums[...] = jnp.zeros_like(sums)
    for load in loads:
        load.wait()

    def dot(a, b):
        return jnp.dot(a, b, preferred_element_type=jnp.float32)

    def plane(index):
        return slice(index * side, (index + 1) * side)

    def bf16(value):
        return value.astype(jnp.bfloat16)

    def step(p, carry):
        slot = lax.rem(p, 2)

        @pl.when(p + 1 < count)
        def _():
            amp_load(p + 1, 1 - slot).start()

        row, col = spots_ref[p, 0] - my_row * rows, spots_ref[p, 1] - my_col * cols
        win_re = window_at(ext, 0, row, col, side)
        win_im = window_at(ext, 1, row, col, side)
        wins[0], wins[1] = win_re, win_im
        sums[plane(2 * modes)] += win_re * win_re + win_im * win_im
        for k in range(modes):
            pr, pi = probe_ref[0, k], probe_ref[1, k]
            for i, psi in enumerate((pr * win_re - pi * win_im, pr * win_im + pi * win_re)):
                stage[0, i * low:(i + 1) * low, plane(k)] = bf16(psi[:low] + psi[low:])
                stage[1, i * low:(i + 1) * low, plane(k)] = bf16(psi[:low] - psi[low:])
        for k in range(modes):
            for parity in range(2):
                half = dot(table_ref[parity], stage[parity, :, plane(k)])
                at = k * side + parity * low
                for i in range(2):
                    left, right = half[i * low:(i + 1) * low, :low], half[i * low:(i + 1) * low, low:]
                    turned[0, at:at + low, i * low:(i + 1) * low] = bf16(left + right)
                    turned[1, at:at + low, i * low:(i + 1) * low] = bf16(left - right)
        for parity in range(2):
            wave[parity] = dot(turned[parity], table_ref[2 + parity])
        amp_load(p, slot).wait()
        for parity in range(2):
            model = jnp.zeros((side, low), jnp.float32)
            for k in range(modes):
                wr, wi = wave[parity, plane(k), :low], wave[parity, plane(k), low:]
                model += wr * wr + wi * wi
            factor = amp_ref[slot, :, parity * low:(parity + 1) * low] * lax.rsqrt(jnp.maximum(model, 1.0)) - 1.0
            for k in range(modes):
                at = k * side + parity * low
                for i in range(2):
                    target = bf16(wave[parity, plane(k), i * low:(i + 1) * low] * factor)
                    stage[0, i * low:(i + 1) * low, at:at + low] = target[:low]
                    stage[1, i * low:(i + 1) * low, at:at + low] = target[low:]
        for k in range(modes):
            even = dot(table_ref[2], stage[0, :, plane(k)])
            odd = dot(table_ref[3], stage[1, :, plane(k)])
            for lower, back in enumerate((bf16(even + odd), bf16(even - odd))):
                at = k * side + lower * low
                for i in range(2):
                    for parity in range(2):
                        turned[parity, at:at + low, i * low:(i + 1) * low] = (
                            back[i * low:(i + 1) * low, parity * low:(parity + 1) * low]
                        )
        for parity in range(2):
            wave[parity] = dot(turned[parity], table_ref[parity])
        grads = []
        for lower in range(2):
            part = slice(lower * low, (lower + 1) * low)
            grad_re = jnp.zeros((side, low), jnp.float32)
            grad_im = jnp.zeros((side, low), jnp.float32)
            win_re, win_im = wins[0, :, part], wins[1, :, part]
            for k in range(modes):
                even_re, even_im = wave[0, plane(k), :low], wave[0, plane(k), low:]
                odd_re, odd_im = wave[1, plane(k), :low], wave[1, plane(k), low:]
                if lower:
                    cr, ci = even_re - odd_re, even_im - odd_im
                else:
                    cr, ci = even_re + odd_re, even_im + odd_im
                pr, pi = probe_ref[0, k, :, part], probe_ref[1, k, :, part]
                grad_re += pr * cr + pi * ci
                grad_im += pr * ci - pi * cr
                sums[plane(k), part] += win_re * cr + win_im * ci
                sums[plane(modes + k), part] += win_re * ci - win_im * cr
            grads.append((grad_re, grad_im))
        for i in range(2):
            add_at(gacc, i, row, col, jnp.concatenate([grads[0][i], grads[1][i]], axis=1), side)
        return carry

    lax.fori_loop(0, count, step, 0)

    pairs = lax.axis_size("row") // 2
    share = mine_ref.shape[1]
    core = lax.rem(my_row, 2)
    stores = []
    for ref, base in ((other_ref, (1 - core) * (share * pairs)), (mine_ref, core * (share * pairs))):
        base = pl.multiple_of(base, SUBLANES)
        for j in range(pairs):
            stores.append((sums.at[pl.ds(base + j * share, share)], ref.at[j]))
    stores.append((gacc.at[:, pl.ds(0, rows), pl.ds(cols, side)], g_right))
    stores.append((gacc.at[:, pl.ds(0, rows), pl.ds(0, cols)], g_tile))
    stores.append((gacc.at[:, pl.ds(rows, side)], g_lower))
    stores = [pltpu.make_async_copy(a, b, out_sem.at[i]) for i, (a, b) in enumerate(stores)]
    for store in stores:
        store.start()
    for store in stores:
        store.wait()


def light_kernel(counts_ref, spots_ref, left_ref, up_ref, diag_ref, probe_ref, light_ref, top_ref, lit, acc):
    side = probe_ref.shape[2]
    rows, cols = light_ref.shape
    my_row, my_col = lax.axis_index("row"), lax.axis_index("col")
    lit[...] = jnp.sum(probe_ref[0] * probe_ref[0] + probe_ref[1] * probe_ref[1], axis=0)
    acc[...] = jnp.zeros_like(acc)
    for ref, d_row, d_col in ((spots_ref, 0, 0), (left_ref, 0, 1), (up_ref, 1, 0), (diag_ref, 1, 1)):
        inside = (my_row >= d_row) & (my_col >= d_col)
        number = counts_ref[jnp.maximum(my_row - d_row, 0), jnp.maximum(my_col - d_col, 0)]

        def step(p, carry, ref=ref):
            row, col = ref[p, 0] - my_row * rows + side, ref[p, 1] - my_col * cols + side

            @pl.when((row > 0) & (col > 0))
            def _():
                add_at(acc, 0, row, col, lit[...], side)

            return carry

        lax.fori_loop(0, jnp.where(inside, number, 0), step, 0)
    light = acc[0, side:side + rows, side:side + cols]
    light_ref[...] = light
    top = jnp.max(light, axis=0, keepdims=True)
    top = jnp.max(top, axis=1, keepdims=True)
    top_ref[...] = jnp.broadcast_to(top, top_ref.shape)


def finish_kernel(tile_ref, light_ref, top_ref, g_tile, g_left, g_up, g_diag, out_ref):
    side = g_left.shape[2]
    rows, cols = light_ref.shape
    top = top_ref[0:1, 0:1]
    for at in range(0, cols, side):
        part = slice(at, at + side)
        scale = 1.0 / (light_ref[:, part] + 0.1 * top)
        for i in range(2):
            total = g_tile[i, :, part] + g_up[i, :, part]
            if at == 0:
                total += g_left[i] + g_diag[i]
            out_ref[i, :, part] = tile_ref[i, :, part] + total * scale


def probe_kernel(parts, probe_ref, *refs):
    pairs, n_col = parts
    block_refs, out_ref, sums = refs[:-2], refs[-2], refs[-1]
    modes, side = probe_ref.shape[1], probe_ref.shape[2]
    share = block_refs[0].shape[0] - SUBLANES
    piece = share // n_col
    my_row, my_col = lax.axis_index("row"), lax.axis_index("col")
    core, pair = lax.rem(my_row, 2), my_row // 2
    for i, ref in enumerate(block_refs):
        flip, d = i // pairs, i % pairs
        base = ((core ^ flip) * pairs + (plane_rank(core ^ flip, pair) ^ d)) * share
        for e in range(n_col):
            to = pl.multiple_of(base + (my_col ^ e) * piece, SUBLANES)
            sums[pl.ds(to, piece)] = ref[e * piece:(e + 1) * piece]
    den = sums[2 * modes * side:(2 * modes + 1) * side]
    top = jnp.max(jnp.max(den, axis=0, keepdims=True), axis=1, keepdims=True)
    scale = 1.0 / (den + 0.1 * top)
    for k in range(modes):
        out_ref[0, k] = probe_ref[0, k] + sums[k * side:(k + 1) * side] * scale
        out_ref[1, k] = probe_ref[1, k] + sums[(modes + k) * side:(modes + k + 1) * side] * scale


def f32(*shape):
    return jax.ShapeDtypeStruct(shape, jnp.float32)


VM = pl.BlockSpec(memory_space=pltpu.VMEM)
SM = pl.BlockSpec(memory_space=pltpu.SMEM)
ANY = pl.BlockSpec(memory_space=pl.ANY)
HBM = pl.BlockSpec(memory_space=pltpu.HBM)


def params(mib):
    return pltpu.CompilerParams(vmem_limit_bytes=mib * MIB)


def hbm(*shape):
    return pltpu.HBM(shape, jnp.float32)


def in_hbm(value):
    return pltpu.with_memory_space_constraint(value, pltpu.HBM)


def cost(flops, moved):
    return pl.CostEstimate(flops=flops, bytes_accessed=moved, transcendentals=0)


def body(object_field, probe, amplitudes, corners, counts):
    rows, cols = object_field.shape[1], object_field.shape[2]
    modes, side = probe.shape[1], probe.shape[2]
    slots = amplitudes.shape[2]
    pairs, n_col = lax.axis_size("row") // 2, lax.axis_size("col")
    step = SUBLANES * 2 * pairs * n_col
    total_rows = -(-(2 * modes + 1) * side // step) * step
    share = total_rows // (2 * pairs)
    piece = share // n_col
    my_row, my_col = lax.axis_index("row"), lax.axis_index("col")
    core, pair = my_row % 2, my_row // 2
    spots = corners[0, 0]

    right = shifted(object_field[:, :, :side], 0, -1)
    measured = evens_first(amplitudes[0, 0])
    tile, measured = lax.optimization_barrier((object_field, measured))
    below = shifted(tile[:, :side, :], -1, 0)
    from_left = shifted(spots, 0, 1)
    right, measured = lax.optimization_barrier((right, measured))
    corner = shifted(right[:, :side, :], -1, 0)
    corner, from_left = lax.optimization_barrier((corner, from_left))
    g_tile, g_lower, g_right, mine, other = pl.pallas_call(
        main_kernel,
        out_shape=(
            hbm(2, rows, cols), hbm(2, side, cols + side), hbm(2, rows, side),
            hbm(pairs, share, side), hbm(pairs, share, side),
        ),
        in_specs=[SM] * 2 + [HBM] + [ANY] * 3 + [HBM] * 3,
        out_specs=(HBM,) * 5,
        scratch_shapes=[
            pltpu.VMEM((2, rows + side, cols + side), jnp.float32),
            pltpu.VMEM((2, rows + side, cols + side), jnp.float32),
            pltpu.VMEM((2, side, modes * side), jnp.bfloat16),
            pltpu.VMEM((2, modes * side, side), jnp.bfloat16),
            pltpu.VMEM((2, modes * side, side), jnp.float32),
            pltpu.VMEM((2, side, side), jnp.float32),
            pltpu.VMEM((total_rows, side), jnp.float32),
            pltpu.VMEM((2, side, side), jnp.float32),
            pltpu.VMEM(probe.shape, jnp.float32),
            pltpu.VMEM((4, side, side), jnp.bfloat16),
            pltpu.SemaphoreType.DMA((6,)),
            pltpu.SemaphoreType.DMA((2,)),
            pltpu.SemaphoreType.DMA((2 * pairs + 3,)),
        ],
        compiler_params=params(22),
        cost_estimate=cost(7 * 10**9, 2 * 10**7),
        name="positions",
    )(counts, spots, in_hbm(object_field), below, right, corner, *map(in_hbm, (measured, probe, tables(side))))

    arrived = swapped(other, 1, 0)
    arrived, from_left = lax.optimization_barrier((arrived, from_left))
    from_up = shifted(jnp.concatenate([spots, from_left], axis=0), 1, 0)
    light, top = pl.pallas_call(
        light_kernel,
        out_shape=(f32(rows, cols), f32(SUBLANES, side)),
        in_specs=[SM] * 5 + [VM],
        out_specs=(VM, VM),
        scratch_shapes=[
            pltpu.VMEM((side, side), jnp.float32),
            pltpu.VMEM((1, rows + 2 * side, cols + 2 * side), jnp.float32),
        ],
        compiler_params=params(12),
        cost_estimate=cost(10**8, 10**7),
        name="lighting",
    )(counts, spots, from_left, from_up[:slots], from_up[slots:], in_hbm(probe))

    g_left = shifted(g_right, 0, 1)

    held = mine + arrived
    for i in range(plane_bits()):
        keep = (plane_rank(core, pair) >> (plane_bits() - 1 - i)) & 1
        held = held.reshape(2, -1, share, side)
        held = held[keep] + flipped(held[1 - keep], i)
        if i == 0:
            held, top = lax.optimization_barrier((held, top))
    plane_sum = held.reshape(share, side)
    plane_sum, g_lower, g_left = lax.optimization_barrier((plane_sum, g_lower, g_left))
    g_up = shifted(g_lower, 1, 0)

    plane_sum = plane_sum.reshape(n_col, piece, side)

    def col_part(e):
        return jnp.concatenate([plane_sum[my_col ^ e], top], axis=0)

    received = [swapped(col_part(e), 0, e) for e in range(1, n_col)]
    own = sum([value[:piece] for value in received], plane_sum[my_col])
    top = functools.reduce(jnp.maximum, [value[piece:] for value in received], top)
    own = jnp.concatenate([own] + [swapped(own, 0, e) for e in range(1, n_col)] + [top], axis=0)
    own, g_up, g_corner = lax.optimization_barrier((own, g_up, g_up[:, :, cols:]))
    g_diag = shifted(g_corner, 0, 1)
    blocks = [own]
    for i in reversed(range(plane_bits())):
        blocks = blocks + [flipped(block, i) for block in blocks]
    blocks[-1], g_diag = lax.optimization_barrier((blocks[-1], g_diag))
    blocks = blocks + [swapped(block, 1, 0) for block in blocks]
    top = functools.reduce(jnp.maximum, [block[share:] for block in blocks])
    object_new = pl.pallas_call(
        finish_kernel,
        out_shape=f32(2, rows, cols),
        in_specs=[VM] * 7,
        out_specs=VM,
        compiler_params=params(10),
        cost_estimate=cost(10**6, 6 * 10**6),
        name="object_update",
    )(in_hbm(object_field), light, top, in_hbm(g_tile), g_left, g_up, g_diag)
    probe_new = pl.pallas_call(
        functools.partial(probe_kernel, (pairs, n_col)),
        out_shape=f32(*probe.shape),
        in_specs=[VM] * (1 + len(blocks)),
        out_specs=VM,
        scratch_shapes=[pltpu.VMEM((total_rows, side), jnp.float32)],
        compiler_params=params(14),
        cost_estimate=cost(10**6, 6 * 10**6),
        name="probe_update",
    )(in_hbm(probe), *blocks)
    return object_new, probe_new


def solution(mesh):
    in_specs = (
        P(None, "row", "col"),
        P(),
        P("row", "col", None, None, None),
        P("row", "col", None, None),
        P(),
    )
    out_specs = (P(None, "row", "col"), P())
    return jax.shard_map(body, mesh=mesh, in_specs=in_specs, out_specs=out_specs, check_vma=False)
```

```python
import functools
import math

import jax
import jax.numpy as jnp
import numpy as np
from jax import lax
from jax.experimental import pallas as pl
from jax.experimental.pallas import tpu as pltpu
from jax.sharding import PartitionSpec as P

LANES = 128
SUBLANES = 8
MIB = 1024 * 1024


def shifted(value, d_row, d_col):
    rows, cols = lax.axis_size("row"), lax.axis_size("col")
    pairs = []
    for r in range(rows):
        for c in range(cols):
            if 0 <= r + d_row < rows and 0 <= c + d_col < cols:
                pairs.append((r * cols + c, (r + d_row) * cols + c + d_col))
    return lax.ppermute(value, ("row", "col"), pairs)


def swapped(value, flip_row, flip_col):
    rows, cols = lax.axis_size("row"), lax.axis_size("col")
    pairs = [(r * cols + c, (r ^ flip_row) * cols + (c ^ flip_col)) for r in range(rows) for c in range(cols)]
    return lax.ppermute(value, ("row", "col"), pairs)


def plane_bits():
    return (lax.axis_size("row") // 2).bit_length() - 1


def plane_bit(core, step):
    return step if core == 0 else plane_bits() - 1 - step


def plane_rank(core, pair):
    ranks = []
    for c in range(2):
        rank = 0
        for step in range(plane_bits()):
            rank = rank * 2 + ((pair >> plane_bit(c, step)) & 1)
        ranks.append(rank)
    return jnp.where(core == 0, ranks[0], ranks[1])


def flipped(value, step):
    rows, cols = lax.axis_size("row"), lax.axis_size("col")
    pairs = [
        (r * cols + c, (r ^ (2 << plane_bit(r % 2, step))) * cols + c) for r in range(rows) for c in range(cols)
    ]
    return lax.ppermute(value, ("row", "col"), pairs)


def tables(side):
    index = np.arange(side)
    angle = (index[:, None] * index[None, :] % side) * (2.0 * math.pi / side)
    scale = 1.0 / math.sqrt(side)
    re = (np.cos(angle) * scale).astype(np.float32)
    im = (-np.sin(angle) * scale).astype(np.float32)
    blocks = []
    for first in (0, 1):
        a, b = re[first::2, :side // 2], im[first::2, :side // 2]
        blocks.append(np.block([[a, -b], [b, a]]))
    return jnp.asarray(np.stack(blocks + [block.T for block in blocks]), jnp.bfloat16)


def evens_first(amplitudes):
    side = amplitudes.shape[-1]
    order = np.concatenate([np.arange(0, side, 2), np.arange(1, side, 2)])
    pick = jnp.asarray(np.eye(side)[order], jnp.float32)
    rows = jnp.einsum("ab,sbc->sac", pick, amplitudes, precision=lax.Precision.HIGHEST)
    return jnp.einsum("sac,dc->sad", rows, pick, precision=lax.Precision.HIGHEST)


def corner_of(row, col):
    row_base = pl.multiple_of(row // SUBLANES * SUBLANES, SUBLANES)
    col_base = pl.multiple_of(col // LANES * LANES, LANES)
    return row_base, row - row_base, col_base, col - col_base


def window_at(ref, part, row, col, side):
    row_base, down, col_base, over = corner_of(row, col)
    groups = side // SUBLANES
    lane = lax.broadcasted_iota(jnp.int32, (side, LANES), 1)
    sub = lax.broadcasted_iota(jnp.int32, (groups, SUBLANES, LANES), 1)
    turned = []
    for j in range(side // LANES + 1):
        block = ref[part, pl.ds(row_base, side + SUBLANES), pl.ds(col_base + j * LANES, LANES)]
        block = block.reshape(groups + 1, SUBLANES, LANES)
        block = pltpu.roll(block, lax.rem(SUBLANES - down, SUBLANES), 1)
        block = jnp.where(sub < SUBLANES - down, block[:groups], block[1:]).reshape(side, LANES)
        turned.append(pltpu.roll(block, lax.rem(LANES - over, LANES), 1))
    parts = [jnp.where(lane < LANES - over, turned[j], turned[j + 1]) for j in range(side // LANES)]
    return jnp.concatenate(parts, axis=1)


def add_at(ref, part, row, col, value, side):
    row_base, down, col_base, over = corner_of(row, col)
    groups = side // SUBLANES
    blocks = side // LANES
    lane = lax.broadcasted_iota(jnp.int32, (side, LANES), 1)
    sub = lax.broadcasted_iota(jnp.int32, (groups + 1, SUBLANES, LANES), 1)
    turned = [pltpu.roll(value[:, j * LANES:(j + 1) * LANES], over, 1) for j in range(blocks)]
    none = jnp.zeros((side, LANES), value.dtype)
    gap = jnp.zeros((1, SUBLANES, LANES), value.dtype)
    for j in range(blocks + 1):
        block = jnp.where(lane >= over, turned[j] if j < blocks else none, turned[j - 1] if j else none)
        block = pltpu.roll(block.reshape(groups, SUBLANES, LANES), down, 1)
        block = jnp.where(
            sub >= down, jnp.concatenate([block, gap], axis=0), jnp.concatenate([gap, block], axis=0)
        )
        place = (part, pl.ds(row_base, side + SUBLANES), pl.ds(col_base + j * LANES, LANES))
        ref[place] += block.reshape(side + SUBLANES, LANES)


def main_kernel(
    counts_ref, spots_ref, tile_hbm, below_hbm, right_hbm, corner_hbm, amp_hbm, probe_hbm, table_hbm,
    g_tile, g_lower, g_right, mine_ref, other_ref,
    ext, gacc, stage, turned, wave, wins, sums, amp_ref, probe_ref, table_ref, in_sem, amp_sem, out_sem,
):
    modes, side = probe_ref.shape[1], probe_ref.shape[2]
    rows, cols = tile_hbm.shape[1], tile_hbm.shape[2]
    low = side // 2
    my_row, my_col = lax.axis_index("row"), lax.axis_index("col")
    count = counts_ref[my_row, my_col]
    loads = [(probe_hbm, probe_ref), (table_hbm, table_ref)]
    for ref, r, c in ((tile_hbm, 0, 0), (below_hbm, rows, 0), (right_hbm, 0, cols), (corner_hbm, rows, cols)):
        loads.append((ref, ext.at[:, pl.ds(r, ref.shape[1]), pl.ds(c, ref.shape[2])]))
    loads = [pltpu.make_async_copy(a, b, in_sem.at[i]) for i, (a, b) in enumerate(loads)]

    def amp_load(p, slot):
        return pltpu.make_async_copy(amp_hbm.at[p], amp_ref.at[slot], amp_sem.at[slot])

    for load in loads:
        load.start()
    amp_load(0, 0).start()
    gacc[...] = jnp.zeros_like(gacc)
    sums[...] = jnp.zeros_like(sums)
    for load in loads:
        load.wait()

    def dot(a, b):
        return jnp.dot(a, b, preferred_element_type=jnp.float32)

    def plane(index):
        return slice(index * side, (index + 1) * side)

    def bf16(value):
        return value.astype(jnp.bfloat16)

    def step(p, carry):
        slot = lax.rem(p, 2)

        @pl.when(p + 1 < count)
        def _():
            amp_load(p + 1, 1 - slot).start()

        row, col = spots_ref[p, 0] - my_row * rows, spots_ref[p, 1] - my_col * cols
        win_re = window_at(ext, 0, row, col, side)
        win_im = window_at(ext, 1, row, col, side)
        wins[0], wins[1] = win_re, win_im
        sums[plane(2 * modes)] += win_re * win_re + win_im * win_im
        for k in range(modes):
            pr, pi = probe_ref[0, k], probe_ref[1, k]
            for i, psi in enumerate((pr * win_re - pi * win_im, pr * win_im + pi * win_re)):
                stage[0, i * low:(i + 1) * low, plane(k)] = bf16(psi[:low] + psi[low:])
                stage[1, i * low:(i + 1) * low, plane(k)] = bf16(psi[:low] - psi[low:])
        for k in range(modes):
            for parity in range(2):
                half = dot(table_ref[parity], stage[parity, :, plane(k)])
                at = k * side + parity * low
                for i in range(2):
                    left, right = half[i * low:(i + 1) * low, :low], half[i * low:(i + 1) * low, low:]
                    turned[0, at:at + low, i * low:(i + 1) * low] = bf16(left + right)
                    turned[1, at:at + low, i * low:(i + 1) * low] = bf16(left - right)
        for parity in range(2):
            wave[parity] = dot(turned[parity], table_ref[2 + parity])
        amp_load(p, slot).wait()
        for parity in range(2):
            model = jnp.zeros((side, low), jnp.float32)
            for k in range(modes):
                wr, wi = wave[parity, plane(k), :low], wave[parity, plane(k), low:]
                model += wr * wr + wi * wi
            factor = amp_ref[slot, :, parity * low:(parity + 1) * low] * lax.rsqrt(jnp.maximum(model, 1.0)) - 1.0
            for k in range(modes):
                at = k * side + parity * low
                for i in range(2):
                    target = bf16(wave[parity, plane(k), i * low:(i + 1) * low] * factor)
                    stage[0, i * low:(i + 1) * low, at:at + low] = target[:low]
                    stage[1, i * low:(i + 1) * low, at:at + low] = target[low:]
        for k in range(modes):
            even = dot(table_ref[2], stage[0, :, plane(k)])
            odd = dot(table_ref[3], stage[1, :, plane(k)])
            for lower, back in enumerate((bf16(even + odd), bf16(even - odd))):
                at = k * side + lower * low
                for i in range(2):
                    for parity in range(2):
                        turned[parity, at:at + low, i * low:(i + 1) * low] = (
                            back[i * low:(i + 1) * low, parity * low:(parity + 1) * low]
                        )
        for parity in range(2):
            wave[parity] = dot(turned[parity], table_ref[parity])
        grads = []
        for lower in range(2):
            part = slice(lower * low, (lower + 1) * low)
            grad_re = jnp.zeros((side, low), jnp.float32)
            grad_im = jnp.zeros((side, low), jnp.float32)
            win_re, win_im = wins[0, :, part], wins[1, :, part]
            for k in range(modes):
                even_re, even_im = wave[0, plane(k), :low], wave[0, plane(k), low:]
                odd_re, odd_im = wave[1, plane(k), :low], wave[1, plane(k), low:]
                if lower:
                    cr, ci = even_re - odd_re, even_im - odd_im
                else:
                    cr, ci = even_re + odd_re, even_im + odd_im
                pr, pi = probe_ref[0, k, :, part], probe_ref[1, k, :, part]
                grad_re += pr * cr + pi * ci
                grad_im += pr * ci - pi * cr
                sums[plane(k), part] += win_re * cr + win_im * ci
                sums[plane(modes + k), part] += win_re * ci - win_im * cr
            grads.append((grad_re, grad_im))
        for i in range(2):
            add_at(gacc, i, row, col, jnp.concatenate([grads[0][i], grads[1][i]], axis=1), side)
        return carry

    lax.fori_loop(0, count, step, 0)

    pairs = lax.axis_size("row") // 2
    share = mine_ref.shape[1]
    core = lax.rem(my_row, 2)
    stores = []
    for ref, base in ((other_ref, (1 - core) * (share * pairs)), (mine_ref, core * (share * pairs))):
        base = pl.multiple_of(base, SUBLANES)
        for j in range(pairs):
            stores.append((sums.at[pl.ds(base + j * share, share)], ref.at[j]))
    stores.append((gacc.at[:, pl.ds(0, rows), pl.ds(cols, side)], g_right))
    stores.append((gacc.at[:, pl.ds(0, rows), pl.ds(0, cols)], g_tile))
    stores.append((gacc.at[:, pl.ds(rows, side)], g_lower))
    stores = [pltpu.make_async_copy(a, b, out_sem.at[i]) for i, (a, b) in enumerate(stores)]
    for store in stores:
        store.start()
    for store in stores:
        store.wait()


def light_kernel(counts_ref, spots_ref, left_ref, up_ref, diag_ref, probe_ref, light_ref, top_ref, lit, acc):
    side = probe_ref.shape[2]
    rows, cols = light_ref.shape
    my_row, my_col = lax.axis_index("row"), lax.axis_index("col")
    lit[...] = jnp.sum(probe_ref[0] * probe_ref[0] + probe_ref[1] * probe_ref[1], axis=0)
    acc[...] = jnp.zeros_like(acc)
    for ref, d_row, d_col in ((spots_ref, 0, 0), (left_ref, 0, 1), (up_ref, 1, 0), (diag_ref, 1, 1)):
        inside = (my_row >= d_row) & (my_col >= d_col)
        number = counts_ref[jnp.maximum(my_row - d_row, 0), jnp.maximum(my_col - d_col, 0)]

        def step(p, carry, ref=ref):
            row, col = ref[p, 0] - my_row * rows + side, ref[p, 1] - my_col * cols + side

            @pl.when((row > 0) & (col > 0))
            def _():
                add_at(acc, 0, row, col, lit[...], side)

            return carry

        lax.fori_loop(0, jnp.where(inside, number, 0), step, 0)
    light = acc[0, side:side + rows, side:side + cols]
    light_ref[...] = light
    top = jnp.max(light, axis=0, keepdims=True)
    top = jnp.max(top, axis=1, keepdims=True)
    top_ref[...] = jnp.broadcast_to(top, top_ref.shape)


def fold_kernel(step, held_ref, got_ref, send_ref, keep_ref):
    half = keep_ref.shape[0]
    my_row = lax.axis_index("row")
    keep = (plane_rank(lax.rem(my_row, 2), my_row // 2) >> (plane_bits() - 1 - step)) & 1
    for ref, at in ((send_ref, (1 - keep) * half), (keep_ref, keep * half)):
        ref[...] = held_ref[pl.ds(at, half)] + got_ref[pl.ds(at, half)]


def fold(step, held, got):
    count, share, side = held.shape
    return pl.pallas_call(
        functools.partial(fold_kernel, step),
        out_shape=(f32(count // 2, share, side),) * 2,
        in_specs=[VM] * 2,
        out_specs=(VM,) * 2,
        compiler_params=params(8),
        cost_estimate=cost(10**6, 12 * count * share * side),
        name="fold_plane",
    )(held, got)


def cut_kernel(held_ref, got_ref, top_ref, own_ref, *send_refs):
    piece = own_ref.shape[0]
    my_col = lax.axis_index("col")
    for e, ref in enumerate((own_ref,) + send_refs):
        at = pl.ds(pl.multiple_of((my_col ^ e) * piece, SUBLANES), piece)
        ref[:piece] = held_ref[0, at] + got_ref[0, at]
        if e:
            ref[piece:] = top_ref[...]


def cut(held, got, top, parts):
    _, share, side = held.shape
    piece = share // parts
    return pl.pallas_call(
        cut_kernel,
        out_shape=(f32(piece, side),) + (f32(piece + SUBLANES, side),) * (parts - 1),
        in_specs=[VM] * 3,
        out_specs=(VM,) * parts,
        compiler_params=params(4),
        cost_estimate=cost(10**6, 12 * share * side),
        name="cut_columns",
    )(held, got, top)


def finish_kernel(tile_ref, light_ref, top_ref, g_tile, g_left, g_up, out_ref):
    side = g_left.shape[2]
    rows, cols = light_ref.shape
    top = top_ref[0:1, 0:1]
    for at in range(0, cols, side):
        part = slice(at, at + side)
        scale = 1.0 / (light_ref[:, part] + 0.1 * top)
        for i in range(2):
            total = g_tile[i, :, part] + g_up[i, :, part]
            if at == 0:
                total += g_left[i]
            out_ref[i, :, part] = tile_ref[i, :, part] + total * scale


def probe_kernel(parts, probe_ref, *refs):
    pairs, n_col = parts
    block_refs, out_ref, sums = refs[:-2], refs[-2], refs[-1]
    modes, side = probe_ref.shape[1], probe_ref.shape[2]
    share = block_refs[0].shape[0] - SUBLANES
    piece = share // n_col
    my_row, my_col = lax.axis_index("row"), lax.axis_index("col")
    core, pair = lax.rem(my_row, 2), my_row // 2
    for i, ref in enumerate(block_refs):
        flip, d = i // pairs, i % pairs
        base = ((core ^ flip) * pairs + (plane_rank(core ^ flip, pair) ^ d)) * share
        for e in range(n_col):
            to = pl.multiple_of(base + (my_col ^ e) * piece, SUBLANES)
            sums[pl.ds(to, piece)] = ref[e * piece:(e + 1) * piece]
    den = sums[2 * modes * side:(2 * modes + 1) * side]
    top = jnp.max(jnp.max(den, axis=0, keepdims=True), axis=1, keepdims=True)
    scale = 1.0 / (den + 0.1 * top)
    for k in range(modes):
        out_ref[0, k] = probe_ref[0, k] + sums[k * side:(k + 1) * side] * scale
        out_ref[1, k] = probe_ref[1, k] + sums[(modes + k) * side:(modes + k + 1) * side] * scale


def f32(*shape):
    return jax.ShapeDtypeStruct(shape, jnp.float32)


VM = pl.BlockSpec(memory_space=pltpu.VMEM)
SM = pl.BlockSpec(memory_space=pltpu.SMEM)
ANY = pl.BlockSpec(memory_space=pl.ANY)
HBM = pl.BlockSpec(memory_space=pltpu.HBM)


def params(mib):
    return pltpu.CompilerParams(vmem_limit_bytes=mib * MIB)


def hbm(*shape):
    return pltpu.HBM(shape, jnp.float32)


def in_hbm(value):
    return pltpu.with_memory_space_constraint(value, pltpu.HBM)


def cost(flops, moved):
    return pl.CostEstimate(flops=flops, bytes_accessed=moved, transcendentals=0)


def body(object_field, probe, amplitudes, corners, counts):
    rows, cols = object_field.shape[1], object_field.shape[2]
    modes, side = probe.shape[1], probe.shape[2]
    slots = amplitudes.shape[2]
    pairs, n_col = lax.axis_size("row") // 2, lax.axis_size("col")
    step = SUBLANES * 2 * pairs * n_col
    total_rows = -(-(2 * modes + 1) * side // step) * step
    share = total_rows // (2 * pairs)
    piece = share // n_col
    my_row, my_col = lax.axis_index("row"), lax.axis_index("col")
    core, pair = my_row % 2, my_row // 2
    spots = corners[0, 0]

    right = shifted(object_field[:, :, :side], 0, -1)
    measured = evens_first(amplitudes[0, 0])
    tile, measured = lax.optimization_barrier((object_field, measured))
    below = shifted(tile[:, :side, :], -1, 0)
    from_left = shifted(spots, 0, 1)
    right, measured, from_left = lax.optimization_barrier((right, measured, from_left))
    corner = shifted(right[:, :side, :], -1, 0)
    from_up = shifted(jnp.concatenate([spots, from_left], axis=0), 1, 0)
    light, top = pl.pallas_call(
        light_kernel,
        out_shape=(f32(rows, cols), f32(SUBLANES, side)),
        in_specs=[SM] * 5 + [VM],
        out_specs=(VM, VM),
        scratch_shapes=[
            pltpu.VMEM((side, side), jnp.float32),
            pltpu.VMEM((1, rows + 2 * side, cols + 2 * side), jnp.float32),
        ],
        compiler_params=params(12),
        cost_estimate=cost(10**8, 10**7),
        name="lighting",
    )(counts, spots, from_left, from_up[:slots], from_up[slots:], probe)
    corner, top = lax.optimization_barrier((corner, top))
    g_tile, g_lower, g_right, mine, other = pl.pallas_call(
        main_kernel,
        out_shape=(
            hbm(2, rows, cols), hbm(2, side, cols + side), hbm(2, rows, side),
            pltpu.VMEM((pairs, share, side), jnp.float32), hbm(pairs, share, side),
        ),
        in_specs=[SM] * 2 + [HBM] + [ANY] * 3 + [HBM] * 3,
        out_specs=(HBM,) * 3 + (VM, HBM),
        scratch_shapes=[
            pltpu.VMEM((2, rows + side, cols + side), jnp.float32),
            pltpu.VMEM((2, rows + side, cols + side), jnp.float32),
            pltpu.VMEM((2, side, modes * side), jnp.bfloat16),
            pltpu.VMEM((2, modes * side, side), jnp.bfloat16),
            pltpu.VMEM((2, modes * side, side), jnp.float32),
            pltpu.VMEM((2, side, side), jnp.float32),
            pltpu.VMEM((total_rows, side), jnp.float32),
            pltpu.VMEM((2, side, side), jnp.float32),
            pltpu.VMEM(probe.shape, jnp.float32),
            pltpu.VMEM((4, side, side), jnp.bfloat16),
            pltpu.SemaphoreType.DMA((6,)),
            pltpu.SemaphoreType.DMA((2,)),
            pltpu.SemaphoreType.DMA((2 * pairs + 3,)),
        ],
        compiler_params=params(22),
        cost_estimate=cost(7 * 10**9, 2 * 10**7),
        name="positions",
    )(counts, spots, in_hbm(object_field), below, right, corner, *map(in_hbm, (measured, probe, tables(side))))

    arrived = swapped(other, 1, 0)
    held, got = mine, arrived
    for i in range(plane_bits()):
        send, held = fold(i, held, got)
        got = flipped(send, i)
    own, *sends = cut(held, got, top, n_col)
    own, g_lower = lax.optimization_barrier((own, g_lower))
    g_up = shifted(g_lower, 1, 0)
    received = [swapped(send, 0, e) for e, send in enumerate(sends, 1)]
    own = sum([value[:piece] for value in received], own)
    top = functools.reduce(jnp.maximum, [value[piece:] for value in received], top)
    own = jnp.concatenate([own] + [swapped(own, 0, e) for e in range(1, n_col)] + [top], axis=0)
    own, g_up, g_right = lax.optimization_barrier((own, g_up, g_right + g_up[:, :, cols:]))
    g_left = shifted(g_right, 0, 1)
    blocks = [own]
    for i in reversed(range(plane_bits())):
        blocks = blocks + [flipped(block, i) for block in blocks]
    blocks[-1], g_left = lax.optimization_barrier((blocks[-1], g_left))
    blocks = blocks + [swapped(block, 1, 0) for block in blocks]
    top = functools.reduce(jnp.maximum, [block[share:] for block in blocks])
    object_new = pl.pallas_call(
        finish_kernel,
        out_shape=f32(2, rows, cols),
        in_specs=[VM] * 6,
        out_specs=VM,
        compiler_params=params(10),
        cost_estimate=cost(10**6, 6 * 10**6),
        name="object_update",
    )(object_field, light, top, g_tile, g_left, g_up)
    probe_new = pl.pallas_call(
        functools.partial(probe_kernel, (pairs, n_col)),
        out_shape=f32(*probe.shape),
        in_specs=[VM] * (1 + len(blocks)),
        out_specs=VM,
        scratch_shapes=[pltpu.VMEM((total_rows, side), jnp.float32)],
        compiler_params=params(14),
        cost_estimate=cost(10**6, 6 * 10**6),
        name="probe_update",
    )(probe, *blocks)
    return object_new, probe_new


def solution(mesh):
    in_specs = (
        P(None, "row", "col"),
        P(),
        P("row", "col", None, None, None),
        P("row", "col", None, None),
        P(),
    )
    out_specs = (P(None, "row", "col"), P())
    return jax.shard_map(body, mesh=mesh, in_specs=in_specs, out_specs=out_specs, check_vma=False)
```

```python
import functools
import math

import jax
import jax.numpy as jnp
import numpy as np
from jax import lax
from jax.experimental import pallas as pl
from jax.experimental.pallas import tpu as pltpu
from jax.sharding import PartitionSpec as P

LANES = 128
SUBLANES = 8
MIB = 1024 * 1024


def shifted(value, d_row, d_col):
    rows, cols = lax.axis_size("row"), lax.axis_size("col")
    pairs = []
    for r in range(rows):
        for c in range(cols):
            if 0 <= r + d_row < rows and 0 <= c + d_col < cols:
                pairs.append((r * cols + c, (r + d_row) * cols + c + d_col))
    return lax.ppermute(value, ("row", "col"), pairs)


def swapped(value, flip_row, flip_col):
    rows, cols = lax.axis_size("row"), lax.axis_size("col")
    pairs = [(r * cols + c, (r ^ flip_row) * cols + (c ^ flip_col)) for r in range(rows) for c in range(cols)]
    return lax.ppermute(value, ("row", "col"), pairs)


def plane_bits():
    return (lax.axis_size("row") // 2).bit_length() - 1


def col_bits():
    return lax.axis_size("col").bit_length() - 1


def plane_bit(core, step):
    return step if core == 0 else plane_bits() - 1 - step


def rank_by(index, bits):
    rank = 0
    for bit in bits:
        rank = rank * 2 + ((index >> bit) & 1)
    return rank


def plane_rank(core, pair):
    ranks = [rank_by(pair, [plane_bit(c, step) for step in range(plane_bits())]) for c in range(2)]
    return jnp.where(core == 0, ranks[0], ranks[1])


def my_plane_rank():
    my_row = lax.axis_index("row")
    return plane_rank(lax.rem(my_row, 2), my_row // 2)


def my_col_rank():
    return rank_by(lax.axis_index("col"), range(col_bits()))


def flipped(value, step):
    rows, cols = lax.axis_size("row"), lax.axis_size("col")
    pairs = [
        (r * cols + c, (r ^ (2 << plane_bit(r % 2, step))) * cols + c) for r in range(rows) for c in range(cols)
    ]
    return lax.ppermute(value, ("row", "col"), pairs)


def tables(side):
    index = np.arange(side)
    angle = (index[:, None] * index[None, :] % side) * (2.0 * math.pi / side)
    scale = 1.0 / math.sqrt(side)
    re = (np.cos(angle) * scale).astype(np.float32)
    im = (-np.sin(angle) * scale).astype(np.float32)
    blocks = []
    for first in (0, 1):
        a, b = re[first::2, :side // 2], im[first::2, :side // 2]
        blocks.append(np.block([[a, -b], [b, a]]))
    return jnp.asarray(np.stack(blocks + [block.T for block in blocks]), jnp.bfloat16)


def evens_first(amplitudes):
    side = amplitudes.shape[-1]
    order = np.concatenate([np.arange(0, side, 2), np.arange(1, side, 2)])
    pick = jnp.asarray(np.eye(side)[order], jnp.float32)
    rows = jnp.einsum("ab,sbc->sac", pick, amplitudes, precision=lax.Precision.HIGH)
    return jnp.einsum("sac,dc->sad", rows, pick, precision=lax.Precision.HIGH)


def corner_of(row, col):
    row_base = pl.multiple_of(row // SUBLANES * SUBLANES, SUBLANES)
    col_base = pl.multiple_of(col // LANES * LANES, LANES)
    return row_base, row - row_base, col_base, col - col_base


def window_at(ref, part, row, col, side):
    row_base, down, col_base, over = corner_of(row, col)
    groups = side // SUBLANES
    lane = lax.broadcasted_iota(jnp.int32, (side, LANES), 1)
    sub = lax.broadcasted_iota(jnp.int32, (groups, SUBLANES, LANES), 1)
    turned = []
    for j in range(side // LANES + 1):
        block = ref[part, pl.ds(row_base, side + SUBLANES), pl.ds(col_base + j * LANES, LANES)]
        block = block.reshape(groups + 1, SUBLANES, LANES)
        block = pltpu.roll(block, lax.rem(SUBLANES - down, SUBLANES), 1)
        block = jnp.where(sub < SUBLANES - down, block[:groups], block[1:]).reshape(side, LANES)
        turned.append(pltpu.roll(block, lax.rem(LANES - over, LANES), 1))
    parts = [jnp.where(lane < LANES - over, turned[j], turned[j + 1]) for j in range(side // LANES)]
    return jnp.concatenate(parts, axis=1)


def add_at(ref, part, row, col, value, side):
    row_base, down, col_base, over = corner_of(row, col)
    groups = side // SUBLANES
    blocks = side // LANES
    lane = lax.broadcasted_iota(jnp.int32, (side, LANES), 1)
    sub = lax.broadcasted_iota(jnp.int32, (groups + 1, SUBLANES, LANES), 1)
    turned = [pltpu.roll(value[:, j * LANES:(j + 1) * LANES], over, 1) for j in range(blocks)]
    none = jnp.zeros((side, LANES), value.dtype)
    gap = jnp.zeros((1, SUBLANES, LANES), value.dtype)
    for j in range(blocks + 1):
        block = jnp.where(lane >= over, turned[j] if j < blocks else none, turned[j - 1] if j else none)
        block = pltpu.roll(block.reshape(groups, SUBLANES, LANES), down, 1)
        block = jnp.where(
            sub >= down, jnp.concatenate([block, gap], axis=0), jnp.concatenate([gap, block], axis=0)
        )
        place = (part, pl.ds(row_base, side + SUBLANES), pl.ds(col_base + j * LANES, LANES))
        ref[place] += block.reshape(side + SUBLANES, LANES)


def main_kernel(
    counts_ref, spots_ref, tile_hbm, below_any, right_any, corner_any, amp_hbm, probe_hbm, table_hbm,
    g_tile, g_lower, g_right, mine_ref, other_ref,
    ext, gacc, stage, turned, wave, wins, sums, amp_ref, probe_ref, table_ref, in_sem, amp_sem, out_sem,
):
    modes, side = probe_ref.shape[1], probe_ref.shape[2]
    rows, cols = tile_hbm.shape[1], tile_hbm.shape[2]
    low = side // 2
    my_row, my_col = lax.axis_index("row"), lax.axis_index("col")
    count = counts_ref[my_row, my_col]
    loads = [(probe_hbm, probe_ref), (table_hbm, table_ref)]
    for ref, r, c in ((tile_hbm, 0, 0), (below_any, rows, 0), (right_any, 0, cols), (corner_any, rows, cols)):
        loads.append((ref, ext.at[:, pl.ds(r, ref.shape[1]), pl.ds(c, ref.shape[2])]))
    loads = [pltpu.make_async_copy(a, b, in_sem.at[i]) for i, (a, b) in enumerate(loads)]

    def amp_load(p, slot):
        return pltpu.make_async_copy(amp_hbm.at[p], amp_ref.at[slot], amp_sem.at[slot])

    for load in loads:
        load.start()
    amp_load(0, 0).start()
    gacc[...] = jnp.zeros_like(gacc)
    sums[...] = jnp.zeros_like(sums)
    for load in loads:
        load.wait()

    def dot(a, b):
        return jnp.dot(a, b, preferred_element_type=jnp.float32)

    def plane(index):
        return slice(index * side, (index + 1) * side)

    def bf16(value):
        return value.astype(jnp.bfloat16)

    def step(p, carry):
        slot = lax.rem(p, 2)

        @pl.when(p + 1 < count)
        def _():
            amp_load(p + 1, 1 - slot).start()

        row, col = spots_ref[p, 0] - my_row * rows, spots_ref[p, 1] - my_col * cols
        win_re = window_at(ext, 0, row, col, side)
        win_im = window_at(ext, 1, row, col, side)
        wins[0], wins[1] = win_re, win_im
        sums[plane(2 * modes)] += win_re * win_re + win_im * win_im
        for k in range(modes):
            pr, pi = probe_ref[0, k], probe_ref[1, k]
            for i, psi in enumerate((pr * win_re - pi * win_im, pr * win_im + pi * win_re)):
                stage[0, i * low:(i + 1) * low, plane(k)] = bf16(psi[:low] + psi[low:])
                stage[1, i * low:(i + 1) * low, plane(k)] = bf16(psi[:low] - psi[low:])
        for k in range(modes):
            for parity in range(2):
                half = dot(table_ref[parity], stage[parity, :, plane(k)])
                at = k * side + parity * low
                for i in range(2):
                    left, right = half[i * low:(i + 1) * low, :low], half[i * low:(i + 1) * low, low:]
                    turned[0, at:at + low, i * low:(i + 1) * low] = bf16(left + right)
                    turned[1, at:at + low, i * low:(i + 1) * low] = bf16(left - right)
        for parity in range(2):
            wave[parity] = dot(turned[parity], table_ref[2 + parity])
        amp_load(p, slot).wait()
        for parity in range(2):
            model = jnp.zeros((side, low), jnp.float32)
            for k in range(modes):
                wr, wi = wave[parity, plane(k), :low], wave[parity, plane(k), low:]
                model += wr * wr + wi * wi
            factor = amp_ref[slot, :, parity * low:(parity + 1) * low] * lax.rsqrt(jnp.maximum(model, 1.0)) - 1.0
            for k in range(modes):
                at = k * side + parity * low
                for i in range(2):
                    target = bf16(wave[parity, plane(k), i * low:(i + 1) * low] * factor)
                    stage[0, i * low:(i + 1) * low, at:at + low] = target[:low]
                    stage[1, i * low:(i + 1) * low, at:at + low] = target[low:]
        for k in range(modes):
            even = dot(table_ref[2], stage[0, :, plane(k)])
            odd = dot(table_ref[3], stage[1, :, plane(k)])
            for lower, back in enumerate((bf16(even + odd), bf16(even - odd))):
                at = k * side + lower * low
                for i in range(2):
                    for parity in range(2):
                        turned[parity, at:at + low, i * low:(i + 1) * low] = (
                            back[i * low:(i + 1) * low, parity * low:(parity + 1) * low]
                        )
        for parity in range(2):
            wave[parity] = dot(turned[parity], table_ref[parity])
        grads = []
        for lower in range(2):
            part = slice(lower * low, (lower + 1) * low)
            grad_re = jnp.zeros((side, low), jnp.float32)
            grad_im = jnp.zeros((side, low), jnp.float32)
            win_re, win_im = wins[0, :, part], wins[1, :, part]
            for k in range(modes):
                even_re, even_im = wave[0, plane(k), :low], wave[0, plane(k), low:]
                odd_re, odd_im = wave[1, plane(k), :low], wave[1, plane(k), low:]
                if lower:
                    cr, ci = even_re - odd_re, even_im - odd_im
                else:
                    cr, ci = even_re + odd_re, even_im + odd_im
                pr, pi = probe_ref[0, k, :, part], probe_ref[1, k, :, part]
                grad_re += pr * cr + pi * ci
                grad_im += pr * ci - pi * cr
                sums[plane(k), part] += win_re * cr + win_im * ci
                sums[plane(modes + k), part] += win_re * ci - win_im * cr
            grads.append((grad_re, grad_im))
        for i in range(2):
            add_at(gacc, i, row, col, jnp.concatenate([grads[0][i], grads[1][i]], axis=1), side)
        return carry

    lax.fori_loop(0, count, step, 0)

    store = pltpu.make_async_copy(gacc.at[:, pl.ds(0, rows), pl.ds(0, cols)], g_tile, out_sem.at[0])
    store.start()
    core = lax.rem(my_row, 2)
    for ref, at in ((other_ref, 1 - core), (mine_ref, core)):
        ref[...] = sums[pl.ds(pl.multiple_of(at * ref.shape[0], SUBLANES), ref.shape[0])]
    g_lower[...] = gacc[:, rows:]
    g_right[...] = gacc[:, :rows, cols:]
    store.wait()


def light_kernel(counts_ref, spots_ref, left_ref, up_ref, diag_ref, lit_ref, light_ref, top_ref, acc):
    side = lit_ref.shape[0]
    rows, cols = light_ref.shape
    my_row, my_col = lax.axis_index("row"), lax.axis_index("col")
    acc[...] = jnp.zeros_like(acc)
    for ref, d_row, d_col in ((spots_ref, 0, 0), (left_ref, 0, 1), (up_ref, 1, 0), (diag_ref, 1, 1)):
        inside = (my_row >= d_row) & (my_col >= d_col)
        number = counts_ref[jnp.maximum(my_row - d_row, 0), jnp.maximum(my_col - d_col, 0)]

        def step(p, carry, ref=ref):
            row, col = ref[p, 0] - my_row * rows + side, ref[p, 1] - my_col * cols + side

            @pl.when((row > 0) & (col > 0))
            def _():
                add_at(acc, 0, row, col, lit_ref[...], side)

            return carry

        lax.fori_loop(0, jnp.where(inside, number, 0), step, 0)
    light = acc[0, side:side + rows, side:side + cols]
    light_ref[...] = light
    top = jnp.max(light, axis=0, keepdims=True)
    top = jnp.max(top, axis=1, keepdims=True)
    top_ref[...] = jnp.broadcast_to(top, top_ref.shape)


def fold_kernel(rank_of, below, with_top, *refs):
    held_ref, got_ref, top_ref = refs[:2] + ((refs[2],) if with_top else (None,))
    send_ref, keep_ref, out_top = refs[2 + with_top:] if with_top else refs[2:] + (None,)
    rows, half = held_ref.shape[0], keep_ref.shape[0]
    keep = (rank_of() >> below) & 1
    for ref, at in ((send_ref, 1 - keep), (keep_ref, keep)):
        part = pl.ds(pl.multiple_of(at * half, SUBLANES), half)
        ref[:half] = held_ref[part] + got_ref[part]
    if with_top:
        top = top_ref[...]
        if got_ref.shape[0] > rows:
            top = jnp.maximum(top, got_ref[rows:])
        out_top[...] = top
        send_ref[half:] = top


def fold(rank_of, below, held, got, top=None):
    rows, side = held.shape
    half = rows // 2
    with_top = top is not None
    extra = SUBLANES if with_top else 0
    return pl.pallas_call(
        functools.partial(fold_kernel, rank_of, below, with_top),
        out_shape=(f32(half + extra, side), f32(half, side)) + ((f32(*top.shape),) if with_top else ()),
        in_specs=[VM] * (2 + with_top),
        out_specs=(VM,) * (2 + with_top),
        compiler_params=params(8),
        cost_estimate=cost(10**6, 12 * rows * side),
        name="fold",
    )(held, got, *((top,) if with_top else ()))


def finish_kernel(parts, tile_ref, light_ref, top_ref, g_tile, g_left, g_up, probe_ref, *refs):
    pairs, n_col = parts
    block_refs = refs[:2 * pairs]
    object_out, probe_out, new_object, new_probe, sums, sem = refs[2 * pairs:]
    modes, side = probe_ref.shape[1], probe_ref.shape[2]
    rows, cols = light_ref.shape
    top = top_ref[0:1, 0:1]
    for at in range(0, cols, side):
        part = slice(at, at + side)
        scale = 1.0 / (light_ref[:, part] + 0.1 * top)
        for i in range(2):
            total = g_tile[i, :, part] + g_up[i, :, part]
            if at == 0:
                total += g_left[i]
            new_object[i, :, part] = tile_ref[i, :, part] + total * scale
    stores = [pltpu.make_async_copy(new_object, object_out, sem.at[0])]
    stores[0].start()

    share = block_refs[0].shape[0] - SUBLANES
    piece = share // n_col
    my_row = lax.axis_index("row")
    core, pair, col_rank = lax.rem(my_row, 2), my_row // 2, my_col_rank()
    for i, ref in enumerate(block_refs):
        flip, d = i // pairs, i % pairs
        base = ((core ^ flip) * pairs + (plane_rank(core ^ flip, pair) ^ d)) * share
        for e in range(n_col):
            to = pl.multiple_of(base + (col_rank ^ e) * piece, SUBLANES)
            sums[pl.ds(to, piece)] = ref[e * piece:(e + 1) * piece]
    den = sums[2 * modes * side:(2 * modes + 1) * side]
    top = jnp.max(jnp.max(den, axis=0, keepdims=True), axis=1, keepdims=True)
    scale = 1.0 / (den + 0.1 * top)
    for i in range(2):
        for k in range(modes):
            at = (i * modes + k) * side
            new_probe[i, k] = probe_ref[i, k] + sums[at:at + side] * scale
        stores.append(pltpu.make_async_copy(new_probe.at[i], probe_out.at[i], sem.at[1 + i]))
        stores[-1].start()
    for store in stores:
        store.wait()


def f32(*shape):
    return jax.ShapeDtypeStruct(shape, jnp.float32)


VM = pl.BlockSpec(memory_space=pltpu.VMEM)
SM = pl.BlockSpec(memory_space=pltpu.SMEM)
ANY = pl.BlockSpec(memory_space=pl.ANY)
HBM = pl.BlockSpec(memory_space=pltpu.HBM)


def params(mib):
    return pltpu.CompilerParams(vmem_limit_bytes=mib * MIB)


def hbm(*shape):
    return pltpu.HBM(shape, jnp.float32)


def vmem(*shape):
    return pltpu.VMEM(shape, jnp.float32)


def in_hbm(value):
    return pltpu.with_memory_space_constraint(value, pltpu.HBM)


def cost(flops, moved):
    return pl.CostEstimate(flops=flops, bytes_accessed=moved, transcendentals=0)


def body(object_field, probe, amplitudes, corners, counts):
    rows, cols = object_field.shape[1], object_field.shape[2]
    modes, side = probe.shape[1], probe.shape[2]
    slots = amplitudes.shape[2]
    pairs, n_col = lax.axis_size("row") // 2, lax.axis_size("col")
    step = SUBLANES * 2 * pairs * n_col
    total_rows = -(-(2 * modes + 1) * side // step) * step
    share = total_rows // (2 * pairs)
    piece = share // n_col
    spots = corners[0, 0]

    right = shifted(object_field[:, :, :side], 0, -1)
    below = shifted(object_field[:, :side, :], -1, 0)
    from_left = shifted(spots, 0, 1)
    from_up = shifted(jnp.concatenate([spots, from_left], axis=0), 1, 0)
    lit = jnp.sum(probe[0] * probe[0] + probe[1] * probe[1], axis=0)
    right, from_up, lit = lax.optimization_barrier((right, from_up, lit))
    corner = shifted(right[:, :side, :], -1, 0)
    measured = evens_first(amplitudes[0, 0])
    light, top = pl.pallas_call(
        light_kernel,
        out_shape=(f32(rows, cols), f32(SUBLANES, side)),
        in_specs=[SM] * 5 + [VM],
        out_specs=(VM, VM),
        scratch_shapes=[
            pltpu.VMEM((1, rows + 2 * side, cols + 2 * side), jnp.float32),
        ],
        compiler_params=params(12),
        cost_estimate=cost(10**8, 10**7),
        name="lighting",
    )(counts, spots, from_left, from_up[:slots], from_up[slots:], lit)
    corner, top, measured = lax.optimization_barrier((corner, top, measured))
    g_tile, g_lower, g_right, mine, other = pl.pallas_call(
        main_kernel,
        out_shape=(
            hbm(2, rows, cols), vmem(2, side, cols + side), vmem(2, rows, side),
            vmem(pairs * share, side), vmem(pairs * share, side),
        ),
        in_specs=[SM] * 2 + [HBM] + [ANY] * 3 + [HBM] * 3,
        out_specs=(HBM,) + (VM,) * 4,
        scratch_shapes=[
            pltpu.VMEM((2, rows + side, cols + side), jnp.float32),
            pltpu.VMEM((2, rows + side, cols + side), jnp.float32),
            pltpu.VMEM((2, side, modes * side), jnp.bfloat16),
            pltpu.VMEM((2, modes * side, side), jnp.bfloat16),
            pltpu.VMEM((2, modes * side, side), jnp.float32),
            pltpu.VMEM((2, side, side), jnp.float32),
            pltpu.VMEM((total_rows, side), jnp.float32),
            pltpu.VMEM((2, side, side), jnp.float32),
            pltpu.VMEM(probe.shape, jnp.float32),
            pltpu.VMEM((4, side, side), jnp.bfloat16),
            pltpu.SemaphoreType.DMA((6,)),
            pltpu.SemaphoreType.DMA((2,)),
            pltpu.SemaphoreType.DMA((1,)),
        ],
        compiler_params=params(22),
        cost_estimate=cost(7 * 10**9, 2 * 10**7),
        name="positions",
    )(counts, spots, in_hbm(object_field), below, right, corner, *map(in_hbm, (measured, probe, tables(side))))

    arrived = swapped(other, 1, 0)
    held, got = mine, arrived
    for i in range(plane_bits()):
        send, held = fold(my_plane_rank, plane_bits() - 1 - i, held, got)
        got = flipped(send, i)
    for i in range(col_bits()):
        send, held, top = fold(my_col_rank, col_bits() - 1 - i, held, got, top)
        if i == 0:
            send, g_lower = lax.optimization_barrier((send, g_lower))
        got = swapped(send, 0, 1 << i)
    g_up = shifted(g_lower, 1, 0)
    own = held + got[:piece]
    top = jnp.maximum(top, got[piece:])
    pieces = [own]
    for e in range(1, n_col):
        pieces.append(swapped(own, 0, rank_by(e, range(col_bits()))))
    own = jnp.concatenate(pieces + [top], axis=0)
    own, g_up, g_right = lax.optimization_barrier((own, g_up, g_right + g_up[:, :, cols:]))
    g_left = shifted(g_right, 0, 1)
    blocks = [own]
    for i in reversed(range(plane_bits())):
        blocks = blocks + [flipped(block, i) for block in blocks]
    blocks[-1], g_left = lax.optimization_barrier((blocks[-1], g_left))
    blocks = blocks + [swapped(block, 1, 0) for block in blocks]
    top = functools.reduce(jnp.maximum, [block[share:] for block in blocks])
    return pl.pallas_call(
        functools.partial(finish_kernel, (pairs, n_col)),
        out_shape=(f32(*object_field.shape), f32(*probe.shape)),
        in_specs=[VM] * (7 + len(blocks)),
        out_specs=(ANY, ANY),
        scratch_shapes=[
            pltpu.VMEM(object_field.shape, jnp.float32),
            pltpu.VMEM(probe.shape, jnp.float32),
            pltpu.VMEM((total_rows, side), jnp.float32),
            pltpu.SemaphoreType.DMA((3,)),
        ],
        compiler_params=params(20),
        cost_estimate=cost(10**6, 10**7),
        name="update",
    )(object_field, light, top, g_tile, g_left, g_up, probe, *blocks)


def solution(mesh):
    in_specs = (
        P(None, "row", "col"),
        P(),
        P("row", "col", None, None, None),
        P("row", "col", None, None),
        P(),
    )
    out_specs = (P(None, "row", "col"), P())
    return jax.shard_map(body, mesh=mesh, in_specs=in_specs, out_specs=out_specs, check_vma=False)
```

```python
import functools
import math

import jax
import jax.numpy as jnp
import numpy as np
from jax import lax
from jax.experimental import pallas as pl
from jax.experimental.pallas import tpu as pltpu
from jax.sharding import PartitionSpec as P

LANES = 128
SUBLANES = 8
MIB = 1024 * 1024


def shifted(value, d_row, d_col):
    rows, cols = lax.axis_size("row"), lax.axis_size("col")
    pairs = []
    for r in range(rows):
        for c in range(cols):
            if 0 <= r + d_row < rows and 0 <= c + d_col < cols:
                pairs.append((r * cols + c, (r + d_row) * cols + c + d_col))
    return lax.ppermute(value, ("row", "col"), pairs)


def swapped(value, flip_row, flip_col):
    rows, cols = lax.axis_size("row"), lax.axis_size("col")
    pairs = [(r * cols + c, (r ^ flip_row) * cols + (c ^ flip_col)) for r in range(rows) for c in range(cols)]
    return lax.ppermute(value, ("row", "col"), pairs)


def plane_bits():
    return (lax.axis_size("row") // 2).bit_length() - 1


def col_bits():
    return lax.axis_size("col").bit_length() - 1


def plane_bit(core, step):
    return step if core == 0 else plane_bits() - 1 - step


def rank_by(index, bits):
    rank = 0
    for bit in bits:
        rank = rank * 2 + ((index >> bit) & 1)
    return rank


def plane_rank(core, pair):
    ranks = [rank_by(pair, [plane_bit(c, step) for step in range(plane_bits())]) for c in range(2)]
    return jnp.where(core == 0, ranks[0], ranks[1])


def my_plane_rank():
    my_row = lax.axis_index("row")
    return plane_rank(lax.rem(my_row, 2), my_row // 2)


def my_col_rank():
    return rank_by(lax.axis_index("col"), range(col_bits()))


def flipped(value, step):
    rows, cols = lax.axis_size("row"), lax.axis_size("col")
    pairs = [
        (r * cols + c, (r ^ (2 << plane_bit(r % 2, step))) * cols + c) for r in range(rows) for c in range(cols)
    ]
    return lax.ppermute(value, ("row", "col"), pairs)


def tables(side):
    index = np.arange(side)
    angle = (index[:, None] * index[None, :] % side) * (2.0 * math.pi / side)
    scale = 1.0 / math.sqrt(side)
    re = (np.cos(angle) * scale).astype(np.float32)
    im = (-np.sin(angle) * scale).astype(np.float32)
    blocks = []
    for first in (0, 1):
        a, b = re[first::2, :side // 2], im[first::2, :side // 2]
        blocks.append(np.block([[a, -b], [b, a]]))
    return jnp.asarray(np.stack(blocks + [block.T for block in blocks]), jnp.bfloat16)


def evens_first(amplitudes, rows):
    side = amplitudes.shape[-1]
    order = np.concatenate([np.arange(0, side, 2), np.arange(1, side, 2)])
    pick = jnp.asarray(np.eye(side)[order], jnp.float32)
    form = "ab,sbc->sac" if rows else "cb,sab->sac"
    return jnp.einsum(form, pick, amplitudes, precision=lax.Precision.HIGH)


def corner_of(row, col):
    row_base = pl.multiple_of(row // SUBLANES * SUBLANES, SUBLANES)
    col_base = pl.multiple_of(col // LANES * LANES, LANES)
    return row_base, row - row_base, col_base, col - col_base


def window_at(ref, part, row, col, side):
    row_base, down, col_base, over = corner_of(row, col)
    groups = side // SUBLANES
    lane = lax.broadcasted_iota(jnp.int32, (side, LANES), 1)
    sub = lax.broadcasted_iota(jnp.int32, (groups, SUBLANES, LANES), 1)
    turned = []
    for j in range(side // LANES + 1):
        block = ref[part, pl.ds(row_base, side + SUBLANES), pl.ds(col_base + j * LANES, LANES)]
        block = block.reshape(groups + 1, SUBLANES, LANES)
        block = pltpu.roll(block, lax.rem(SUBLANES - down, SUBLANES), 1)
        block = jnp.where(sub < SUBLANES - down, block[:groups], block[1:]).reshape(side, LANES)
        turned.append(pltpu.roll(block, lax.rem(LANES - over, LANES), 1))
    parts = [jnp.where(lane < LANES - over, turned[j], turned[j + 1]) for j in range(side // LANES)]
    return jnp.concatenate(parts, axis=1)


def add_at(ref, part, row, col, value, side):
    row_base, down, col_base, over = corner_of(row, col)
    groups = side // SUBLANES
    blocks = side // LANES
    lane = lax.broadcasted_iota(jnp.int32, (side, LANES), 1)
    sub = lax.broadcasted_iota(jnp.int32, (groups + 1, SUBLANES, LANES), 1)
    turned = [pltpu.roll(value[:, j * LANES:(j + 1) * LANES], over, 1) for j in range(blocks)]
    none = jnp.zeros((side, LANES), value.dtype)
    gap = jnp.zeros((1, SUBLANES, LANES), value.dtype)
    for j in range(blocks + 1):
        block = jnp.where(lane >= over, turned[j] if j < blocks else none, turned[j - 1] if j else none)
        block = pltpu.roll(block.reshape(groups, SUBLANES, LANES), down, 1)
        block = jnp.where(
            sub >= down, jnp.concatenate([block, gap], axis=0), jnp.concatenate([gap, block], axis=0)
        )
        place = (part, pl.ds(row_base, side + SUBLANES), pl.ds(col_base + j * LANES, LANES))
        ref[place] += block.reshape(side + SUBLANES, LANES)


def main_kernel(
    counts_ref, spots_ref, tile_hbm, below_any, right_any, corner_any, amp_hbm, probe_hbm, table_hbm,
    g_tile, g_lower, g_right, *rest
):
    chains = (len(rest) - 13) // 2
    mine_refs, other_refs = rest[:chains], rest[chains:2 * chains]
    (
        ext, gacc, stage, turned, wave, wins, sums, amp_ref, probe_ref, table_ref, in_sem, amp_sem, out_sem,
    ) = rest[2 * chains:]
    modes, side = probe_ref.shape[1], probe_ref.shape[2]
    rows, cols = tile_hbm.shape[1], tile_hbm.shape[2]
    low = side // 2
    my_row, my_col = lax.axis_index("row"), lax.axis_index("col")
    count = counts_ref[my_row, my_col]
    loads = [(probe_hbm, probe_ref), (table_hbm, table_ref)]
    for ref, r, c in ((tile_hbm, 0, 0), (below_any, rows, 0), (right_any, 0, cols), (corner_any, rows, cols)):
        loads.append((ref, ext.at[:, pl.ds(r, ref.shape[1]), pl.ds(c, ref.shape[2])]))
    loads = [pltpu.make_async_copy(a, b, in_sem.at[i]) for i, (a, b) in enumerate(loads)]

    def amp_load(p, slot):
        return pltpu.make_async_copy(amp_hbm.at[p], amp_ref.at[slot], amp_sem.at[slot])

    for load in loads:
        load.start()
    amp_load(0, 0).start()
    gacc[...] = jnp.zeros_like(gacc)
    sums[...] = jnp.zeros_like(sums)
    for load in loads:
        load.wait()

    def dot(a, b):
        return jnp.dot(a, b, preferred_element_type=jnp.float32)

    def plane(index):
        return slice(index * side, (index + 1) * side)

    def bf16(value):
        return value.astype(jnp.bfloat16)

    def step(p, carry):
        slot = lax.rem(p, 2)

        @pl.when(p + 1 < count)
        def _():
            amp_load(p + 1, 1 - slot).start()

        row, col = spots_ref[p, 0] - my_row * rows, spots_ref[p, 1] - my_col * cols
        win_re = window_at(ext, 0, row, col, side)
        win_im = window_at(ext, 1, row, col, side)
        wins[0], wins[1] = win_re, win_im
        sums[plane(2 * modes)] += win_re * win_re + win_im * win_im
        for k in range(modes):
            pr, pi = probe_ref[0, k], probe_ref[1, k]
            for i, psi in enumerate((pr * win_re - pi * win_im, pr * win_im + pi * win_re)):
                stage[0, i * low:(i + 1) * low, plane(k)] = bf16(psi[:low] + psi[low:])
                stage[1, i * low:(i + 1) * low, plane(k)] = bf16(psi[:low] - psi[low:])
        for k in range(modes):
            for parity in range(2):
                half = dot(table_ref[parity], stage[parity, :, plane(k)])
                at = k * side + parity * low
                for i in range(2):
                    left, right = half[i * low:(i + 1) * low, :low], half[i * low:(i + 1) * low, low:]
                    turned[0, at:at + low, i * low:(i + 1) * low] = bf16(left + right)
                    turned[1, at:at + low, i * low:(i + 1) * low] = bf16(left - right)
        for parity in range(2):
            wave[parity] = dot(turned[parity], table_ref[2 + parity])
        amp_load(p, slot).wait()
        for parity in range(2):
            model = jnp.zeros((side, low), jnp.float32)
            for k in range(modes):
                wr, wi = wave[parity, plane(k), :low], wave[parity, plane(k), low:]
                model += wr * wr + wi * wi
            factor = amp_ref[slot, :, parity * low:(parity + 1) * low] * lax.rsqrt(jnp.maximum(model, 1.0)) - 1.0
            for k in range(modes):
                at = k * side + parity * low
                for i in range(2):
                    target = bf16(wave[parity, plane(k), i * low:(i + 1) * low] * factor)
                    stage[0, i * low:(i + 1) * low, at:at + low] = target[:low]
                    stage[1, i * low:(i + 1) * low, at:at + low] = target[low:]
        for k in range(modes):
            even = dot(table_ref[2], stage[0, :, plane(k)])
            odd = dot(table_ref[3], stage[1, :, plane(k)])
            for lower, back in enumerate((bf16(even + odd), bf16(even - odd))):
                at = k * side + lower * low
                for i in range(2):
                    for parity in range(2):
                        turned[parity, at:at + low, i * low:(i + 1) * low] = (
                            back[i * low:(i + 1) * low, parity * low:(parity + 1) * low]
                        )
        for parity in range(2):
            wave[parity] = dot(turned[parity], table_ref[parity])
        grads = []
        for lower in range(2):
            part = slice(lower * low, (lower + 1) * low)
            grad_re = jnp.zeros((side, low), jnp.float32)
            grad_im = jnp.zeros((side, low), jnp.float32)
            win_re, win_im = wins[0, :, part], wins[1, :, part]
            for k in range(modes):
                even_re, even_im = wave[0, plane(k), :low], wave[0, plane(k), low:]
                odd_re, odd_im = wave[1, plane(k), :low], wave[1, plane(k), low:]
                if lower:
                    cr, ci = even_re - odd_re, even_im - odd_im
                else:
                    cr, ci = even_re + odd_re, even_im + odd_im
                pr, pi = probe_ref[0, k, :, part], probe_ref[1, k, :, part]
                grad_re += pr * cr + pi * ci
                grad_im += pr * ci - pi * cr
                sums[plane(k), part] += win_re * cr + win_im * ci
                sums[plane(modes + k), part] += win_re * ci - win_im * cr
            grads.append((grad_re, grad_im))
        for i in range(2):
            add_at(gacc, i, row, col, jnp.concatenate([grads[0][i], grads[1][i]], axis=1), side)
        return carry

    lax.fori_loop(0, count, step, 0)

    store = pltpu.make_async_copy(gacc.at[:, pl.ds(0, rows), pl.ds(0, cols)], g_tile, out_sem.at[0])
    store.start()
    core = lax.rem(my_row, 2)
    half = sums.shape[0] // 2
    for refs, at in ((other_refs, 1 - core), (mine_refs, core)):
        start = 0
        for ref in refs:
            ref[...] = sums[pl.ds(pl.multiple_of(at * half + start, SUBLANES), ref.shape[0])]
            start += ref.shape[0]
    g_lower[...] = gacc[:, rows:]
    g_right[...] = gacc[:, :rows, cols:]
    store.wait()


def light_kernel(counts_ref, spots_ref, left_ref, up_ref, diag_ref, lit_ref, light_ref, top_ref, acc):
    side = lit_ref.shape[0]
    rows, cols = light_ref.shape
    my_row, my_col = lax.axis_index("row"), lax.axis_index("col")
    acc[...] = jnp.zeros_like(acc)
    for ref, d_row, d_col in ((spots_ref, 0, 0), (left_ref, 0, 1), (up_ref, 1, 0), (diag_ref, 1, 1)):
        inside = (my_row >= d_row) & (my_col >= d_col)
        number = counts_ref[jnp.maximum(my_row - d_row, 0), jnp.maximum(my_col - d_col, 0)]

        def step(p, carry, ref=ref):
            row, col = ref[p, 0] - my_row * rows + side, ref[p, 1] - my_col * cols + side

            @pl.when((row > 0) & (col > 0))
            def _():
                add_at(acc, 0, row, col, lit_ref[...], side)

            return carry

        lax.fori_loop(0, jnp.where(inside, number, 0), step, 0)
    light = acc[0, side:side + rows, side:side + cols]
    light_ref[...] = light
    top = jnp.max(light, axis=0, keepdims=True)
    top = jnp.max(top, axis=1, keepdims=True)
    top_ref[...] = jnp.broadcast_to(top, top_ref.shape)


def fold_kernel(rank_of, below, with_top, *refs):
    held_ref, got_ref, top_ref = refs[:2] + ((refs[2],) if with_top else (None,))
    send_ref, keep_ref, out_top = refs[2 + with_top:] if with_top else refs[2:] + (None,)
    rows, half = held_ref.shape[0], keep_ref.shape[0]
    keep = (rank_of() >> below) & 1
    for ref, at in ((send_ref, 1 - keep), (keep_ref, keep)):
        part = pl.ds(pl.multiple_of(at * half, SUBLANES), half)
        ref[:half] = held_ref[part] + got_ref[part]
    if with_top:
        top = top_ref[...]
        if got_ref.shape[0] > rows:
            top = jnp.maximum(top, got_ref[rows:])
        out_top[...] = top
        send_ref[half:] = top


def fold(rank_of, below, held, got, top=None):
    rows, side = held.shape
    half = rows // 2
    with_top = top is not None
    extra = SUBLANES if with_top else 0
    return pl.pallas_call(
        functools.partial(fold_kernel, rank_of, below, with_top),
        out_shape=(f32(half + extra, side), f32(half, side)) + ((f32(*top.shape),) if with_top else ()),
        in_specs=[VM] * (2 + with_top),
        out_specs=(VM,) * (2 + with_top),
        compiler_params=params(8),
        cost_estimate=cost(10**6, 12 * rows * side),
        name="fold",
    )(held, got, *((top,) if with_top else ()))


def finish_kernel(parts, tile_ref, light_ref, top_ref, g_tile, g_left, g_up, probe_ref, *refs):
    pairs, n_col, pieces = parts
    count = 2 * pairs * len(pieces)
    block_refs = refs[:count]
    object_out, probe_out, new_object, new_probe, sums, sem = refs[count:]
    modes, side = probe_ref.shape[1], probe_ref.shape[2]
    rows, cols = light_ref.shape
    top = top_ref[0:1, 0:1]
    for at in range(0, cols, side):
        part = slice(at, at + side)
        scale = 1.0 / (light_ref[:, part] + 0.1 * top)
        for i in range(2):
            total = g_tile[i, :, part] + g_up[i, :, part]
            if at == 0:
                total += g_left[i]
            new_object[i, :, part] = tile_ref[i, :, part] + total * scale
    stores = [pltpu.make_async_copy(new_object, object_out, sem.at[0])]
    stores[0].start()

    my_row = lax.axis_index("row")
    core, pair, col_rank = lax.rem(my_row, 2), my_row // 2, my_col_rank()
    half, start = sums.shape[0] // 2, 0
    for j, piece in enumerate(pieces):
        for i in range(2 * pairs):
            ref, flip, d = block_refs[j * 2 * pairs + i], i // pairs, i % pairs
            base = (core ^ flip) * half + start + (plane_rank(core ^ flip, pair) ^ d) * (n_col * piece)
            for e in range(n_col):
                to = pl.multiple_of(base + (col_rank ^ e) * piece, SUBLANES)
                sums[pl.ds(to, piece)] = ref[e * piece:(e + 1) * piece]
        start += pairs * n_col * piece
    den = sums[2 * modes * side:(2 * modes + 1) * side]
    top = jnp.max(jnp.max(den, axis=0, keepdims=True), axis=1, keepdims=True)
    scale = 1.0 / (den + 0.1 * top)
    for i in range(2):
        for k in range(modes):
            at = (i * modes + k) * side
            new_probe[i, k] = probe_ref[i, k] + sums[at:at + side] * scale
        stores.append(pltpu.make_async_copy(new_probe.at[i], probe_out.at[i], sem.at[1 + i]))
        stores[-1].start()
    for store in stores:
        store.wait()


def f32(*shape):
    return jax.ShapeDtypeStruct(shape, jnp.float32)


VM = pl.BlockSpec(memory_space=pltpu.VMEM)
SM = pl.BlockSpec(memory_space=pltpu.SMEM)
ANY = pl.BlockSpec(memory_space=pl.ANY)
HBM = pl.BlockSpec(memory_space=pltpu.HBM)


def params(mib):
    return pltpu.CompilerParams(vmem_limit_bytes=mib * MIB)


def hbm(*shape):
    return pltpu.HBM(shape, jnp.float32)


def vmem(*shape):
    return pltpu.VMEM(shape, jnp.float32)


def in_hbm(value):
    return pltpu.with_memory_space_constraint(value, pltpu.HBM)


def cost(flops, moved):
    return pl.CostEstimate(flops=flops, bytes_accessed=moved, transcendentals=0)


def body(object_field, probe, amplitudes, corners, counts):
    rows, cols = object_field.shape[1], object_field.shape[2]
    modes, side = probe.shape[1], probe.shape[2]
    slots = amplitudes.shape[2]
    pairs, n_col = lax.axis_size("row") // 2, lax.axis_size("col")
    step = SUBLANES * 2 * pairs * n_col
    total_rows = -(-(2 * modes + 1) * side // step) * step
    piece = total_rows // (2 * pairs * n_col)
    first = -(-piece // (2 * SUBLANES)) * SUBLANES
    pieces = [first, piece - first] if piece > first else [piece]
    spots = corners[0, 0]

    right = shifted(object_field[:, :, :side], 0, -1)
    lit = jnp.sum(probe[0] * probe[0] + probe[1] * probe[1], axis=0)
    measured = evens_first(amplitudes[0, 0], True)
    tile, measured, spots_now = lax.optimization_barrier((object_field, measured, spots))
    below = shifted(tile[:, :side, :], -1, 0)
    from_left = shifted(spots_now, 0, 1)
    right, from_left, lit = lax.optimization_barrier((right, from_left, lit))
    corner = shifted(right[:, :side, :], -1, 0)
    from_up = shifted(jnp.concatenate([spots, from_left], axis=0), 1, 0)
    measured = evens_first(measured, False)
    light, top = pl.pallas_call(
        light_kernel,
        out_shape=(f32(rows, cols), f32(SUBLANES, side)),
        in_specs=[SM] * 5 + [VM],
        out_specs=(VM, VM),
        scratch_shapes=[
            pltpu.VMEM((1, rows + 2 * side, cols + 2 * side), jnp.float32),
        ],
        compiler_params=params(12),
        cost_estimate=cost(10**8, 10**7),
        name="lighting",
    )(counts, spots, from_left, from_up[:slots], from_up[slots:], lit)
    corner, top, measured = lax.optimization_barrier((corner, top, measured))
    g_tile, g_lower, g_right, *halves = pl.pallas_call(
        main_kernel,
        out_shape=(
            hbm(2, rows, cols), vmem(2, side, cols + side), vmem(2, rows, side),
        ) + tuple(vmem(pairs * n_col * piece, side) for piece in pieces) * 2,
        in_specs=[SM] * 2 + [HBM] + [ANY] * 3 + [HBM] * 3,
        out_specs=(HBM,) + (VM,) * (2 + 2 * len(pieces)),
        scratch_shapes=[
            pltpu.VMEM((2, rows + side, cols + side), jnp.float32),
            pltpu.VMEM((2, rows + side, cols + side), jnp.float32),
            pltpu.VMEM((2, side, modes * side), jnp.bfloat16),
            pltpu.VMEM((2, modes * side, side), jnp.bfloat16),
            pltpu.VMEM((2, modes * side, side), jnp.float32),
            pltpu.VMEM((2, side, side), jnp.float32),
            pltpu.VMEM((total_rows, side), jnp.float32),
            pltpu.VMEM((2, side, side), jnp.float32),
            pltpu.VMEM(probe.shape, jnp.float32),
            pltpu.VMEM((4, side, side), jnp.bfloat16),
            pltpu.SemaphoreType.DMA((6,)),
            pltpu.SemaphoreType.DMA((2,)),
            pltpu.SemaphoreType.DMA((1,)),
        ],
        compiler_params=params(22),
        cost_estimate=cost(7 * 10**9, 2 * 10**7),
        name="positions",
    )(counts, spots, in_hbm(object_field), below, right, corner, *map(in_hbm, (measured, probe, tables(side))))

    chains = []
    for i, piece in enumerate(pieces):
        chains.append((halves[i], swapped(halves[len(pieces) + i], 1, 0), None if i else top))
    for i in range(plane_bits()):
        for j, (held, got, ride) in enumerate(chains):
            send, held = fold(my_plane_rank, plane_bits() - 1 - i, held, got)
            chains[j] = (held, flipped(send, i), ride)
    for i in range(col_bits()):
        for j, (held, got, ride) in enumerate(chains):
            send, held, *ride = fold(my_col_rank, col_bits() - 1 - i, held, got, ride)
            if i == 0 and j == 0:
                send, g_lower = lax.optimization_barrier((send, g_lower))
            chains[j] = (held, swapped(send, 0, 1 << i), ride[0] if ride else None)
    g_up = shifted(g_lower, 1, 0)
    owns = []
    for piece, (held, got, ride) in zip(pieces, chains):
        own = held + got[:piece]
        parts = [own] + [swapped(own, 0, rank_by(e, range(col_bits()))) for e in range(1, n_col)]
        if ride is not None:
            parts.append(jnp.maximum(ride, got[piece:]))
        owns.append(jnp.concatenate(parts, axis=0))
    owns[0], g_up, g_right = lax.optimization_barrier((owns[0], g_up, g_right + g_up[:, :, cols:]))
    g_left = shifted(g_right, 0, 1)
    gathered = []
    for j, own in enumerate(owns):
        blocks = [own]
        for i in reversed(range(plane_bits())):
            blocks = blocks + [flipped(block, i) for block in blocks]
        if j == len(owns) - 1:
            blocks[-1], g_left = lax.optimization_barrier((blocks[-1], g_left))
        gathered.append(blocks + [swapped(block, 1, 0) for block in blocks])
    top = functools.reduce(jnp.maximum, [block[n_col * pieces[0]:] for block in gathered[0]])
    blocks = sum(gathered, [])
    return pl.pallas_call(
        functools.partial(finish_kernel, (pairs, n_col, pieces)),
        out_shape=(f32(*object_field.shape), f32(*probe.shape)),
        in_specs=[VM] * (7 + len(blocks)),
        out_specs=(ANY, ANY),
        scratch_shapes=[
            pltpu.VMEM(object_field.shape, jnp.float32),
            pltpu.VMEM(probe.shape, jnp.float32),
            pltpu.VMEM((total_rows, side), jnp.float32),
            pltpu.SemaphoreType.DMA((3,)),
        ],
        compiler_params=params(20),
        cost_estimate=cost(10**6, 10**7),
        name="update",
    )(object_field, light, top, g_tile, g_left, g_up, probe, *blocks)


def solution(mesh):
    in_specs = (
        P(None, "row", "col"),
        P(),
        P("row", "col", None, None, None),
        P("row", "col", None, None),
        P(),
    )
    out_specs = (P(None, "row", "col"), P())
    return jax.shard_map(body, mesh=mesh, in_specs=in_specs, out_specs=out_specs, check_vma=False)
```

```python
import functools
import math

import jax
import jax.numpy as jnp
import numpy as np
from jax import lax
from jax.experimental import pallas as pl
from jax.experimental.pallas import tpu as pltpu
from jax.sharding import PartitionSpec as P

LANES = 128
SUBLANES = 8
MIB = 1024 * 1024


def shifted(value, d_row, d_col):
    rows, cols = lax.axis_size("row"), lax.axis_size("col")
    pairs = []
    for r in range(rows):
        for c in range(cols):
            if 0 <= r + d_row < rows and 0 <= c + d_col < cols:
                pairs.append((r * cols + c, (r + d_row) * cols + c + d_col))
    return lax.ppermute(value, ("row", "col"), pairs)


def swapped(value, flip_row, flip_col):
    rows, cols = lax.axis_size("row"), lax.axis_size("col")
    pairs = [(r * cols + c, (r ^ flip_row) * cols + (c ^ flip_col)) for r in range(rows) for c in range(cols)]
    return lax.ppermute(value, ("row", "col"), pairs)


def plane_bits():
    return (lax.axis_size("row") // 2).bit_length() - 1


def col_bits():
    return lax.axis_size("col").bit_length() - 1


def plane_bit(core, step):
    return step if core == 0 else plane_bits() - 1 - step


def rank_by(index, bits):
    rank = 0
    for bit in bits:
        rank = rank * 2 + ((index >> bit) & 1)
    return rank


def plane_rank(core, pair):
    ranks = [rank_by(pair, [plane_bit(c, step) for step in range(plane_bits())]) for c in range(2)]
    return jnp.where(core == 0, ranks[0], ranks[1])


def my_plane_rank():
    my_row = lax.axis_index("row")
    return plane_rank(lax.rem(my_row, 2), my_row // 2)


def my_col_rank():
    return rank_by(lax.axis_index("col"), range(col_bits()))


def flipped(value, step):
    rows, cols = lax.axis_size("row"), lax.axis_size("col")
    pairs = [
        (r * cols + c, (r ^ (2 << plane_bit(r % 2, step))) * cols + c) for r in range(rows) for c in range(cols)
    ]
    return lax.ppermute(value, ("row", "col"), pairs)


def tables(side):
    index = np.arange(side)
    angle = (index[:, None] * index[None, :] % side) * (2.0 * math.pi / side)
    scale = 1.0 / math.sqrt(side)
    re = (np.cos(angle) * scale).astype(np.float32)
    im = (-np.sin(angle) * scale).astype(np.float32)
    blocks = []
    for first in (0, 1):
        a, b = re[first::2, :side // 2], im[first::2, :side // 2]
        blocks.append(np.block([[a, -b], [b, a]]))
    return jnp.asarray(np.stack(blocks + [block.T for block in blocks]), jnp.bfloat16)


def evens_first(amplitudes, rows):
    side = amplitudes.shape[-1]
    order = np.concatenate([np.arange(0, side, 2), np.arange(1, side, 2)])
    pick = jnp.asarray(np.eye(side)[order], jnp.float32)
    form = "ab,sbc->sac" if rows else "cb,sab->sac"
    return jnp.einsum(form, pick, amplitudes, precision=lax.Precision.HIGH)


def corner_of(row, col):
    row_base = pl.multiple_of(row // SUBLANES * SUBLANES, SUBLANES)
    col_base = pl.multiple_of(col // LANES * LANES, LANES)
    return row_base, row - row_base, col_base, col - col_base


def window_at(ref, part, row, col, side):
    row_base, down, col_base, over = corner_of(row, col)
    groups = side // SUBLANES
    lane = lax.broadcasted_iota(jnp.int32, (side, LANES), 1)
    sub = lax.broadcasted_iota(jnp.int32, (groups, SUBLANES, LANES), 1)
    turned = []
    for j in range(side // LANES + 1):
        block = ref[part, pl.ds(row_base, side + SUBLANES), pl.ds(col_base + j * LANES, LANES)]
        block = block.reshape(groups + 1, SUBLANES, LANES)
        block = pltpu.roll(block, lax.rem(SUBLANES - down, SUBLANES), 1)
        block = jnp.where(sub < SUBLANES - down, block[:groups], block[1:]).reshape(side, LANES)
        turned.append(pltpu.roll(block, lax.rem(LANES - over, LANES), 1))
    parts = [jnp.where(lane < LANES - over, turned[j], turned[j + 1]) for j in range(side // LANES)]
    return jnp.concatenate(parts, axis=1)


def add_at(ref, part, row, col, value, side):
    row_base, down, col_base, over = corner_of(row, col)
    groups = side // SUBLANES
    blocks = side // LANES
    lane = lax.broadcasted_iota(jnp.int32, (side, LANES), 1)
    sub = lax.broadcasted_iota(jnp.int32, (groups + 1, SUBLANES, LANES), 1)
    turned = [pltpu.roll(value[:, j * LANES:(j + 1) * LANES], over, 1) for j in range(blocks)]
    none = jnp.zeros((side, LANES), value.dtype)
    gap = jnp.zeros((1, SUBLANES, LANES), value.dtype)
    for j in range(blocks + 1):
        block = jnp.where(lane >= over, turned[j] if j < blocks else none, turned[j - 1] if j else none)
        block = pltpu.roll(block.reshape(groups, SUBLANES, LANES), down, 1)
        block = jnp.where(
            sub >= down, jnp.concatenate([block, gap], axis=0), jnp.concatenate([gap, block], axis=0)
        )
        place = (part, pl.ds(row_base, side + SUBLANES), pl.ds(col_base + j * LANES, LANES))
        ref[place] += block.reshape(side + SUBLANES, LANES)


def main_kernel(
    counts_ref, spots_ref, tile_hbm, below_any, right_any, corner_any, amp_hbm, probe_hbm, table_hbm,
    g_tile, g_lower, g_right, *rest
):
    chains = (len(rest) - 13) // 2
    mine_refs, other_refs = rest[:chains], rest[chains:2 * chains]
    (
        ext, gacc, stage, turned, wave, wins, sums, amp_ref, probe_ref, table_ref, in_sem, amp_sem, out_sem,
    ) = rest[2 * chains:]
    modes, side = probe_ref.shape[1], probe_ref.shape[2]
    rows, cols = tile_hbm.shape[1], tile_hbm.shape[2]
    low = side // 2
    my_row, my_col = lax.axis_index("row"), lax.axis_index("col")
    count = counts_ref[my_row, my_col]
    loads = [(probe_hbm, probe_ref), (table_hbm, table_ref)]
    for ref, r, c in ((tile_hbm, 0, 0), (below_any, rows, 0), (right_any, 0, cols), (corner_any, rows, cols)):
        loads.append((ref, ext.at[:, pl.ds(r, ref.shape[1]), pl.ds(c, ref.shape[2])]))
    loads = [pltpu.make_async_copy(a, b, in_sem.at[i]) for i, (a, b) in enumerate(loads)]

    def amp_load(p, slot):
        return pltpu.make_async_copy(amp_hbm.at[p], amp_ref.at[slot], amp_sem.at[slot])

    for load in loads:
        load.start()
    amp_load(0, 0).start()
    gacc[...] = jnp.zeros_like(gacc)
    sums[...] = jnp.zeros_like(sums)
    for load in loads:
        load.wait()

    def dot(a, b):
        return jnp.dot(a, b, preferred_element_type=jnp.float32)

    def plane(index):
        return slice(index * side, (index + 1) * side)

    def bf16(value):
        return value.astype(jnp.bfloat16)

    def step(p, carry):
        slot = lax.rem(p, 2)

        @pl.when(p + 1 < count)
        def _():
            amp_load(p + 1, 1 - slot).start()

        row, col = spots_ref[p, 0] - my_row * rows, spots_ref[p, 1] - my_col * cols
        win_re = window_at(ext, 0, row, col, side)
        win_im = window_at(ext, 1, row, col, side)
        wins[0], wins[1] = win_re, win_im
        sums[plane(2 * modes)] += win_re * win_re + win_im * win_im
        for k in range(modes):
            pr, pi = probe_ref[0, k], probe_ref[1, k]
            for i, psi in enumerate((pr * win_re - pi * win_im, pr * win_im + pi * win_re)):
                stage[0, i * low:(i + 1) * low, plane(k)] = bf16(psi[:low] + psi[low:])
                stage[1, i * low:(i + 1) * low, plane(k)] = bf16(psi[:low] - psi[low:])
        for k in range(modes):
            for parity in range(2):
                half = dot(table_ref[parity], stage[parity, :, plane(k)])
                at = k * side + parity * low
                for i in range(2):
                    left, right = half[i * low:(i + 1) * low, :low], half[i * low:(i + 1) * low, low:]
                    turned[0, at:at + low, i * low:(i + 1) * low] = bf16(left + right)
                    turned[1, at:at + low, i * low:(i + 1) * low] = bf16(left - right)
        for parity in range(2):
            wave[parity] = dot(turned[parity], table_ref[2 + parity])
        amp_load(p, slot).wait()
        for parity in range(2):
            model = jnp.zeros((side, low), jnp.float32)
            for k in range(modes):
                wr, wi = wave[parity, plane(k), :low], wave[parity, plane(k), low:]
                model += wr * wr + wi * wi
            factor = amp_ref[slot, :, parity * low:(parity + 1) * low] * lax.rsqrt(jnp.maximum(model, 1.0)) - 1.0
            for k in range(modes):
                at = k * side + parity * low
                for i in range(2):
                    target = bf16(wave[parity, plane(k), i * low:(i + 1) * low] * factor)
                    stage[0, i * low:(i + 1) * low, at:at + low] = target[:low]
                    stage[1, i * low:(i + 1) * low, at:at + low] = target[low:]
        for k in range(modes):
            even = dot(table_ref[2], stage[0, :, plane(k)])
            odd = dot(table_ref[3], stage[1, :, plane(k)])
            for lower, back in enumerate((bf16(even + odd), bf16(even - odd))):
                at = k * side + lower * low
                for i in range(2):
                    for parity in range(2):
                        turned[parity, at:at + low, i * low:(i + 1) * low] = (
                            back[i * low:(i + 1) * low, parity * low:(parity + 1) * low]
                        )
        for parity in range(2):
            wave[parity] = dot(turned[parity], table_ref[parity])
        grads = []
        for lower in range(2):
            part = slice(lower * low, (lower + 1) * low)
            grad_re = jnp.zeros((side, low), jnp.float32)
            grad_im = jnp.zeros((side, low), jnp.float32)
            win_re, win_im = wins[0, :, part], wins[1, :, part]
            for k in range(modes):
                even_re, even_im = wave[0, plane(k), :low], wave[0, plane(k), low:]
                odd_re, odd_im = wave[1, plane(k), :low], wave[1, plane(k), low:]
                if lower:
                    cr, ci = even_re - odd_re, even_im - odd_im
                else:
                    cr, ci = even_re + odd_re, even_im + odd_im
                pr, pi = probe_ref[0, k, :, part], probe_ref[1, k, :, part]
                grad_re += pr * cr + pi * ci
                grad_im += pr * ci - pi * cr
                sums[plane(k), part] += win_re * cr + win_im * ci
                sums[plane(modes + k), part] += win_re * ci - win_im * cr
            grads.append((grad_re, grad_im))
        for i in range(2):
            add_at(gacc, i, row, col, jnp.concatenate([grads[0][i], grads[1][i]], axis=1), side)
        return carry

    lax.fori_loop(0, count, step, 0)

    store = pltpu.make_async_copy(gacc.at[:, pl.ds(0, rows), pl.ds(0, cols)], g_tile, out_sem.at[0])
    store.start()
    core = lax.rem(my_row, 2)
    half = sums.shape[0] // 2
    for refs, at in ((other_refs, 1 - core), (mine_refs, core)):
        start = 0
        for ref in refs:
            ref[...] = sums[pl.ds(pl.multiple_of(at * half + start, SUBLANES), ref.shape[0])]
            start += ref.shape[0]
    g_lower[...] = gacc[:, rows:]
    g_right[...] = gacc[:, :rows, cols:]
    store.wait()


def light_kernel(counts_ref, spots_ref, left_ref, up_ref, diag_ref, lit_ref, light_ref, top_ref, acc):
    side = lit_ref.shape[0]
    rows, cols = light_ref.shape
    my_row, my_col = lax.axis_index("row"), lax.axis_index("col")
    acc[...] = jnp.zeros_like(acc)
    for ref, d_row, d_col in ((spots_ref, 0, 0), (left_ref, 0, 1), (up_ref, 1, 0), (diag_ref, 1, 1)):
        inside = (my_row >= d_row) & (my_col >= d_col)
        number = counts_ref[jnp.maximum(my_row - d_row, 0), jnp.maximum(my_col - d_col, 0)]

        def step(p, carry, ref=ref):
            row, col = ref[p, 0] - my_row * rows + side, ref[p, 1] - my_col * cols + side

            @pl.when((row > 0) & (col > 0))
            def _():
                add_at(acc, 0, row, col, lit_ref[...], side)

            return carry

        lax.fori_loop(0, jnp.where(inside, number, 0), step, 0)
    light = acc[0, side:side + rows, side:side + cols]
    light_ref[...] = light
    top = jnp.max(light, axis=0, keepdims=True)
    top = jnp.max(top, axis=1, keepdims=True)
    top_ref[...] = jnp.broadcast_to(top, top_ref.shape)


def fold_kernel(rank_of, below, with_top, *refs):
    held_ref, got_ref, top_ref = refs[:2] + ((refs[2],) if with_top else (None,))
    send_ref, keep_ref, out_top = refs[2 + with_top:] if with_top else refs[2:] + (None,)
    rows, half = held_ref.shape[0], keep_ref.shape[0]
    keep = (rank_of() >> below) & 1
    for ref, at in ((send_ref, 1 - keep), (keep_ref, keep)):
        part = pl.ds(pl.multiple_of(at * half, SUBLANES), half)
        ref[:half] = held_ref[part] + got_ref[part]
    if with_top:
        top = top_ref[...]
        if got_ref.shape[0] > rows:
            top = jnp.maximum(top, got_ref[rows:])
        out_top[...] = top
        send_ref[half:] = top


def fold(rank_of, below, held, got, top=None):
    rows, side = held.shape
    half = rows // 2
    with_top = top is not None
    extra = SUBLANES if with_top else 0
    return pl.pallas_call(
        functools.partial(fold_kernel, rank_of, below, with_top),
        out_shape=(f32(half + extra, side), f32(half, side)) + ((f32(*top.shape),) if with_top else ()),
        in_specs=[VM] * (2 + with_top),
        out_specs=(VM,) * (2 + with_top),
        compiler_params=params(8),
        cost_estimate=cost(10**6, 12 * rows * side),
        name="fold",
    )(held, got, *((top,) if with_top else ()))


def finish_kernel(parts, tile_ref, light_ref, top_ref, g_tile, g_left, g_up, probe_ref, *refs):
    pairs, n_col, pieces = parts
    count = 2 * pairs * len(pieces)
    block_refs = refs[:count]
    object_out, probe_out, new_object, new_probe, sums, sem = refs[count:]
    modes, side = probe_ref.shape[1], probe_ref.shape[2]
    rows, cols = light_ref.shape
    top = top_ref[0:1, 0:1]
    for at in range(0, cols, side):
        part = slice(at, at + side)
        scale = 1.0 / (light_ref[:, part] + 0.1 * top)
        for i in range(2):
            total = g_tile[i, :, part] + g_up[i, :, part]
            if at == 0:
                total += g_left[i]
            new_object[i, :, part] = tile_ref[i, :, part] + total * scale
    stores = [pltpu.make_async_copy(new_object, object_out, sem.at[0])]
    stores[0].start()

    my_row = lax.axis_index("row")
    core, pair, col_rank = lax.rem(my_row, 2), my_row // 2, my_col_rank()
    half, start = sums.shape[0] // 2, 0
    for j, piece in enumerate(pieces):
        for i in range(2 * pairs):
            ref, flip, d = block_refs[j * 2 * pairs + i], i // pairs, i % pairs
            base = (core ^ flip) * half + start + (plane_rank(core ^ flip, pair) ^ d) * (n_col * piece)
            for e in range(n_col):
                to = pl.multiple_of(base + (col_rank ^ e) * piece, SUBLANES)
                sums[pl.ds(to, piece)] = ref[e * piece:(e + 1) * piece]
        start += pairs * n_col * piece
    den = sums[2 * modes * side:(2 * modes + 1) * side]
    top = jnp.max(jnp.max(den, axis=0, keepdims=True), axis=1, keepdims=True)
    scale = 1.0 / (den + 0.1 * top)
    for i in range(2):
        for k in range(modes):
            at = (i * modes + k) * side
            new_probe[i, k] = probe_ref[i, k] + sums[at:at + side] * scale
        stores.append(pltpu.make_async_copy(new_probe.at[i], probe_out.at[i], sem.at[1 + i]))
        stores[-1].start()
    for store in stores:
        store.wait()


def f32(*shape):
    return jax.ShapeDtypeStruct(shape, jnp.float32)


VM = pl.BlockSpec(memory_space=pltpu.VMEM)
SM = pl.BlockSpec(memory_space=pltpu.SMEM)
ANY = pl.BlockSpec(memory_space=pl.ANY)
HBM = pl.BlockSpec(memory_space=pltpu.HBM)


def params(mib):
    return pltpu.CompilerParams(vmem_limit_bytes=mib * MIB)


def hbm(*shape):
    return pltpu.HBM(shape, jnp.float32)


def vmem(*shape):
    return pltpu.VMEM(shape, jnp.float32)


def in_hbm(value):
    return pltpu.with_memory_space_constraint(value, pltpu.HBM)


def cost(flops, moved):
    return pl.CostEstimate(flops=flops, bytes_accessed=moved, transcendentals=0)


def body(object_field, probe, amplitudes, corners, counts):
    rows, cols = object_field.shape[1], object_field.shape[2]
    modes, side = probe.shape[1], probe.shape[2]
    slots = amplitudes.shape[2]
    pairs, n_col = lax.axis_size("row") // 2, lax.axis_size("col")
    step = SUBLANES * 2 * pairs * n_col
    total_rows = -(-(2 * modes + 1) * side // step) * step
    piece = total_rows // (2 * pairs * n_col)
    pieces = [piece]
    spots = corners[0, 0]

    right = shifted(object_field[:, :, :side], 0, -1)
    lit = jnp.sum(probe[0] * probe[0] + probe[1] * probe[1], axis=0)
    measured = evens_first(amplitudes[0, 0], True)
    tile, measured, spots_now = lax.optimization_barrier((object_field, measured, spots))
    below = shifted(tile[:, :side, :], -1, 0)
    from_left = shifted(spots_now, 0, 1)
    measured = evens_first(measured, False)
    right, from_left, lit, measured = lax.optimization_barrier((right, from_left, lit, measured))
    corner = shifted(right[:, :side, :], -1, 0)
    from_up = shifted(jnp.concatenate([spots, from_left], axis=0), 1, 0)
    light, top = pl.pallas_call(
        light_kernel,
        out_shape=(f32(rows, cols), f32(SUBLANES, side)),
        in_specs=[SM] * 5 + [VM],
        out_specs=(VM, VM),
        scratch_shapes=[
            pltpu.VMEM((1, rows + 2 * side, cols + 2 * side), jnp.float32),
        ],
        compiler_params=params(12),
        cost_estimate=cost(10**8, 10**7),
        name="lighting",
    )(counts, spots, from_left, from_up[:slots], from_up[slots:], lit)
    corner, top, measured = lax.optimization_barrier((corner, top, measured))
    g_tile, g_lower, g_right, *halves = pl.pallas_call(
        main_kernel,
        out_shape=(
            hbm(2, rows, cols), vmem(2, side, cols + side), vmem(2, rows, side),
        ) + tuple(vmem(pairs * n_col * piece, side) for piece in pieces) * 2,
        in_specs=[SM] * 2 + [HBM] + [ANY] * 3 + [HBM] * 3,
        out_specs=(HBM,) + (VM,) * (2 + 2 * len(pieces)),
        scratch_shapes=[
            pltpu.VMEM((2, rows + side, cols + side), jnp.float32),
            pltpu.VMEM((2, rows + side, cols + side), jnp.float32),
            pltpu.VMEM((2, side, modes * side), jnp.bfloat16),
            pltpu.VMEM((2, modes * side, side), jnp.bfloat16),
            pltpu.VMEM((2, modes * side, side), jnp.float32),
            pltpu.VMEM((2, side, side), jnp.float32),
            pltpu.VMEM((total_rows, side), jnp.float32),
            pltpu.VMEM((2, side, side), jnp.float32),
            pltpu.VMEM(probe.shape, jnp.float32),
            pltpu.VMEM((4, side, side), jnp.bfloat16),
            pltpu.SemaphoreType.DMA((6,)),
            pltpu.SemaphoreType.DMA((2,)),
            pltpu.SemaphoreType.DMA((1,)),
        ],
        compiler_params=params(22),
        cost_estimate=cost(7 * 10**9, 2 * 10**7),
        name="positions",
    )(counts, spots, in_hbm(object_field), below, right, corner, *map(in_hbm, (measured, probe, tables(side))))

    chains = []
    for i, piece in enumerate(pieces):
        chains.append((halves[i], swapped(halves[len(pieces) + i], 1, 0), None if i else top))
    for i in range(plane_bits()):
        for j, (held, got, ride) in enumerate(chains):
            send, held = fold(my_plane_rank, plane_bits() - 1 - i, held, got)
            chains[j] = (held, flipped(send, i), ride)
    for i in range(col_bits()):
        for j, (held, got, ride) in enumerate(chains):
            send, held, *ride = fold(my_col_rank, col_bits() - 1 - i, held, got, ride)
            if i == 0 and j == 0:
                send, g_lower = lax.optimization_barrier((send, g_lower))
            chains[j] = (held, swapped(send, 0, 1 << i), ride[0] if ride else None)
    g_up = shifted(g_lower, 1, 0)
    owns = []
    for piece, (held, got, ride) in zip(pieces, chains):
        own = held + got[:piece]
        parts = [own] + [swapped(own, 0, rank_by(e, range(col_bits()))) for e in range(1, n_col)]
        if ride is not None:
            parts.append(jnp.maximum(ride, got[piece:]))
        owns.append(jnp.concatenate(parts, axis=0))
    owns[0], g_up, g_right = lax.optimization_barrier((owns[0], g_up, g_right + g_up[:, :, cols:]))
    g_left = shifted(g_right, 0, 1)
    gathered = []
    for j, own in enumerate(owns):
        blocks = [own]
        for i in reversed(range(plane_bits())):
            blocks = blocks + [flipped(block, i) for block in blocks]
        if j == len(owns) - 1:
            blocks[-1], g_left = lax.optimization_barrier((blocks[-1], g_left))
        gathered.append(blocks + [swapped(block, 1, 0) for block in blocks])
    top = functools.reduce(jnp.maximum, [block[n_col * pieces[0]:] for block in gathered[0]])
    blocks = sum(gathered, [])
    return pl.pallas_call(
        functools.partial(finish_kernel, (pairs, n_col, pieces)),
        out_shape=(f32(*object_field.shape), f32(*probe.shape)),
        in_specs=[VM] * (7 + len(blocks)),
        out_specs=(ANY, ANY),
        scratch_shapes=[
            pltpu.VMEM(object_field.shape, jnp.float32),
            pltpu.VMEM(probe.shape, jnp.float32),
            pltpu.VMEM((total_rows, side), jnp.float32),
            pltpu.SemaphoreType.DMA((3,)),
        ],
        compiler_params=params(20),
        cost_estimate=cost(10**6, 10**7),
        name="update",
    )(object_field, light, top, g_tile, g_left, g_up, probe, *blocks)


def solution(mesh):
    in_specs = (
        P(None, "row", "col"),
        P(),
        P("row", "col", None, None, None),
        P("row", "col", None, None),
        P(),
    )
    out_specs = (P(None, "row", "col"), P())
    return jax.shard_map(body, mesh=mesh, in_specs=in_specs, out_specs=out_specs, check_vma=False)
```

```python
import functools
import math

import jax
import jax.numpy as jnp
import numpy as np
from jax import lax
from jax.experimental import pallas as pl
from jax.experimental.pallas import tpu as pltpu
from jax.sharding import PartitionSpec as P

LANES = 128
SUBLANES = 8
MIB = 1024 * 1024


def shifted(value, d_row, d_col):
    rows, cols = lax.axis_size("row"), lax.axis_size("col")
    pairs = []
    for r in range(rows):
        for c in range(cols):
            if 0 <= r + d_row < rows and 0 <= c + d_col < cols:
                pairs.append((r * cols + c, (r + d_row) * cols + c + d_col))
    return lax.ppermute(value, ("row", "col"), pairs)


def swapped(value, flip_row, flip_col):
    rows, cols = lax.axis_size("row"), lax.axis_size("col")
    pairs = [(r * cols + c, (r ^ flip_row) * cols + (c ^ flip_col)) for r in range(rows) for c in range(cols)]
    return lax.ppermute(value, ("row", "col"), pairs)


def plane_bits():
    return (lax.axis_size("row") // 2).bit_length() - 1


def col_bits():
    return lax.axis_size("col").bit_length() - 1


def plane_bit(core, step):
    return step if core == 0 else plane_bits() - 1 - step


def rank_by(index, bits):
    rank = 0
    for bit in bits:
        rank = rank * 2 + ((index >> bit) & 1)
    return rank


def plane_rank(core, pair):
    ranks = [rank_by(pair, [plane_bit(c, step) for step in range(plane_bits())]) for c in range(2)]
    return jnp.where(core == 0, ranks[0], ranks[1])


def my_plane_rank():
    my_row = lax.axis_index("row")
    return plane_rank(lax.rem(my_row, 2), my_row // 2)


def my_col_rank():
    return rank_by(lax.axis_index("col"), range(col_bits()))


def flipped(value, step):
    rows, cols = lax.axis_size("row"), lax.axis_size("col")
    pairs = [
        (r * cols + c, (r ^ (2 << plane_bit(r % 2, step))) * cols + c) for r in range(rows) for c in range(cols)
    ]
    return lax.ppermute(value, ("row", "col"), pairs)


def tables(side):
    index = np.arange(side)
    angle = (index[:, None] * index[None, :] % side) * (2.0 * math.pi / side)
    scale = 1.0 / math.sqrt(side)
    re = (np.cos(angle) * scale).astype(np.float32)
    im = (-np.sin(angle) * scale).astype(np.float32)
    blocks = []
    for first in (0, 1):
        a, b = re[first::2, :side // 2], im[first::2, :side // 2]
        blocks.append(np.block([[a, -b], [b, a]]))
    return jnp.asarray(np.stack(blocks + [block.T for block in blocks]), jnp.bfloat16)


def evens_first(amplitudes, rows):
    side = amplitudes.shape[-1]
    order = np.concatenate([np.arange(0, side, 2), np.arange(1, side, 2)])
    pick = jnp.asarray(np.eye(side)[order], jnp.float32)
    form = "ab,sbc->sac" if rows else "cb,sab->sac"
    return jnp.einsum(form, pick, amplitudes, precision=lax.Precision.HIGH)


def corner_of(row, col):
    row_base = pl.multiple_of(row // SUBLANES * SUBLANES, SUBLANES)
    col_base = pl.multiple_of(col // LANES * LANES, LANES)
    return row_base, row - row_base, col_base, col - col_base


def window_at(ref, part, row, col, side):
    row_base, down, col_base, over = corner_of(row, col)
    groups = side // SUBLANES
    lane = lax.broadcasted_iota(jnp.int32, (side, LANES), 1)
    sub = lax.broadcasted_iota(jnp.int32, (groups, SUBLANES, LANES), 1)
    turned = []
    for j in range(side // LANES + 1):
        block = ref[part, pl.ds(row_base, side + SUBLANES), pl.ds(col_base + j * LANES, LANES)]
        block = block.reshape(groups + 1, SUBLANES, LANES)
        block = pltpu.roll(block, lax.rem(SUBLANES - down, SUBLANES), 1)
        block = jnp.where(sub < SUBLANES - down, block[:groups], block[1:]).reshape(side, LANES)
        turned.append(pltpu.roll(block, lax.rem(LANES - over, LANES), 1))
    parts = [jnp.where(lane < LANES - over, turned[j], turned[j + 1]) for j in range(side // LANES)]
    return jnp.concatenate(parts, axis=1)


def add_at(ref, part, row, col, value, side):
    row_base, down, col_base, over = corner_of(row, col)
    groups = side // SUBLANES
    blocks = side // LANES
    lane = lax.broadcasted_iota(jnp.int32, (side, LANES), 1)
    sub = lax.broadcasted_iota(jnp.int32, (groups + 1, SUBLANES, LANES), 1)
    turned = [pltpu.roll(value[:, j * LANES:(j + 1) * LANES], over, 1) for j in range(blocks)]
    none = jnp.zeros((side, LANES), value.dtype)
    gap = jnp.zeros((1, SUBLANES, LANES), value.dtype)
    for j in range(blocks + 1):
        block = jnp.where(lane >= over, turned[j] if j < blocks else none, turned[j - 1] if j else none)
        block = pltpu.roll(block.reshape(groups, SUBLANES, LANES), down, 1)
        block = jnp.where(
            sub >= down, jnp.concatenate([block, gap], axis=0), jnp.concatenate([gap, block], axis=0)
        )
        place = (part, pl.ds(row_base, side + SUBLANES), pl.ds(col_base + j * LANES, LANES))
        ref[place] += block.reshape(side + SUBLANES, LANES)


def main_kernel(
    counts_ref, spots_ref, tile_hbm, below_any, right_any, corner_any, amp_hbm, probe_hbm, table_hbm,
    g_tile, g_lower, g_right, *rest
):
    chains = (len(rest) - 13) // 2
    mine_refs, other_refs = rest[:chains], rest[chains:2 * chains]
    (
        ext, gacc, stage, turned, wave, wins, sums, amp_ref, probe_ref, table_ref, in_sem, amp_sem, out_sem,
    ) = rest[2 * chains:]
    modes, side = probe_ref.shape[1], probe_ref.shape[2]
    rows, cols = tile_hbm.shape[1], tile_hbm.shape[2]
    low = side // 2
    my_row, my_col = lax.axis_index("row"), lax.axis_index("col")
    count = counts_ref[my_row, my_col]
    loads = [(probe_hbm, probe_ref), (table_hbm, table_ref)]
    for ref, r, c in ((tile_hbm, 0, 0), (below_any, rows, 0), (right_any, 0, cols), (corner_any, rows, cols)):
        loads.append((ref, ext.at[:, pl.ds(r, ref.shape[1]), pl.ds(c, ref.shape[2])]))
    loads = [pltpu.make_async_copy(a, b, in_sem.at[i]) for i, (a, b) in enumerate(loads)]

    def amp_load(p, slot):
        return pltpu.make_async_copy(amp_hbm.at[p], amp_ref.at[slot], amp_sem.at[slot])

    for load in loads:
        load.start()
    amp_load(0, 0).start()
    gacc[...] = jnp.zeros_like(gacc)
    sums[...] = jnp.zeros_like(sums)
    for load in loads:
        load.wait()

    def dot(a, b):
        return jnp.dot(a, b, preferred_element_type=jnp.float32)

    def plane(index):
        return slice(index * side, (index + 1) * side)

    def bf16(value):
        return value.astype(jnp.bfloat16)

    def step(p, carry):
        slot = lax.rem(p, 2)

        @pl.when(p + 1 < count)
        def _():
            amp_load(p + 1, 1 - slot).start()

        row, col = spots_ref[p, 0] - my_row * rows, spots_ref[p, 1] - my_col * cols
        win_re = window_at(ext, 0, row, col, side)
        win_im = window_at(ext, 1, row, col, side)
        wins[0], wins[1] = win_re, win_im
        sums[plane(2 * modes)] += win_re * win_re + win_im * win_im
        for k in range(modes):
            pr, pi = probe_ref[0, k], probe_ref[1, k]
            for i, psi in enumerate((pr * win_re - pi * win_im, pr * win_im + pi * win_re)):
                stage[0, i * low:(i + 1) * low, plane(k)] = bf16(psi[:low] + psi[low:])
                stage[1, i * low:(i + 1) * low, plane(k)] = bf16(psi[:low] - psi[low:])
        for k in range(modes):
            for parity in range(2):
                half = dot(table_ref[parity], stage[parity, :, plane(k)])
                at = k * side + parity * low
                for i in range(2):
                    left, right = half[i * low:(i + 1) * low, :low], half[i * low:(i + 1) * low, low:]
                    turned[0, at:at + low, i * low:(i + 1) * low] = bf16(left + right)
                    turned[1, at:at + low, i * low:(i + 1) * low] = bf16(left - right)
        models = [jnp.zeros((side, low), jnp.float32)] * 2
        for parity in range(2):
            for k in range(modes):
                got = dot(turned[parity, plane(k)], table_ref[2 + parity])
                wave[parity, plane(k)] = got
                models[parity] += got[:, :low] * got[:, :low] + got[:, low:] * got[:, low:]
        amp_load(p, slot).wait()
        for parity in range(2):
            model = models[parity]
            factor = amp_ref[slot, :, parity * low:(parity + 1) * low] * lax.rsqrt(jnp.maximum(model, 1.0)) - 1.0
            for k in range(modes):
                at = k * side + parity * low
                for i in range(2):
                    target = bf16(wave[parity, plane(k), i * low:(i + 1) * low] * factor)
                    stage[0, i * low:(i + 1) * low, at:at + low] = target[:low]
                    stage[1, i * low:(i + 1) * low, at:at + low] = target[low:]
        for k in range(modes):
            even = dot(table_ref[2], stage[0, :, plane(k)])
            odd = dot(table_ref[3], stage[1, :, plane(k)])
            for lower, back in enumerate((bf16(even + odd), bf16(even - odd))):
                at = k * side + lower * low
                for i in range(2):
                    for parity in range(2):
                        turned[parity, at:at + low, i * low:(i + 1) * low] = (
                            back[i * low:(i + 1) * low, parity * low:(parity + 1) * low]
                        )
        grads = [[jnp.zeros((side, low), jnp.float32)] * 2 for _ in range(2)]
        for k in range(modes):
            even = dot(turned[0, plane(k)], table_ref[0])
            odd = dot(turned[1, plane(k)], table_ref[1])
            for lower, chi in enumerate((even + odd, even - odd)):
                part = slice(lower * low, (lower + 1) * low)
                cr, ci = chi[:, :low], chi[:, low:]
                pr, pi = probe_ref[0, k, :, part], probe_ref[1, k, :, part]
                win_re, win_im = wins[0, :, part], wins[1, :, part]
                grads[lower][0] += pr * cr + pi * ci
                grads[lower][1] += pr * ci - pi * cr
                sums[plane(k), part] += win_re * cr + win_im * ci
                sums[plane(modes + k), part] += win_re * ci - win_im * cr
        for i in range(2):
            add_at(gacc, i, row, col, jnp.concatenate([grads[0][i], grads[1][i]], axis=1), side)
        return carry

    lax.fori_loop(0, count, step, 0)

    store = pltpu.make_async_copy(gacc.at[:, pl.ds(0, rows), pl.ds(0, cols)], g_tile, out_sem.at[0])
    store.start()
    core = lax.rem(my_row, 2)
    half = sums.shape[0] // 2
    for refs, at in ((other_refs, 1 - core), (mine_refs, core)):
        start = 0
        for ref in refs:
            ref[...] = sums[pl.ds(pl.multiple_of(at * half + start, SUBLANES), ref.shape[0])]
            start += ref.shape[0]
    g_lower[...] = gacc[:, rows:]
    g_right[...] = gacc[:, :rows, cols:]
    store.wait()


def light_kernel(counts_ref, spots_ref, left_ref, up_ref, diag_ref, lit_ref, light_ref, top_ref, acc):
    side = lit_ref.shape[0]
    rows, cols = light_ref.shape
    my_row, my_col = lax.axis_index("row"), lax.axis_index("col")
    acc[...] = jnp.zeros_like(acc)
    for ref, d_row, d_col in ((spots_ref, 0, 0), (left_ref, 0, 1), (up_ref, 1, 0), (diag_ref, 1, 1)):
        inside = (my_row >= d_row) & (my_col >= d_col)
        number = counts_ref[jnp.maximum(my_row - d_row, 0), jnp.maximum(my_col - d_col, 0)]

        def step(p, carry, ref=ref):
            row, col = ref[p, 0] - my_row * rows + side, ref[p, 1] - my_col * cols + side

            @pl.when((row > 0) & (col > 0))
            def _():
                add_at(acc, 0, row, col, lit_ref[...], side)

            return carry

        lax.fori_loop(0, jnp.where(inside, number, 0), step, 0)
    light = acc[0, side:side + rows, side:side + cols]
    light_ref[...] = light
    top = jnp.max(light, axis=0, keepdims=True)
    top = jnp.max(top, axis=1, keepdims=True)
    top_ref[...] = jnp.broadcast_to(top, top_ref.shape)


def fold_kernel(rank_of, below, with_top, *refs):
    held_ref, got_ref, top_ref = refs[:2] + ((refs[2],) if with_top else (None,))
    send_ref, keep_ref, out_top = refs[2 + with_top:] if with_top else refs[2:] + (None,)
    rows, half = held_ref.shape[0], keep_ref.shape[0]
    keep = (rank_of() >> below) & 1
    for ref, at in ((send_ref, 1 - keep), (keep_ref, keep)):
        part = pl.ds(pl.multiple_of(at * half, SUBLANES), half)
        ref[:half] = held_ref[part] + got_ref[part]
    if with_top:
        top = top_ref[...]
        if got_ref.shape[0] > rows:
            top = jnp.maximum(top, got_ref[rows:])
        out_top[...] = top
        send_ref[half:] = top


def fold(rank_of, below, held, got, top=None):
    rows, side = held.shape
    half = rows // 2
    with_top = top is not None
    extra = SUBLANES if with_top else 0
    return pl.pallas_call(
        functools.partial(fold_kernel, rank_of, below, with_top),
        out_shape=(f32(half + extra, side), f32(half, side)) + ((f32(*top.shape),) if with_top else ()),
        in_specs=[VM] * (2 + with_top),
        out_specs=(VM,) * (2 + with_top),
        compiler_params=params(8),
        cost_estimate=cost(10**6, 12 * rows * side),
        name="fold",
    )(held, got, *((top,) if with_top else ()))


def finish_kernel(parts, tile_ref, light_ref, top_ref, g_tile, g_left, g_up, probe_ref, *refs):
    pairs, n_col, pieces = parts
    count = 2 * pairs * len(pieces)
    block_refs = refs[:count]
    object_out, probe_out, new_object, new_probe, sums, sem = refs[count:]
    modes, side = probe_ref.shape[1], probe_ref.shape[2]
    rows, cols = light_ref.shape
    top = top_ref[0:1, 0:1]
    for at in range(0, cols, side):
        part = slice(at, at + side)
        scale = 1.0 / (light_ref[:, part] + 0.1 * top)
        for i in range(2):
            total = g_tile[i, :, part] + g_up[i, :, part]
            if at == 0:
                total += g_left[i]
            new_object[i, :, part] = tile_ref[i, :, part] + total * scale
    stores = [pltpu.make_async_copy(new_object, object_out, sem.at[0])]
    stores[0].start()

    my_row = lax.axis_index("row")
    core, pair, col_rank = lax.rem(my_row, 2), my_row // 2, my_col_rank()
    half, start = sums.shape[0] // 2, 0
    for j, piece in enumerate(pieces):
        for i in range(2 * pairs):
            ref, flip, d = block_refs[j * 2 * pairs + i], i // pairs, i % pairs
            base = (core ^ flip) * half + start + (plane_rank(core ^ flip, pair) ^ d) * (n_col * piece)
            for e in range(n_col):
                to = pl.multiple_of(base + (col_rank ^ e) * piece, SUBLANES)
                sums[pl.ds(to, piece)] = ref[e * piece:(e + 1) * piece]
        start += pairs * n_col * piece
    den = sums[2 * modes * side:(2 * modes + 1) * side]
    top = jnp.max(jnp.max(den, axis=0, keepdims=True), axis=1, keepdims=True)
    scale = 1.0 / (den + 0.1 * top)
    for i in range(2):
        for k in range(modes):
            at = (i * modes + k) * side
            new_probe[i, k] = probe_ref[i, k] + sums[at:at + side] * scale
        stores.append(pltpu.make_async_copy(new_probe.at[i], probe_out.at[i], sem.at[1 + i]))
        stores[-1].start()
    for store in stores:
        store.wait()


def f32(*shape):
    return jax.ShapeDtypeStruct(shape, jnp.float32)


VM = pl.BlockSpec(memory_space=pltpu.VMEM)
SM = pl.BlockSpec(memory_space=pltpu.SMEM)
ANY = pl.BlockSpec(memory_space=pl.ANY)
HBM = pl.BlockSpec(memory_space=pltpu.HBM)


def params(mib):
    return pltpu.CompilerParams(vmem_limit_bytes=mib * MIB)


def hbm(*shape):
    return pltpu.HBM(shape, jnp.float32)


def vmem(*shape):
    return pltpu.VMEM(shape, jnp.float32)


def in_hbm(value):
    return pltpu.with_memory_space_constraint(value, pltpu.HBM)


def cost(flops, moved):
    return pl.CostEstimate(flops=flops, bytes_accessed=moved, transcendentals=0)


def body(object_field, probe, amplitudes, corners, counts):
    rows, cols = object_field.shape[1], object_field.shape[2]
    modes, side = probe.shape[1], probe.shape[2]
    slots = amplitudes.shape[2]
    pairs, n_col = lax.axis_size("row") // 2, lax.axis_size("col")
    step = SUBLANES * 2 * pairs * n_col
    total_rows = -(-(2 * modes + 1) * side // step) * step
    piece = total_rows // (2 * pairs * n_col)
    pieces = [piece]
    spots = corners[0, 0]

    right = shifted(object_field[:, :, :side], 0, -1)
    measured = evens_first(amplitudes[0, 0], True)
    tile, measured, spots_now = lax.optimization_barrier((object_field, measured, spots))
    below = shifted(tile[:, :side, :], -1, 0)
    from_left = shifted(spots_now, 0, 1)
    measured = evens_first(measured, False)
    right, from_left, measured, modes_now = lax.optimization_barrier((right, from_left, measured, probe))
    corner = shifted(right[:, :side, :], -1, 0)
    from_up = shifted(jnp.concatenate([spots, from_left], axis=0), 1, 0)
    lit = jnp.sum(modes_now[0] * modes_now[0] + modes_now[1] * modes_now[1], axis=0)
    light, top = pl.pallas_call(
        light_kernel,
        out_shape=(f32(rows, cols), f32(SUBLANES, side)),
        in_specs=[SM] * 5 + [VM],
        out_specs=(VM, VM),
        scratch_shapes=[
            pltpu.VMEM((1, rows + 2 * side, cols + 2 * side), jnp.float32),
        ],
        compiler_params=params(12),
        cost_estimate=cost(10**8, 10**7),
        name="lighting",
    )(counts, spots, from_left, from_up[:slots], from_up[slots:], lit)
    corner, top, measured = lax.optimization_barrier((corner, top, measured))
    g_tile, g_lower, g_right, *halves = pl.pallas_call(
        main_kernel,
        out_shape=(
            hbm(2, rows, cols), vmem(2, side, cols + side), vmem(2, rows, side),
        ) + tuple(vmem(pairs * n_col * piece, side) for piece in pieces) * 2,
        in_specs=[SM] * 2 + [HBM] + [ANY] * 3 + [HBM] * 3,
        out_specs=(HBM,) + (VM,) * (2 + 2 * len(pieces)),
        scratch_shapes=[
            pltpu.VMEM((2, rows + side, cols + side), jnp.float32),
            pltpu.VMEM((2, rows + side, cols + side), jnp.float32),
            pltpu.VMEM((2, side, modes * side), jnp.bfloat16),
            pltpu.VMEM((2, modes * side, side), jnp.bfloat16),
            pltpu.VMEM((2, modes * side, side), jnp.float32),
            pltpu.VMEM((2, side, side), jnp.float32),
            pltpu.VMEM((total_rows, side), jnp.float32),
            pltpu.VMEM((2, side, side), jnp.float32),
            pltpu.VMEM(probe.shape, jnp.float32),
            pltpu.VMEM((4, side, side), jnp.bfloat16),
            pltpu.SemaphoreType.DMA((6,)),
            pltpu.SemaphoreType.DMA((2,)),
            pltpu.SemaphoreType.DMA((1,)),
        ],
        compiler_params=params(22),
        cost_estimate=cost(7 * 10**9, 2 * 10**7),
        name="positions",
    )(counts, spots, in_hbm(object_field), below, right, corner, *map(in_hbm, (measured, probe, tables(side))))

    chains = []
    for i, piece in enumerate(pieces):
        chains.append((halves[i], swapped(halves[len(pieces) + i], 1, 0), None if i else top))
    for i in range(plane_bits()):
        for j, (held, got, ride) in enumerate(chains):
            send, held = fold(my_plane_rank, plane_bits() - 1 - i, held, got)
            chains[j] = (held, flipped(send, i), ride)
    for i in range(col_bits()):
        for j, (held, got, ride) in enumerate(chains):
            send, held, *ride = fold(my_col_rank, col_bits() - 1 - i, held, got, ride)
            if i == 0 and j == 0:
                send, g_lower = lax.optimization_barrier((send, g_lower))
            chains[j] = (held, swapped(send, 0, 1 << i), ride[0] if ride else None)
    g_up = shifted(g_lower, 1, 0)
    owns = []
    for piece, (held, got, ride) in zip(pieces, chains):
        own = held + got[:piece]
        parts = [own] + [swapped(own, 0, rank_by(e, range(col_bits()))) for e in range(1, n_col)]
        if ride is not None:
            parts.append(jnp.maximum(ride, got[piece:]))
        owns.append(jnp.concatenate(parts, axis=0))
    owns[0], g_up, g_right = lax.optimization_barrier((owns[0], g_up, g_right + g_up[:, :, cols:]))
    g_left = shifted(g_right, 0, 1)
    gathered = []
    for j, own in enumerate(owns):
        blocks = [own]
        for i in reversed(range(plane_bits())):
            blocks = blocks + [flipped(block, i) for block in blocks]
        if j == len(owns) - 1:
            blocks[-1], g_left = lax.optimization_barrier((blocks[-1], g_left))
        gathered.append(blocks + [swapped(block, 1, 0) for block in blocks])
    top = functools.reduce(jnp.maximum, [block[n_col * pieces[0]:] for block in gathered[0]])
    blocks = sum(gathered, [])
    return pl.pallas_call(
        functools.partial(finish_kernel, (pairs, n_col, pieces)),
        out_shape=(f32(*object_field.shape), f32(*probe.shape)),
        in_specs=[VM] * (7 + len(blocks)),
        out_specs=(ANY, ANY),
        scratch_shapes=[
            pltpu.VMEM(object_field.shape, jnp.float32),
            pltpu.VMEM(probe.shape, jnp.float32),
            pltpu.VMEM((total_rows, side), jnp.float32),
            pltpu.SemaphoreType.DMA((3,)),
        ],
        compiler_params=params(20),
        cost_estimate=cost(10**6, 10**7),
        name="update",
    )(object_field, light, top, g_tile, g_left, g_up, probe, *blocks)


def solution(mesh):
    in_specs = (
        P(None, "row", "col"),
        P(),
        P("row", "col", None, None, None),
        P("row", "col", None, None),
        P(),
    )
    out_specs = (P(None, "row", "col"), P())
    return jax.shard_map(body, mesh=mesh, in_specs=in_specs, out_specs=out_specs, check_vma=False)
```

```python
import functools
import math

import jax
import jax.numpy as jnp
import numpy as np
from jax import lax
from jax.experimental import pallas as pl
from jax.experimental.pallas import tpu as pltpu
from jax.sharding import PartitionSpec as P

LANES = 128
SUBLANES = 8
MIB = 1024 * 1024


def shifted(value, d_row, d_col):
    rows, cols = lax.axis_size("row"), lax.axis_size("col")
    pairs = []
    for r in range(rows):
        for c in range(cols):
            if 0 <= r + d_row < rows and 0 <= c + d_col < cols:
                pairs.append((r * cols + c, (r + d_row) * cols + c + d_col))
    return lax.ppermute(value, ("row", "col"), pairs)


def swapped(value, flip_row, flip_col):
    rows, cols = lax.axis_size("row"), lax.axis_size("col")
    pairs = [(r * cols + c, (r ^ flip_row) * cols + (c ^ flip_col)) for r in range(rows) for c in range(cols)]
    return lax.ppermute(value, ("row", "col"), pairs)


def plane_bits():
    return (lax.axis_size("row") // 2).bit_length() - 1


def col_bits():
    return lax.axis_size("col").bit_length() - 1


def plane_bit(core, step):
    return step if core == 0 else plane_bits() - 1 - step


def rank_by(index, bits):
    rank = 0
    for bit in bits:
        rank = rank * 2 + ((index >> bit) & 1)
    return rank


def plane_rank(core, pair):
    ranks = [rank_by(pair, [plane_bit(c, step) for step in range(plane_bits())]) for c in range(2)]
    return jnp.where(core == 0, ranks[0], ranks[1])


def my_plane_rank():
    my_row = lax.axis_index("row")
    return plane_rank(lax.rem(my_row, 2), my_row // 2)


def my_col_rank():
    return rank_by(lax.axis_index("col"), range(col_bits()))


def flipped(value, step):
    rows, cols = lax.axis_size("row"), lax.axis_size("col")
    pairs = [
        (r * cols + c, (r ^ (2 << plane_bit(r % 2, step))) * cols + c) for r in range(rows) for c in range(cols)
    ]
    return lax.ppermute(value, ("row", "col"), pairs)


def tables(side):
    index = np.arange(side)
    angle = (index[:, None] * index[None, :] % side) * (2.0 * math.pi / side)
    scale = 1.0 / math.sqrt(side)
    re = (np.cos(angle) * scale).astype(np.float32)
    im = (-np.sin(angle) * scale).astype(np.float32)
    blocks = []
    for first in (0, 1):
        a, b = re[first::2, :side // 2], im[first::2, :side // 2]
        blocks.append(np.block([[a, -b], [b, a]]))
    return jnp.asarray(np.stack(blocks + [block.T for block in blocks]), jnp.bfloat16)


def reorder_kernel(amp_ref, pick_ref, out_ref):
    def split(value):
        high = value.astype(jnp.bfloat16)
        return high, (value - high.astype(jnp.float32)).astype(jnp.bfloat16)

    def dot(a, b):
        return jnp.dot(a, b, preferred_element_type=jnp.float32)

    rows = sum(dot(pick_ref[0], part) for part in split(amp_ref[0]))
    out_ref[0] = sum(dot(part, pick_ref[1]) for part in split(rows))


def evens_first(amplitudes):
    slots, side, _ = amplitudes.shape
    order = np.concatenate([np.arange(0, side, 2), np.arange(1, side, 2)])
    pick = np.eye(side)[order]
    spec = pl.BlockSpec((1, side, side), lambda p: (p, 0, 0))
    return pl.pallas_call(
        reorder_kernel,
        grid=(slots,),
        out_shape=f32(slots, side, side),
        in_specs=[spec, pl.BlockSpec((2, side, side), lambda p: (0, 0, 0))],
        out_specs=spec,
        compiler_params=params(8),
        cost_estimate=cost(slots * 8 * side**3, 8 * slots * side * side),
        name="reorder",
    )(amplitudes, jnp.asarray(np.stack([pick, pick.T]), jnp.bfloat16))


def corner_of(row, col):
    row_base = pl.multiple_of(row // SUBLANES * SUBLANES, SUBLANES)
    col_base = pl.multiple_of(col // LANES * LANES, LANES)
    return row_base, row - row_base, col_base, col - col_base


def window_at(ref, part, row, col, side):
    row_base, down, col_base, over = corner_of(row, col)
    groups = side // SUBLANES
    lane = lax.broadcasted_iota(jnp.int32, (side, LANES), 1)
    sub = lax.broadcasted_iota(jnp.int32, (groups, SUBLANES, LANES), 1)
    turned = []
    for j in range(side // LANES + 1):
        block = ref[part, pl.ds(row_base, side + SUBLANES), pl.ds(col_base + j * LANES, LANES)]
        block = block.reshape(groups + 1, SUBLANES, LANES)
        block = pltpu.roll(block, lax.rem(SUBLANES - down, SUBLANES), 1)
        block = jnp.where(sub < SUBLANES - down, block[:groups], block[1:]).reshape(side, LANES)
        turned.append(pltpu.roll(block, lax.rem(LANES - over, LANES), 1))
    parts = [jnp.where(lane < LANES - over, turned[j], turned[j + 1]) for j in range(side // LANES)]
    return jnp.concatenate(parts, axis=1)


def add_at(ref, part, row, col, value, side):
    row_base, down, col_base, over = corner_of(row, col)
    groups = side // SUBLANES
    blocks = side // LANES
    lane = lax.broadcasted_iota(jnp.int32, (side, LANES), 1)
    sub = lax.broadcasted_iota(jnp.int32, (groups + 1, SUBLANES, LANES), 1)
    turned = [pltpu.roll(value[:, j * LANES:(j + 1) * LANES], over, 1) for j in range(blocks)]
    none = jnp.zeros((side, LANES), value.dtype)
    gap = jnp.zeros((1, SUBLANES, LANES), value.dtype)
    for j in range(blocks + 1):
        block = jnp.where(lane >= over, turned[j] if j < blocks else none, turned[j - 1] if j else none)
        block = pltpu.roll(block.reshape(groups, SUBLANES, LANES), down, 1)
        block = jnp.where(
            sub >= down, jnp.concatenate([block, gap], axis=0), jnp.concatenate([gap, block], axis=0)
        )
        place = (part, pl.ds(row_base, side + SUBLANES), pl.ds(col_base + j * LANES, LANES))
        ref[place] += block.reshape(side + SUBLANES, LANES)


def main_kernel(
    counts_ref, spots_ref, tile_hbm, below_any, right_any, corner_any, amp_hbm, probe_hbm, table_hbm,
    g_tile, g_lower, g_right, *rest
):
    chains = (len(rest) - 13) // 2
    mine_refs, other_refs = rest[:chains], rest[chains:2 * chains]
    (
        ext, gacc, stage, turned, wave, wins, sums, amp_ref, probe_ref, table_ref, in_sem, amp_sem, out_sem,
    ) = rest[2 * chains:]
    modes, side = probe_ref.shape[1], probe_ref.shape[2]
    rows, cols = tile_hbm.shape[1], tile_hbm.shape[2]
    low = side // 2
    my_row, my_col = lax.axis_index("row"), lax.axis_index("col")
    count = counts_ref[my_row, my_col]
    loads = [(probe_hbm, probe_ref), (table_hbm, table_ref)]
    for ref, r, c in ((tile_hbm, 0, 0), (below_any, rows, 0), (right_any, 0, cols), (corner_any, rows, cols)):
        loads.append((ref, ext.at[:, pl.ds(r, ref.shape[1]), pl.ds(c, ref.shape[2])]))
    loads = [pltpu.make_async_copy(a, b, in_sem.at[i]) for i, (a, b) in enumerate(loads)]

    def amp_load(p, slot):
        return pltpu.make_async_copy(amp_hbm.at[p], amp_ref.at[slot], amp_sem.at[slot])

    for load in loads:
        load.start()
    amp_load(0, 0).start()
    gacc[...] = jnp.zeros_like(gacc)
    sums[...] = jnp.zeros_like(sums)
    for load in loads:
        load.wait()

    def dot(a, b):
        return jnp.dot(a, b, preferred_element_type=jnp.float32)

    def plane(index):
        return slice(index * side, (index + 1) * side)

    def bf16(value):
        return value.astype(jnp.bfloat16)

    def step(p, carry):
        slot = lax.rem(p, 2)

        @pl.when(p + 1 < count)
        def _():
            amp_load(p + 1, 1 - slot).start()

        row, col = spots_ref[p, 0] - my_row * rows, spots_ref[p, 1] - my_col * cols
        win_re = window_at(ext, 0, row, col, side)
        win_im = window_at(ext, 1, row, col, side)
        wins[0], wins[1] = win_re, win_im
        sums[plane(2 * modes)] += win_re * win_re + win_im * win_im
        for k in range(modes):
            pr, pi = probe_ref[0, k], probe_ref[1, k]
            for i, psi in enumerate((pr * win_re - pi * win_im, pr * win_im + pi * win_re)):
                stage[0, i * low:(i + 1) * low, plane(k)] = bf16(psi[:low] + psi[low:])
                stage[1, i * low:(i + 1) * low, plane(k)] = bf16(psi[:low] - psi[low:])
        for k in range(modes):
            for parity in range(2):
                half = dot(table_ref[parity], stage[parity, :, plane(k)])
                at = k * side + parity * low
                for i in range(2):
                    left, right = half[i * low:(i + 1) * low, :low], half[i * low:(i + 1) * low, low:]
                    turned[0, at:at + low, i * low:(i + 1) * low] = bf16(left + right)
                    turned[1, at:at + low, i * low:(i + 1) * low] = bf16(left - right)
        models = [jnp.zeros((side, low), jnp.float32)] * 2
        for parity in range(2):
            for k in range(modes):
                got = dot(turned[parity, plane(k)], table_ref[2 + parity])
                wave[parity, plane(k)] = got
                models[parity] += got[:, :low] * got[:, :low] + got[:, low:] * got[:, low:]
        amp_load(p, slot).wait()
        for parity in range(2):
            model = models[parity]
            factor = amp_ref[slot, :, parity * low:(parity + 1) * low] * lax.rsqrt(jnp.maximum(model, 1.0)) - 1.0
            for k in range(modes):
                at = k * side + parity * low
                for i in range(2):
                    target = bf16(wave[parity, plane(k), i * low:(i + 1) * low] * factor)
                    stage[0, i * low:(i + 1) * low, at:at + low] = target[:low]
                    stage[1, i * low:(i + 1) * low, at:at + low] = target[low:]
        for k in range(modes):
            even = dot(table_ref[2], stage[0, :, plane(k)])
            odd = dot(table_ref[3], stage[1, :, plane(k)])
            for lower, back in enumerate((bf16(even + odd), bf16(even - odd))):
                at = k * side + lower * low
                for i in range(2):
                    for parity in range(2):
                        turned[parity, at:at + low, i * low:(i + 1) * low] = (
                            back[i * low:(i + 1) * low, parity * low:(parity + 1) * low]
                        )
        grads = [[jnp.zeros((side, low), jnp.float32)] * 2 for _ in range(2)]
        for k in range(modes):
            even = dot(turned[0, plane(k)], table_ref[0])
            odd = dot(turned[1, plane(k)], table_ref[1])
            for lower, chi in enumerate((even + odd, even - odd)):
                part = slice(lower * low, (lower + 1) * low)
                cr, ci = chi[:, :low], chi[:, low:]
                pr, pi = probe_ref[0, k, :, part], probe_ref[1, k, :, part]
                win_re, win_im = wins[0, :, part], wins[1, :, part]
                grads[lower][0] += pr * cr + pi * ci
                grads[lower][1] += pr * ci - pi * cr
                sums[plane(k), part] += win_re * cr + win_im * ci
                sums[plane(modes + k), part] += win_re * ci - win_im * cr
        for i in range(2):
            add_at(gacc, i, row, col, jnp.concatenate([grads[0][i], grads[1][i]], axis=1), side)
        return carry

    lax.fori_loop(0, count, step, 0)

    store = pltpu.make_async_copy(gacc.at[:, pl.ds(0, rows), pl.ds(0, cols)], g_tile, out_sem.at[0])
    store.start()
    core = lax.rem(my_row, 2)
    half = sums.shape[0] // 2
    for refs, at in ((other_refs, 1 - core), (mine_refs, core)):
        start = 0
        for ref in refs:
            ref[...] = sums[pl.ds(pl.multiple_of(at * half + start, SUBLANES), ref.shape[0])]
            start += ref.shape[0]
    g_lower[...] = gacc[:, rows:]
    g_right[...] = gacc[:, :rows, cols:]
    store.wait()


def light_kernel(counts_ref, spots_ref, left_ref, up_ref, diag_ref, lit_ref, light_ref, top_ref, acc):
    side = lit_ref.shape[0]
    rows, cols = light_ref.shape
    my_row, my_col = lax.axis_index("row"), lax.axis_index("col")
    acc[...] = jnp.zeros_like(acc)
    for ref, d_row, d_col in ((spots_ref, 0, 0), (left_ref, 0, 1), (up_ref, 1, 0), (diag_ref, 1, 1)):
        inside = (my_row >= d_row) & (my_col >= d_col)
        number = counts_ref[jnp.maximum(my_row - d_row, 0), jnp.maximum(my_col - d_col, 0)]

        def step(p, carry, ref=ref):
            row, col = ref[p, 0] - my_row * rows + side, ref[p, 1] - my_col * cols + side

            @pl.when((row > 0) & (col > 0))
            def _():
                add_at(acc, 0, row, col, lit_ref[...], side)

            return carry

        lax.fori_loop(0, jnp.where(inside, number, 0), step, 0)
    light = acc[0, side:side + rows, side:side + cols]
    light_ref[...] = light
    top = jnp.max(light, axis=0, keepdims=True)
    top = jnp.max(top, axis=1, keepdims=True)
    top_ref[...] = jnp.broadcast_to(top, top_ref.shape)


def fold_kernel(rank_of, below, with_top, *refs):
    held_ref, got_ref, top_ref = refs[:2] + ((refs[2],) if with_top else (None,))
    send_ref, keep_ref, out_top = refs[2 + with_top:] if with_top else refs[2:] + (None,)
    rows, half = held_ref.shape[0], keep_ref.shape[0]
    keep = (rank_of() >> below) & 1
    for ref, at in ((send_ref, 1 - keep), (keep_ref, keep)):
        part = pl.ds(pl.multiple_of(at * half, SUBLANES), half)
        ref[:half] = held_ref[part] + got_ref[part]
    if with_top:
        top = top_ref[...]
        if got_ref.shape[0] > rows:
            top = jnp.maximum(top, got_ref[rows:])
        out_top[...] = top
        send_ref[half:] = top


def fold(rank_of, below, held, got, top=None):
    rows, side = held.shape
    half = rows // 2
    with_top = top is not None
    extra = SUBLANES if with_top else 0
    return pl.pallas_call(
        functools.partial(fold_kernel, rank_of, below, with_top),
        out_shape=(f32(half + extra, side), f32(half, side)) + ((f32(*top.shape),) if with_top else ()),
        in_specs=[VM] * (2 + with_top),
        out_specs=(VM,) * (2 + with_top),
        compiler_params=params(8),
        cost_estimate=cost(10**6, 12 * rows * side),
        name="fold",
    )(held, got, *((top,) if with_top else ()))


def finish_kernel(parts, tile_ref, light_ref, top_ref, g_tile, g_left, g_up, probe_ref, *refs):
    pairs, n_col, pieces = parts
    count = 2 * pairs * len(pieces)
    block_refs = refs[:count]
    object_out, probe_out, new_object, new_probe, sums, sem = refs[count:]
    modes, side = probe_ref.shape[1], probe_ref.shape[2]
    rows, cols = light_ref.shape
    top = top_ref[0:1, 0:1]
    for at in range(0, cols, side):
        part = slice(at, at + side)
        scale = 1.0 / (light_ref[:, part] + 0.1 * top)
        for i in range(2):
            total = g_tile[i, :, part] + g_up[i, :, part]
            if at == 0:
                total += g_left[i]
            new_object[i, :, part] = tile_ref[i, :, part] + total * scale
    stores = [pltpu.make_async_copy(new_object, object_out, sem.at[0])]
    stores[0].start()

    my_row = lax.axis_index("row")
    core, pair, col_rank = lax.rem(my_row, 2), my_row // 2, my_col_rank()
    half, start = sums.shape[0] // 2, 0
    for j, piece in enumerate(pieces):
        for i in range(2 * pairs):
            ref, flip, d = block_refs[j * 2 * pairs + i], i // pairs, i % pairs
            base = (core ^ flip) * half + start + (plane_rank(core ^ flip, pair) ^ d) * (n_col * piece)
            for e in range(n_col):
                to = pl.multiple_of(base + (col_rank ^ e) * piece, SUBLANES)
                sums[pl.ds(to, piece)] = ref[e * piece:(e + 1) * piece]
        start += pairs * n_col * piece
    den = sums[2 * modes * side:(2 * modes + 1) * side]
    top = jnp.max(jnp.max(den, axis=0, keepdims=True), axis=1, keepdims=True)
    scale = 1.0 / (den + 0.1 * top)
    for i in range(2):
        for k in range(modes):
            at = (i * modes + k) * side
            new_probe[i, k] = probe_ref[i, k] + sums[at:at + side] * scale
        stores.append(pltpu.make_async_copy(new_probe.at[i], probe_out.at[i], sem.at[1 + i]))
        stores[-1].start()
    for store in stores:
        store.wait()


def f32(*shape):
    return jax.ShapeDtypeStruct(shape, jnp.float32)


VM = pl.BlockSpec(memory_space=pltpu.VMEM)
SM = pl.BlockSpec(memory_space=pltpu.SMEM)
ANY = pl.BlockSpec(memory_space=pl.ANY)
HBM = pl.BlockSpec(memory_space=pltpu.HBM)


def params(mib):
    return pltpu.CompilerParams(vmem_limit_bytes=mib * MIB)


def hbm(*shape):
    return pltpu.HBM(shape, jnp.float32)


def vmem(*shape):
    return pltpu.VMEM(shape, jnp.float32)


def in_hbm(value):
    return pltpu.with_memory_space_constraint(value, pltpu.HBM)


def cost(flops, moved):
    return pl.CostEstimate(flops=flops, bytes_accessed=moved, transcendentals=0)


def body(object_field, probe, amplitudes, corners, counts):
    rows, cols = object_field.shape[1], object_field.shape[2]
    modes, side = probe.shape[1], probe.shape[2]
    slots = amplitudes.shape[2]
    pairs, n_col = lax.axis_size("row") // 2, lax.axis_size("col")
    step = SUBLANES * 2 * pairs * n_col
    total_rows = -(-(2 * modes + 1) * side // step) * step
    piece = total_rows // (2 * pairs * n_col)
    pieces = [piece]
    spots = corners[0, 0]

    right = shifted(object_field[:, :, :side], 0, -1)
    measured = evens_first(amplitudes[0, 0])
    tile, measured, spots_now = lax.optimization_barrier((object_field, measured, spots))
    below = shifted(tile[:, :side, :], -1, 0)
    from_left = shifted(spots_now, 0, 1)
    from_up = shifted(jnp.concatenate([spots_now, from_left], axis=0), 1, 0)
    right, from_up, measured, modes_now = lax.optimization_barrier((right, from_up, measured, probe))
    corner = shifted(right[:, :side, :], -1, 0)
    lit = jnp.sum(modes_now[0] * modes_now[0] + modes_now[1] * modes_now[1], axis=0)
    light, top = pl.pallas_call(
        light_kernel,
        out_shape=(f32(rows, cols), f32(SUBLANES, side)),
        in_specs=[SM] * 5 + [VM],
        out_specs=(VM, VM),
        scratch_shapes=[
            pltpu.VMEM((1, rows + 2 * side, cols + 2 * side), jnp.float32),
        ],
        compiler_params=params(12),
        cost_estimate=cost(10**8, 10**7),
        name="lighting",
    )(counts, spots, from_left, from_up[:slots], from_up[slots:], lit)
    corner, top, measured = lax.optimization_barrier((corner, top, measured))
    g_tile, g_lower, g_right, *halves = pl.pallas_call(
        main_kernel,
        out_shape=(
            hbm(2, rows, cols), vmem(2, side, cols + side), vmem(2, rows, side),
        ) + tuple(vmem(pairs * n_col * piece, side) for piece in pieces) * 2,
        in_specs=[SM] * 2 + [HBM] + [ANY] * 3 + [HBM] * 3,
        out_specs=(HBM,) + (VM,) * (2 + 2 * len(pieces)),
        scratch_shapes=[
            pltpu.VMEM((2, rows + side, cols + side), jnp.float32),
            pltpu.VMEM((2, rows + side, cols + side), jnp.float32),
            pltpu.VMEM((2, side, modes * side), jnp.bfloat16),
            pltpu.VMEM((2, modes * side, side), jnp.bfloat16),
            pltpu.VMEM((2, modes * side, side), jnp.float32),
            pltpu.VMEM((2, side, side), jnp.float32),
            pltpu.VMEM((total_rows, side), jnp.float32),
            pltpu.VMEM((2, side, side), jnp.float32),
            pltpu.VMEM(probe.shape, jnp.float32),
            pltpu.VMEM((4, side, side), jnp.bfloat16),
            pltpu.SemaphoreType.DMA((6,)),
            pltpu.SemaphoreType.DMA((2,)),
            pltpu.SemaphoreType.DMA((1,)),
        ],
        compiler_params=params(22),
        cost_estimate=cost(7 * 10**9, 2 * 10**7),
        name="positions",
    )(counts, spots, in_hbm(object_field), below, right, corner, *map(in_hbm, (measured, probe, tables(side))))

    chains = []
    for i, piece in enumerate(pieces):
        chains.append((halves[i], swapped(halves[len(pieces) + i], 1, 0), None if i else top))
    for i in range(plane_bits()):
        for j, (held, got, ride) in enumerate(chains):
            send, held = fold(my_plane_rank, plane_bits() - 1 - i, held, got)
            chains[j] = (held, flipped(send, i), ride)
    for i in range(col_bits()):
        for j, (held, got, ride) in enumerate(chains):
            send, held, *ride = fold(my_col_rank, col_bits() - 1 - i, held, got, ride)
            if i == 0 and j == 0:
                send, g_lower = lax.optimization_barrier((send, g_lower))
            chains[j] = (held, swapped(send, 0, 1 << i), ride[0] if ride else None)
    g_up = shifted(g_lower, 1, 0)
    owns = []
    for piece, (held, got, ride) in zip(pieces, chains):
        own = held + got[:piece]
        parts = [own] + [swapped(own, 0, rank_by(e, range(col_bits()))) for e in range(1, n_col)]
        if ride is not None:
            parts.append(jnp.maximum(ride, got[piece:]))
        owns.append(jnp.concatenate(parts, axis=0))
    owns[0], g_up, g_right = lax.optimization_barrier((owns[0], g_up, g_right + g_up[:, :, cols:]))
    g_left = shifted(g_right, 0, 1)
    gathered = []
    for j, own in enumerate(owns):
        blocks = [own]
        for i in reversed(range(plane_bits())):
            blocks = blocks + [flipped(block, i) for block in blocks]
        if j == len(owns) - 1:
            blocks[-1], g_left = lax.optimization_barrier((blocks[-1], g_left))
        gathered.append(blocks + [swapped(block, 1, 0) for block in blocks])
    top = functools.reduce(jnp.maximum, [block[n_col * pieces[0]:] for block in gathered[0]])
    blocks = sum(gathered, [])
    return pl.pallas_call(
        functools.partial(finish_kernel, (pairs, n_col, pieces)),
        out_shape=(f32(*object_field.shape), f32(*probe.shape)),
        in_specs=[VM] * (7 + len(blocks)),
        out_specs=(ANY, ANY),
        scratch_shapes=[
            pltpu.VMEM(object_field.shape, jnp.float32),
            pltpu.VMEM(probe.shape, jnp.float32),
            pltpu.VMEM((total_rows, side), jnp.float32),
            pltpu.SemaphoreType.DMA((3,)),
        ],
        compiler_params=params(20),
        cost_estimate=cost(10**6, 10**7),
        name="update",
    )(object_field, light, top, g_tile, g_left, g_up, probe, *blocks)


def solution(mesh):
    in_specs = (
        P(None, "row", "col"),
        P(),
        P("row", "col", None, None, None),
        P("row", "col", None, None),
        P(),
    )
    out_specs = (P(None, "row", "col"), P())
    return jax.shard_map(body, mesh=mesh, in_specs=in_specs, out_specs=out_specs, check_vma=False)
```

```python
import functools
import math

import jax
import jax.numpy as jnp
import numpy as np
from jax import lax
from jax.experimental import pallas as pl
from jax.experimental.pallas import tpu as pltpu
from jax.sharding import PartitionSpec as P

LANES = 128
SUBLANES = 8
MIB = 1024 * 1024


def shifted(value, d_row, d_col):
    rows, cols = lax.axis_size("row"), lax.axis_size("col")
    pairs = []
    for r in range(rows):
        for c in range(cols):
            if 0 <= r + d_row < rows and 0 <= c + d_col < cols:
                pairs.append((r * cols + c, (r + d_row) * cols + c + d_col))
    return lax.ppermute(value, ("row", "col"), pairs)


def swapped(value, flip_row, flip_col):
    rows, cols = lax.axis_size("row"), lax.axis_size("col")
    pairs = [(r * cols + c, (r ^ flip_row) * cols + (c ^ flip_col)) for r in range(rows) for c in range(cols)]
    return lax.ppermute(value, ("row", "col"), pairs)


def plane_bits():
    return (lax.axis_size("row") // 2).bit_length() - 1


def col_bits():
    return lax.axis_size("col").bit_length() - 1


def plane_bit(core, step):
    return step if core == 0 else plane_bits() - 1 - step


def rank_by(index, bits):
    rank = 0
    for bit in bits:
        rank = rank * 2 + ((index >> bit) & 1)
    return rank


def plane_rank(core, pair):
    ranks = [rank_by(pair, [plane_bit(c, step) for step in range(plane_bits())]) for c in range(2)]
    return jnp.where(core == 0, ranks[0], ranks[1])


def my_plane_rank():
    my_row = lax.axis_index("row")
    return plane_rank(lax.rem(my_row, 2), my_row // 2)


def my_col_rank():
    return rank_by(lax.axis_index("col"), range(col_bits()))


def flipped(value, step):
    rows, cols = lax.axis_size("row"), lax.axis_size("col")
    pairs = [
        (r * cols + c, (r ^ (2 << plane_bit(r % 2, step))) * cols + c) for r in range(rows) for c in range(cols)
    ]
    return lax.ppermute(value, ("row", "col"), pairs)


def tables(side):
    index = np.arange(side)
    angle = (index[:, None] * index[None, :] % side) * (2.0 * math.pi / side)
    scale = 1.0 / math.sqrt(side)
    re = (np.cos(angle) * scale).astype(np.float32)
    im = (-np.sin(angle) * scale).astype(np.float32)
    blocks = []
    for first in (0, 1):
        a, b = re[first::2, :side // 2], im[first::2, :side // 2]
        blocks.append(np.block([[a, -b], [b, a]]))
    return jnp.asarray(np.stack(blocks + [block.T for block in blocks]), jnp.bfloat16)


def evens_first(amplitudes, rows):
    side = amplitudes.shape[-1]
    order = np.concatenate([np.arange(0, side, 2), np.arange(1, side, 2)])
    pick = jnp.asarray(np.eye(side)[order], jnp.float32)
    form = "ab,sbc->sac" if rows else "cb,sab->sac"
    return jnp.einsum(form, pick, amplitudes, precision=lax.Precision.HIGH)


def corner_of(row, col):
    row_base = pl.multiple_of(row // SUBLANES * SUBLANES, SUBLANES)
    col_base = pl.multiple_of(col // LANES * LANES, LANES)
    return row_base, row - row_base, col_base, col - col_base


def window_at(ref, part, row, col, side):
    row_base, down, col_base, over = corner_of(row, col)
    groups = side // SUBLANES
    lane = lax.broadcasted_iota(jnp.int32, (side, LANES), 1)
    sub = lax.broadcasted_iota(jnp.int32, (groups, SUBLANES, LANES), 1)
    turned = []
    for j in range(side // LANES + 1):
        block = ref[part, pl.ds(row_base, side + SUBLANES), pl.ds(col_base + j * LANES, LANES)]
        block = block.reshape(groups + 1, SUBLANES, LANES)
        block = pltpu.roll(block, lax.rem(SUBLANES - down, SUBLANES), 1)
        block = jnp.where(sub < SUBLANES - down, block[:groups], block[1:]).reshape(side, LANES)
        turned.append(pltpu.roll(block, lax.rem(LANES - over, LANES), 1))
    parts = [jnp.where(lane < LANES - over, turned[j], turned[j + 1]) for j in range(side // LANES)]
    return jnp.concatenate(parts, axis=1)


def add_at(ref, part, row, col, value, side):
    row_base, down, col_base, over = corner_of(row, col)
    groups = side // SUBLANES
    blocks = side // LANES
    lane = lax.broadcasted_iota(jnp.int32, (side, LANES), 1)
    sub = lax.broadcasted_iota(jnp.int32, (groups + 1, SUBLANES, LANES), 1)
    turned = [pltpu.roll(value[:, j * LANES:(j + 1) * LANES], over, 1) for j in range(blocks)]
    none = jnp.zeros((side, LANES), value.dtype)
    gap = jnp.zeros((1, SUBLANES, LANES), value.dtype)
    for j in range(blocks + 1):
        block = jnp.where(lane >= over, turned[j] if j < blocks else none, turned[j - 1] if j else none)
        block = pltpu.roll(block.reshape(groups, SUBLANES, LANES), down, 1)
        block = jnp.where(
            sub >= down, jnp.concatenate([block, gap], axis=0), jnp.concatenate([gap, block], axis=0)
        )
        place = (part, pl.ds(row_base, side + SUBLANES), pl.ds(col_base + j * LANES, LANES))
        ref[place] += block.reshape(side + SUBLANES, LANES)


def main_kernel(
    counts_ref, spots_ref, tile_hbm, below_any, right_any, corner_any, amp_hbm, probe_hbm, table_hbm,
    g_tile, g_lower, g_right, *rest
):
    chains = (len(rest) - 13) // 2
    mine_refs, other_refs = rest[:chains], rest[chains:2 * chains]
    (
        ext, gacc, stage, turned, wave, wins, sums, amp_ref, probe_ref, table_ref, in_sem, amp_sem, out_sem,
    ) = rest[2 * chains:]
    modes, side = probe_ref.shape[1], probe_ref.shape[2]
    rows, cols = tile_hbm.shape[1], tile_hbm.shape[2]
    low = side // 2
    my_row, my_col = lax.axis_index("row"), lax.axis_index("col")
    count = counts_ref[my_row, my_col]
    loads = [(probe_hbm, probe_ref), (table_hbm, table_ref)]
    for ref, r, c in ((tile_hbm, 0, 0), (below_any, rows, 0), (right_any, 0, cols), (corner_any, rows, cols)):
        loads.append((ref, ext.at[:, pl.ds(r, ref.shape[1]), pl.ds(c, ref.shape[2])]))
    loads = [pltpu.make_async_copy(a, b, in_sem.at[i]) for i, (a, b) in enumerate(loads)]

    def amp_load(p, slot):
        return pltpu.make_async_copy(amp_hbm.at[p], amp_ref.at[slot], amp_sem.at[slot])

    for load in loads:
        load.start()
    amp_load(0, 0).start()
    gacc[...] = jnp.zeros_like(gacc)
    sums[...] = jnp.zeros_like(sums)
    for load in loads:
        load.wait()

    def dot(a, b):
        return jnp.dot(a, b, preferred_element_type=jnp.float32)

    def plane(index):
        return slice(index * side, (index + 1) * side)

    def bf16(value):
        return value.astype(jnp.bfloat16)

    def step(p, carry):
        slot = lax.rem(p, 2)

        @pl.when(p + 1 < count)
        def _():
            amp_load(p + 1, 1 - slot).start()

        row, col = spots_ref[p, 0] - my_row * rows, spots_ref[p, 1] - my_col * cols
        win_re = window_at(ext, 0, row, col, side)
        win_im = window_at(ext, 1, row, col, side)
        wins[0], wins[1] = win_re, win_im
        sums[plane(2 * modes)] += win_re * win_re + win_im * win_im
        for k in range(modes):
            pr, pi = probe_ref[0, k], probe_ref[1, k]
            for i, psi in enumerate((pr * win_re - pi * win_im, pr * win_im + pi * win_re)):
                stage[0, i * low:(i + 1) * low, plane(k)] = bf16(psi[:low] + psi[low:])
                stage[1, i * low:(i + 1) * low, plane(k)] = bf16(psi[:low] - psi[low:])
        for k in range(modes):
            for parity in range(2):
                half = dot(table_ref[parity], stage[parity, :, plane(k)])
                at = k * side + parity * low
                for i in range(2):
                    left, right = half[i * low:(i + 1) * low, :low], half[i * low:(i + 1) * low, low:]
                    turned[0, at:at + low, i * low:(i + 1) * low] = bf16(left + right)
                    turned[1, at:at + low, i * low:(i + 1) * low] = bf16(left - right)
        models = [jnp.zeros((side, low), jnp.float32)] * 2
        for parity in range(2):
            for k in range(modes):
                got = dot(turned[parity, plane(k)], table_ref[2 + parity])
                wave[parity, plane(k)] = got
                models[parity] += got[:, :low] * got[:, :low] + got[:, low:] * got[:, low:]
        amp_load(p, slot).wait()
        for parity in range(2):
            model = models[parity]
            factor = amp_ref[slot, :, parity * low:(parity + 1) * low] * lax.rsqrt(jnp.maximum(model, 1.0)) - 1.0
            for k in range(modes):
                at = k * side + parity * low
                for i in range(2):
                    target = bf16(wave[parity, plane(k), i * low:(i + 1) * low] * factor)
                    stage[0, i * low:(i + 1) * low, at:at + low] = target[:low]
                    stage[1, i * low:(i + 1) * low, at:at + low] = target[low:]
        for k in range(modes):
            even = dot(table_ref[2], stage[0, :, plane(k)])
            odd = dot(table_ref[3], stage[1, :, plane(k)])
            for lower, back in enumerate((bf16(even + odd), bf16(even - odd))):
                at = k * side + lower * low
                for i in range(2):
                    for parity in range(2):
                        turned[parity, at:at + low, i * low:(i + 1) * low] = (
                            back[i * low:(i + 1) * low, parity * low:(parity + 1) * low]
                        )
        grads = [[jnp.zeros((side, low), jnp.float32)] * 2 for _ in range(2)]
        for k in range(modes):
            even = dot(turned[0, plane(k)], table_ref[0])
            odd = dot(turned[1, plane(k)], table_ref[1])
            for lower, chi in enumerate((even + odd, even - odd)):
                part = slice(lower * low, (lower + 1) * low)
                cr, ci = chi[:, :low], chi[:, low:]
                pr, pi = probe_ref[0, k, :, part], probe_ref[1, k, :, part]
                win_re, win_im = wins[0, :, part], wins[1, :, part]
                grads[lower][0] += pr * cr + pi * ci
                grads[lower][1] += pr * ci - pi * cr
                sums[plane(k), part] += win_re * cr + win_im * ci
                sums[plane(modes + k), part] += win_re * ci - win_im * cr
        for i in range(2):
            add_at(gacc, i, row, col, jnp.concatenate([grads[0][i], grads[1][i]], axis=1), side)
        return carry

    lax.fori_loop(0, count, step, 0)

    store = pltpu.make_async_copy(gacc.at[:, pl.ds(0, rows), pl.ds(0, cols)], g_tile, out_sem.at[0])
    store.start()
    core = lax.rem(my_row, 2)
    half = sums.shape[0] // 2
    for refs, at in ((other_refs, 1 - core), (mine_refs, core)):
        start = 0
        for ref in refs:
            ref[...] = sums[pl.ds(pl.multiple_of(at * half + start, SUBLANES), ref.shape[0])]
            start += ref.shape[0]
    g_lower[...] = gacc[:, rows:]
    g_right[...] = gacc[:, :rows, cols:]
    store.wait()


def light_kernel(sides, last, counts_ref, *refs):
    spot_refs, (lit_ref, *rest) = refs[:len(sides)], refs[len(sides):]
    light_ref, acc = rest[1 if last else 0], rest[-1]
    side = lit_ref.shape[0]
    rows, cols = light_ref.shape
    my_row, my_col = lax.axis_index("row"), lax.axis_index("col")
    acc[...] = jnp.zeros_like(acc)
    for ref, (d_row, d_col) in zip(spot_refs, sides):
        inside = (my_row >= d_row) & (my_col >= d_col)
        number = counts_ref[jnp.maximum(my_row - d_row, 0), jnp.maximum(my_col - d_col, 0)]

        def step(p, carry, ref=ref):
            row, col = ref[p, 0] - my_row * rows + side, ref[p, 1] - my_col * cols + side

            @pl.when((row > 0) & (col > 0))
            def _():
                add_at(acc, 0, row, col, lit_ref[...], side)

            return carry

        lax.fori_loop(0, jnp.where(inside, number, 0), step, 0)
    light = acc[0, side:side + rows, side:side + cols]
    if last:
        light += rest[0][...]
        top_ref = rest[2]
        top = jnp.max(light, axis=0, keepdims=True)
        top = jnp.max(top, axis=1, keepdims=True)
        top_ref[...] = jnp.broadcast_to(top, top_ref.shape)
    light_ref[...] = light


def add_light(sides, counts, spots, lit, shape, before=None):
    last = before is not None
    (rows, cols), side = shape, lit.shape[0]
    return pl.pallas_call(
        functools.partial(light_kernel, sides, last),
        out_shape=(f32(rows, cols), f32(SUBLANES, side)) if last else f32(rows, cols),
        in_specs=[SM] * (1 + len(sides)) + [VM] * (1 + last),
        out_specs=(VM, VM) if last else VM,
        scratch_shapes=[pltpu.VMEM((1, rows + 2 * side, cols + 2 * side), jnp.float32)],
        compiler_params=params(12),
        cost_estimate=cost(10**8, 6 * 10**6),
        name="lighting_end" if last else "lighting_start",
    )(counts, *spots, lit, *((before,) if last else ()))


def fold_kernel(rank_of, below, with_top, *refs):
    held_ref, got_ref, top_ref = refs[:2] + ((refs[2],) if with_top else (None,))
    send_ref, keep_ref, out_top = refs[2 + with_top:] if with_top else refs[2:] + (None,)
    rows, half = held_ref.shape[0], keep_ref.shape[0]
    keep = (rank_of() >> below) & 1
    for ref, at in ((send_ref, 1 - keep), (keep_ref, keep)):
        part = pl.ds(pl.multiple_of(at * half, SUBLANES), half)
        ref[:half] = held_ref[part] + got_ref[part]
    if with_top:
        top = top_ref[...]
        if got_ref.shape[0] > rows:
            top = jnp.maximum(top, got_ref[rows:])
        out_top[...] = top
        send_ref[half:] = top


def fold(rank_of, below, held, got, top=None):
    rows, side = held.shape
    half = rows // 2
    with_top = top is not None
    extra = SUBLANES if with_top else 0
    return pl.pallas_call(
        functools.partial(fold_kernel, rank_of, below, with_top),
        out_shape=(f32(half + extra, side), f32(half, side)) + ((f32(*top.shape),) if with_top else ()),
        in_specs=[VM] * (2 + with_top),
        out_specs=(VM,) * (2 + with_top),
        compiler_params=params(8),
        cost_estimate=cost(10**6, 12 * rows * side),
        name="fold",
    )(held, got, *((top,) if with_top else ()))


def finish_kernel(parts, tile_ref, light_ref, top_ref, g_tile, g_left, g_up, probe_ref, *refs):
    pairs, n_col, pieces = parts
    count = 2 * pairs * len(pieces)
    block_refs = refs[:count]
    object_out, probe_out, new_object, new_probe, sums, sem = refs[count:]
    modes, side = probe_ref.shape[1], probe_ref.shape[2]
    rows, cols = light_ref.shape
    top = top_ref[0:1, 0:1]
    for at in range(0, cols, side):
        part = slice(at, at + side)
        scale = 1.0 / (light_ref[:, part] + 0.1 * top)
        for i in range(2):
            total = g_tile[i, :, part] + g_up[i, :, part]
            if at == 0:
                total += g_left[i]
            new_object[i, :, part] = tile_ref[i, :, part] + total * scale
    stores = [pltpu.make_async_copy(new_object, object_out, sem.at[0])]
    stores[0].start()

    my_row = lax.axis_index("row")
    core, pair, col_rank = lax.rem(my_row, 2), my_row // 2, my_col_rank()
    half, start = sums.shape[0] // 2, 0
    for j, piece in enumerate(pieces):
        for i in range(2 * pairs):
            ref, flip, d = block_refs[j * 2 * pairs + i], i // pairs, i % pairs
            base = (core ^ flip) * half + start + (plane_rank(core ^ flip, pair) ^ d) * (n_col * piece)
            for e in range(n_col):
                to = pl.multiple_of(base + (col_rank ^ e) * piece, SUBLANES)
                sums[pl.ds(to, piece)] = ref[e * piece:(e + 1) * piece]
        start += pairs * n_col * piece
    den = sums[2 * modes * side:(2 * modes + 1) * side]
    top = jnp.max(jnp.max(den, axis=0, keepdims=True), axis=1, keepdims=True)
    scale = 1.0 / (den + 0.1 * top)
    for i in range(2):
        for k in range(modes):
            at = (i * modes + k) * side
            new_probe[i, k] = probe_ref[i, k] + sums[at:at + side] * scale
        stores.append(pltpu.make_async_copy(new_probe.at[i], probe_out.at[i], sem.at[1 + i]))
        stores[-1].start()
    for store in stores:
        store.wait()


def f32(*shape):
    return jax.ShapeDtypeStruct(shape, jnp.float32)


VM = pl.BlockSpec(memory_space=pltpu.VMEM)
SM = pl.BlockSpec(memory_space=pltpu.SMEM)
ANY = pl.BlockSpec(memory_space=pl.ANY)
HBM = pl.BlockSpec(memory_space=pltpu.HBM)


def params(mib):
    return pltpu.CompilerParams(vmem_limit_bytes=mib * MIB)


def hbm(*shape):
    return pltpu.HBM(shape, jnp.float32)


def vmem(*shape):
    return pltpu.VMEM(shape, jnp.float32)


def in_hbm(value):
    return pltpu.with_memory_space_constraint(value, pltpu.HBM)


def cost(flops, moved):
    return pl.CostEstimate(flops=flops, bytes_accessed=moved, transcendentals=0)


def body(object_field, probe, amplitudes, corners, counts):
    rows, cols = object_field.shape[1], object_field.shape[2]
    modes, side = probe.shape[1], probe.shape[2]
    slots = amplitudes.shape[2]
    pairs, n_col = lax.axis_size("row") // 2, lax.axis_size("col")
    step = SUBLANES * 2 * pairs * n_col
    total_rows = -(-(2 * modes + 1) * side // step) * step
    piece = total_rows // (2 * pairs * n_col)
    pieces = [piece]
    spots = corners[0, 0]

    right = shifted(object_field[:, :, :side], 0, -1)
    measured = evens_first(amplitudes[0, 0], True)
    tile, measured, spots_now = lax.optimization_barrier((object_field, measured, spots))
    below = shifted(tile[:, :side, :], -1, 0)
    from_left = shifted(spots_now, 0, 1)
    measured = evens_first(measured, False)
    right, from_left, measured, modes_now = lax.optimization_barrier((right, from_left, measured, probe))
    corner = shifted(right[:, :side, :], -1, 0)
    from_up = shifted(jnp.concatenate([spots, from_left], axis=0), 1, 0)
    lit = jnp.sum(modes_now[0] * modes_now[0] + modes_now[1] * modes_now[1], axis=0)
    light = add_light(((0, 0), (0, 1)), counts, (spots, from_left), lit, (rows, cols))
    light, top = add_light(
        ((1, 0), (1, 1)), counts, (from_up[:slots], from_up[slots:]), lit, (rows, cols), light
    )
    corner, top, measured = lax.optimization_barrier((corner, top, measured))
    g_tile, g_lower, g_right, *halves = pl.pallas_call(
        main_kernel,
        out_shape=(
            hbm(2, rows, cols), vmem(2, side, cols + side), vmem(2, rows, side),
        ) + tuple(vmem(pairs * n_col * piece, side) for piece in pieces) * 2,
        in_specs=[SM] * 2 + [HBM] + [ANY] * 3 + [HBM] * 3,
        out_specs=(HBM,) + (VM,) * (2 + 2 * len(pieces)),
        scratch_shapes=[
            pltpu.VMEM((2, rows + side, cols + side), jnp.float32),
            pltpu.VMEM((2, rows + side, cols + side), jnp.float32),
            pltpu.VMEM((2, side, modes * side), jnp.bfloat16),
            pltpu.VMEM((2, modes * side, side), jnp.bfloat16),
            pltpu.VMEM((2, modes * side, side), jnp.float32),
            pltpu.VMEM((2, side, side), jnp.float32),
            pltpu.VMEM((total_rows, side), jnp.float32),
            pltpu.VMEM((2, side, side), jnp.float32),
            pltpu.VMEM(probe.shape, jnp.float32),
            pltpu.VMEM((4, side, side), jnp.bfloat16),
            pltpu.SemaphoreType.DMA((6,)),
            pltpu.SemaphoreType.DMA((2,)),
            pltpu.SemaphoreType.DMA((1,)),
        ],
        compiler_params=params(22),
        cost_estimate=cost(7 * 10**9, 2 * 10**7),
        name="positions",
    )(counts, spots, in_hbm(object_field), below, right, corner, *map(in_hbm, (measured, probe, tables(side))))

    chains = []
    for i, piece in enumerate(pieces):
        chains.append((halves[i], swapped(halves[len(pieces) + i], 1, 0), None if i else top))
    for i in range(plane_bits()):
        for j, (held, got, ride) in enumerate(chains):
            send, held = fold(my_plane_rank, plane_bits() - 1 - i, held, got)
            chains[j] = (held, flipped(send, i), ride)
    for i in range(col_bits()):
        for j, (held, got, ride) in enumerate(chains):
            send, held, *ride = fold(my_col_rank, col_bits() - 1 - i, held, got, ride)
            if i == 0 and j == 0:
                send, g_lower = lax.optimization_barrier((send, g_lower))
            chains[j] = (held, swapped(send, 0, 1 << i), ride[0] if ride else None)
    g_up = shifted(g_lower, 1, 0)
    owns = []
    for piece, (held, got, ride) in zip(pieces, chains):
        own = held + got[:piece]
        parts = [own] + [swapped(own, 0, rank_by(e, range(col_bits()))) for e in range(1, n_col)]
        if ride is not None:
            parts.append(jnp.maximum(ride, got[piece:]))
        owns.append(jnp.concatenate(parts, axis=0))
    owns[0], g_up, g_right = lax.optimization_barrier((owns[0], g_up, g_right + g_up[:, :, cols:]))
    g_left = shifted(g_right, 0, 1)
    gathered = []
    for j, own in enumerate(owns):
        blocks = [own]
        for i in reversed(range(plane_bits())):
            blocks = blocks + [flipped(block, i) for block in blocks]
        if j == len(owns) - 1:
            blocks[-1], g_left = lax.optimization_barrier((blocks[-1], g_left))
        gathered.append(blocks + [swapped(block, 1, 0) for block in blocks])
    top = functools.reduce(jnp.maximum, [block[n_col * pieces[0]:] for block in gathered[0]])
    blocks = sum(gathered, [])
    return pl.pallas_call(
        functools.partial(finish_kernel, (pairs, n_col, pieces)),
        out_shape=(f32(*object_field.shape), f32(*probe.shape)),
        in_specs=[VM] * (7 + len(blocks)),
        out_specs=(ANY, ANY),
        scratch_shapes=[
            pltpu.VMEM(object_field.shape, jnp.float32),
            pltpu.VMEM(probe.shape, jnp.float32),
            pltpu.VMEM((total_rows, side), jnp.float32),
            pltpu.SemaphoreType.DMA((3,)),
        ],
        compiler_params=params(20),
        cost_estimate=cost(10**6, 10**7),
        name="update",
    )(object_field, light, top, g_tile, g_left, g_up, probe, *blocks)


def solution(mesh):
    in_specs = (
        P(None, "row", "col"),
        P(),
        P("row", "col", None, None, None),
        P("row", "col", None, None),
        P(),
    )
    out_specs = (P(None, "row", "col"), P())
    return jax.shard_map(body, mesh=mesh, in_specs=in_specs, out_specs=out_specs, check_vma=False)
```

```python
import functools
import math

import jax
import jax.numpy as jnp
import numpy as np
from jax import lax
from jax.experimental import pallas as pl
from jax.experimental.pallas import tpu as pltpu
from jax.sharding import PartitionSpec as P

LANES = 128
SUBLANES = 8
MIB = 1024 * 1024


def shifted(value, d_row, d_col):
    rows, cols = lax.axis_size("row"), lax.axis_size("col")
    pairs = []
    for r in range(rows):
        for c in range(cols):
            if 0 <= r + d_row < rows and 0 <= c + d_col < cols:
                pairs.append((r * cols + c, (r + d_row) * cols + c + d_col))
    return lax.ppermute(value, ("row", "col"), pairs)


def swapped(value, flip_row, flip_col):
    rows, cols = lax.axis_size("row"), lax.axis_size("col")
    pairs = [(r * cols + c, (r ^ flip_row) * cols + (c ^ flip_col)) for r in range(rows) for c in range(cols)]
    return lax.ppermute(value, ("row", "col"), pairs)


def plane_bits():
    return (lax.axis_size("row") // 2).bit_length() - 1


def col_bits():
    return lax.axis_size("col").bit_length() - 1


def plane_bit(core, step):
    return step if core == 0 else plane_bits() - 1 - step


def rank_by(index, bits):
    rank = 0
    for bit in bits:
        rank = rank * 2 + ((index >> bit) & 1)
    return rank


def plane_rank(core, pair):
    ranks = [rank_by(pair, [plane_bit(c, step) for step in range(plane_bits())]) for c in range(2)]
    return jnp.where(core == 0, ranks[0], ranks[1])


def my_plane_rank():
    my_row = lax.axis_index("row")
    return plane_rank(lax.rem(my_row, 2), my_row // 2)


def my_col_rank():
    return rank_by(lax.axis_index("col"), range(col_bits()))


def flipped(value, step):
    rows, cols = lax.axis_size("row"), lax.axis_size("col")
    pairs = [
        (r * cols + c, (r ^ (2 << plane_bit(r % 2, step))) * cols + c) for r in range(rows) for c in range(cols)
    ]
    return lax.ppermute(value, ("row", "col"), pairs)


def tables(side):
    index = np.arange(side)
    angle = (index[:, None] * index[None, :] % side) * (2.0 * math.pi / side)
    scale = 1.0 / math.sqrt(side)
    re = (np.cos(angle) * scale).astype(np.float32)
    im = (-np.sin(angle) * scale).astype(np.float32)
    blocks = []
    for first in (0, 1):
        a, b = re[first::2, :side // 2], im[first::2, :side // 2]
        blocks.append(np.block([[a, -b], [b, a]]))
    return jnp.asarray(np.stack(blocks + [block.T for block in blocks]), jnp.bfloat16)


def evens_first(amplitudes, rows):
    side = amplitudes.shape[-1]
    order = np.concatenate([np.arange(0, side, 2), np.arange(1, side, 2)])
    pick = jnp.asarray(np.eye(side)[order], jnp.float32)
    form = "ab,sbc->sac" if rows else "cb,sab->sac"
    return jnp.einsum(form, pick, amplitudes, precision=lax.Precision.HIGH)


def corner_of(row, col):
    row_base = pl.multiple_of(row // SUBLANES * SUBLANES, SUBLANES)
    col_base = pl.multiple_of(col // LANES * LANES, LANES)
    return row_base, row - row_base, col_base, col - col_base


def window_at(ref, part, row, col, side):
    row_base, down, col_base, over = corner_of(row, col)
    groups = side // SUBLANES
    lane = lax.broadcasted_iota(jnp.int32, (side, LANES), 1)
    sub = lax.broadcasted_iota(jnp.int32, (groups, SUBLANES, LANES), 1)
    turned = []
    for j in range(side // LANES + 1):
        block = ref[part, pl.ds(row_base, side + SUBLANES), pl.ds(col_base + j * LANES, LANES)]
        block = block.reshape(groups + 1, SUBLANES, LANES)
        block = pltpu.roll(block, lax.rem(SUBLANES - down, SUBLANES), 1)
        block = jnp.where(sub < SUBLANES - down, block[:groups], block[1:]).reshape(side, LANES)
        turned.append(pltpu.roll(block, lax.rem(LANES - over, LANES), 1))
    parts = [jnp.where(lane < LANES - over, turned[j], turned[j + 1]) for j in range(side // LANES)]
    return jnp.concatenate(parts, axis=1)


def add_at(ref, part, row, col, value, side):
    row_base, down, col_base, over = corner_of(row, col)
    groups = side // SUBLANES
    blocks = side // LANES
    lane = lax.broadcasted_iota(jnp.int32, (side, LANES), 1)
    sub = lax.broadcasted_iota(jnp.int32, (groups + 1, SUBLANES, LANES), 1)
    turned = [pltpu.roll(value[:, j * LANES:(j + 1) * LANES], over, 1) for j in range(blocks)]
    none = jnp.zeros((side, LANES), value.dtype)
    gap = jnp.zeros((1, SUBLANES, LANES), value.dtype)
    for j in range(blocks + 1):
        block = jnp.where(lane >= over, turned[j] if j < blocks else none, turned[j - 1] if j else none)
        block = pltpu.roll(block.reshape(groups, SUBLANES, LANES), down, 1)
        block = jnp.where(
            sub >= down, jnp.concatenate([block, gap], axis=0), jnp.concatenate([gap, block], axis=0)
        )
        place = (part, pl.ds(row_base, side + SUBLANES), pl.ds(col_base + j * LANES, LANES))
        ref[place] += block.reshape(side + SUBLANES, LANES)


def main_kernel(
    counts_ref, spots_ref, tile_hbm, below_any, right_any, corner_any, amp_hbm, probe_hbm, table_hbm,
    g_tile, g_lower, g_right, *rest
):
    chains = (len(rest) - 13) // 2
    mine_refs, other_refs = rest[:chains], rest[chains:2 * chains]
    (
        ext, gacc, stage, turned, wave, wins, sums, amp_ref, probe_ref, table_ref, in_sem, amp_sem, out_sem,
    ) = rest[2 * chains:]
    modes, side = probe_ref.shape[1], probe_ref.shape[2]
    rows, cols = tile_hbm.shape[1], tile_hbm.shape[2]
    low = side // 2
    my_row, my_col = lax.axis_index("row"), lax.axis_index("col")
    count = counts_ref[my_row, my_col]
    loads = [(probe_hbm, probe_ref), (table_hbm, table_ref)]
    for ref, r, c in ((tile_hbm, 0, 0), (below_any, rows, 0), (right_any, 0, cols), (corner_any, rows, cols)):
        loads.append((ref, ext.at[:, pl.ds(r, ref.shape[1]), pl.ds(c, ref.shape[2])]))
    loads = [pltpu.make_async_copy(a, b, in_sem.at[i]) for i, (a, b) in enumerate(loads)]

    def amp_load(p, slot):
        return pltpu.make_async_copy(amp_hbm.at[p], amp_ref.at[slot], amp_sem.at[slot])

    for load in loads:
        load.start()
    amp_load(0, 0).start()
    gacc[...] = jnp.zeros_like(gacc)
    sums[...] = jnp.zeros_like(sums)
    for load in loads:
        load.wait()

    def dot(a, b):
        return jnp.dot(a, b, preferred_element_type=jnp.float32)

    def plane(index):
        return slice(index * side, (index + 1) * side)

    def bf16(value):
        return value.astype(jnp.bfloat16)

    def step(p, carry):
        slot = lax.rem(p, 2)

        @pl.when(p + 1 < count)
        def _():
            amp_load(p + 1, 1 - slot).start()

        row, col = spots_ref[p, 0] - my_row * rows, spots_ref[p, 1] - my_col * cols
        win_re = window_at(ext, 0, row, col, side)
        win_im = window_at(ext, 1, row, col, side)
        wins[0], wins[1] = win_re, win_im
        sums[plane(2 * modes)] += win_re * win_re + win_im * win_im
        for k in range(modes):
            pr, pi = probe_ref[0, k], probe_ref[1, k]
            for i, psi in enumerate((pr * win_re - pi * win_im, pr * win_im + pi * win_re)):
                stage[0, i * low:(i + 1) * low, plane(k)] = bf16(psi[:low] + psi[low:])
                stage[1, i * low:(i + 1) * low, plane(k)] = bf16(psi[:low] - psi[low:])
        for k in range(modes):
            for parity in range(2):
                half = dot(table_ref[parity], stage[parity, :, plane(k)])
                at = k * side + parity * low
                for i in range(2):
                    left, right = half[i * low:(i + 1) * low, :low], half[i * low:(i + 1) * low, low:]
                    turned[0, at:at + low, i * low:(i + 1) * low] = bf16(left + right)
                    turned[1, at:at + low, i * low:(i + 1) * low] = bf16(left - right)
        models = [jnp.zeros((side, low), jnp.float32)] * 2
        for parity in range(2):
            for k in range(modes):
                got = dot(turned[parity, plane(k)], table_ref[2 + parity])
                wave[parity, plane(k)] = got
                models[parity] += got[:, :low] * got[:, :low] + got[:, low:] * got[:, low:]
        amp_load(p, slot).wait()
        for parity in range(2):
            model = models[parity]
            factor = amp_ref[slot, :, parity * low:(parity + 1) * low] * lax.rsqrt(jnp.maximum(model, 1.0)) - 1.0
            for k in range(modes):
                at = k * side + parity * low
                for i in range(2):
                    target = bf16(wave[parity, plane(k), i * low:(i + 1) * low] * factor)
                    stage[0, i * low:(i + 1) * low, at:at + low] = target[:low]
                    stage[1, i * low:(i + 1) * low, at:at + low] = target[low:]
        for k in range(modes):
            even = dot(table_ref[2], stage[0, :, plane(k)])
            odd = dot(table_ref[3], stage[1, :, plane(k)])
            for lower, back in enumerate((bf16(even + odd), bf16(even - odd))):
                at = k * side + lower * low
                for i in range(2):
                    for parity in range(2):
                        turned[parity, at:at + low, i * low:(i + 1) * low] = (
                            back[i * low:(i + 1) * low, parity * low:(parity + 1) * low]
                        )
        grads = [[jnp.zeros((side, low), jnp.float32)] * 2 for _ in range(2)]
        for k in range(modes):
            even = dot(turned[0, plane(k)], table_ref[0])
            odd = dot(turned[1, plane(k)], table_ref[1])
            for lower, chi in enumerate((even + odd, even - odd)):
                part = slice(lower * low, (lower + 1) * low)
                cr, ci = chi[:, :low], chi[:, low:]
                pr, pi = probe_ref[0, k, :, part], probe_ref[1, k, :, part]
                win_re, win_im = wins[0, :, part], wins[1, :, part]
                grads[lower][0] += pr * cr + pi * ci
                grads[lower][1] += pr * ci - pi * cr
                sums[plane(k), part] += win_re * cr + win_im * ci
                sums[plane(modes + k), part] += win_re * ci - win_im * cr
        for i in range(2):
            add_at(gacc, i, row, col, jnp.concatenate([grads[0][i], grads[1][i]], axis=1), side)
        return carry

    lax.fori_loop(0, count, step, 0)

    store = pltpu.make_async_copy(gacc.at[:, pl.ds(0, rows), pl.ds(0, cols)], g_tile, out_sem.at[0])
    store.start()
    core = lax.rem(my_row, 2)
    half = sums.shape[0] // 2
    for refs, at in ((other_refs, 1 - core), (mine_refs, core)):
        start = 0
        for ref in refs:
            ref[...] = sums[pl.ds(pl.multiple_of(at * half + start, SUBLANES), ref.shape[0])]
            start += ref.shape[0]
    g_lower[...] = gacc[:, rows:]
    g_right[...] = gacc[:, :rows, cols:]
    store.wait()


def light_kernel(sides, last, counts_ref, *refs):
    spot_refs, (lit_ref, *rest) = refs[:len(sides)], refs[len(sides):]
    light_ref, acc = rest[1 if last else 0], rest[-1]
    side = lit_ref.shape[0]
    rows, cols = light_ref.shape
    my_row, my_col = lax.axis_index("row"), lax.axis_index("col")
    acc[...] = jnp.zeros_like(acc)
    for ref, (d_row, d_col) in zip(spot_refs, sides):
        inside = (my_row >= d_row) & (my_col >= d_col)
        number = counts_ref[jnp.maximum(my_row - d_row, 0), jnp.maximum(my_col - d_col, 0)]

        def step(p, carry, ref=ref):
            row, col = ref[p, 0] - my_row * rows + side, ref[p, 1] - my_col * cols + side

            @pl.when((row > 0) & (col > 0))
            def _():
                add_at(acc, 0, row, col, lit_ref[...], side)

            return carry

        lax.fori_loop(0, jnp.where(inside, number, 0), step, 0)
    light = acc[0, side:side + rows, side:side + cols]
    if last:
        light += rest[0][...]
        top_ref = rest[2]
        top = jnp.max(light, axis=0, keepdims=True)
        top = jnp.max(top, axis=1, keepdims=True)
        top_ref[...] = jnp.broadcast_to(top, top_ref.shape)
    light_ref[...] = light


def add_light(sides, counts, spots, lit, shape, before=None):
    last = before is not None
    (rows, cols), side = shape, lit.shape[0]
    return pl.pallas_call(
        functools.partial(light_kernel, sides, last),
        out_shape=(f32(rows, cols), f32(SUBLANES, side)) if last else f32(rows, cols),
        in_specs=[SM] * (1 + len(sides)) + [VM] * (1 + last),
        out_specs=(VM, VM) if last else VM,
        scratch_shapes=[pltpu.VMEM((1, rows + 2 * side, cols + 2 * side), jnp.float32)],
        compiler_params=params(12),
        cost_estimate=cost(10**8, 6 * 10**6),
        name="lighting_end" if last else "lighting_start",
    )(counts, *spots, lit, *((before,) if last else ()))


def fold_kernel(rank_of, below, with_top, *refs):
    held_ref, got_ref, top_ref = refs[:2] + ((refs[2],) if with_top else (None,))
    send_ref, keep_ref, out_top = refs[2 + with_top:] if with_top else refs[2:] + (None,)
    rows, half = held_ref.shape[0], keep_ref.shape[0]
    keep = (rank_of() >> below) & 1
    for ref, at in ((send_ref, 1 - keep), (keep_ref, keep)):
        part = pl.ds(pl.multiple_of(at * half, SUBLANES), half)
        ref[:half] = held_ref[part] + got_ref[part]
    if with_top:
        top = top_ref[...]
        if got_ref.shape[0] > rows:
            top = jnp.maximum(top, got_ref[rows:])
        out_top[...] = top
        send_ref[half:] = top


def fold(rank_of, below, held, got, top=None):
    rows, side = held.shape
    half = rows // 2
    with_top = top is not None
    extra = SUBLANES if with_top else 0
    return pl.pallas_call(
        functools.partial(fold_kernel, rank_of, below, with_top),
        out_shape=(f32(half + extra, side), f32(half, side)) + ((f32(*top.shape),) if with_top else ()),
        in_specs=[VM] * (2 + with_top),
        out_specs=(VM,) * (2 + with_top),
        compiler_params=params(8),
        cost_estimate=cost(10**6, 12 * rows * side),
        name="fold",
    )(held, got, *((top,) if with_top else ()))


def finish_kernel(parts, tile_ref, light_ref, top_ref, g_tile, g_left, g_up, probe_ref, *refs):
    pairs, n_col, pieces = parts
    count = 2 * pairs * len(pieces)
    block_refs = refs[:count]
    object_out, probe_out, new_object, new_probe, sums, sem = refs[count:]
    modes, side = probe_ref.shape[1], probe_ref.shape[2]
    rows, cols = light_ref.shape
    top = top_ref[0:1, 0:1]
    for at in range(0, cols, side):
        part = slice(at, at + side)
        scale = 1.0 / (light_ref[:, part] + 0.1 * top)
        for i in range(2):
            total = g_tile[i, :, part] + g_up[i, :, part]
            if at == 0:
                total += g_left[i]
            new_object[i, :, part] = tile_ref[i, :, part] + total * scale
    stores = [pltpu.make_async_copy(new_object, object_out, sem.at[0])]
    stores[0].start()

    my_row = lax.axis_index("row")
    core, pair, col_rank = lax.rem(my_row, 2), my_row // 2, my_col_rank()
    half, start = sums.shape[0] // 2, 0
    for j, piece in enumerate(pieces):
        for i in range(2 * pairs):
            ref, flip, d = block_refs[j * 2 * pairs + i], i // pairs, i % pairs
            base = (core ^ flip) * half + start + (plane_rank(core ^ flip, pair) ^ d) * (n_col * piece)
            for e in range(n_col):
                to = pl.multiple_of(base + (col_rank ^ e) * piece, SUBLANES)
                sums[pl.ds(to, piece)] = ref[e * piece:(e + 1) * piece]
        start += pairs * n_col * piece
    den = sums[2 * modes * side:(2 * modes + 1) * side]
    top = jnp.max(jnp.max(den, axis=0, keepdims=True), axis=1, keepdims=True)
    scale = 1.0 / (den + 0.1 * top)
    for i in range(2):
        for k in range(modes):
            at = (i * modes + k) * side
            new_probe[i, k] = probe_ref[i, k] + sums[at:at + side] * scale
        stores.append(pltpu.make_async_copy(new_probe.at[i], probe_out.at[i], sem.at[1 + i]))
        stores[-1].start()
    for store in stores:
        store.wait()


def f32(*shape):
    return jax.ShapeDtypeStruct(shape, jnp.float32)


VM = pl.BlockSpec(memory_space=pltpu.VMEM)
SM = pl.BlockSpec(memory_space=pltpu.SMEM)
ANY = pl.BlockSpec(memory_space=pl.ANY)
HBM = pl.BlockSpec(memory_space=pltpu.HBM)


def params(mib):
    return pltpu.CompilerParams(vmem_limit_bytes=mib * MIB)


def hbm(*shape):
    return pltpu.HBM(shape, jnp.float32)


def vmem(*shape):
    return pltpu.VMEM(shape, jnp.float32)


def in_hbm(value):
    return pltpu.with_memory_space_constraint(value, pltpu.HBM)


def cost(flops, moved):
    return pl.CostEstimate(flops=flops, bytes_accessed=moved, transcendentals=0)


def body(object_field, probe, amplitudes, corners, counts):
    rows, cols = object_field.shape[1], object_field.shape[2]
    modes, side = probe.shape[1], probe.shape[2]
    slots = amplitudes.shape[2]
    pairs, n_col = lax.axis_size("row") // 2, lax.axis_size("col")
    step = SUBLANES * 2 * pairs * n_col
    total_rows = -(-(2 * modes + 1) * side // step) * step
    piece = total_rows // (2 * pairs * n_col)
    pieces = [piece]
    spots = corners[0, 0]

    right = shifted(object_field[:, :, :side], 0, -1)
    measured = evens_first(amplitudes[0, 0], True)
    tile, measured, spots_now = lax.optimization_barrier((object_field, measured, spots))
    below = shifted(tile[:, :side, :], -1, 0)
    from_left = shifted(spots_now, 0, 1)
    measured = evens_first(measured, False)
    right, from_left, measured, modes_now = lax.optimization_barrier((right, from_left, measured, probe))
    corner = shifted(right[:, :side, :], -1, 0)
    from_up = shifted(jnp.concatenate([spots, from_left], axis=0), 1, 0)
    lit = jnp.sum(modes_now[0] * modes_now[0] + modes_now[1] * modes_now[1], axis=0)
    light = add_light(((0, 0), (0, 1)), counts, (spots, from_left), lit, (rows, cols))
    light, top = add_light(
        ((1, 0), (1, 1)), counts, (from_up[:slots], from_up[slots:]), lit, (rows, cols), light
    )
    corner, top, measured = lax.optimization_barrier((corner, top, measured))
    g_tile, g_lower, g_right, *halves = pl.pallas_call(
        main_kernel,
        out_shape=(
            hbm(2, rows, cols), vmem(2, side, cols + side), vmem(2, rows, side),
        ) + tuple(vmem(pairs * n_col * piece, side) for piece in pieces) * 2,
        in_specs=[SM] * 2 + [HBM] + [ANY] * 3 + [HBM] * 3,
        out_specs=(HBM,) + (VM,) * (2 + 2 * len(pieces)),
        scratch_shapes=[
            pltpu.VMEM((2, rows + side, cols + side), jnp.float32),
            pltpu.VMEM((2, rows + side, cols + side), jnp.float32),
            pltpu.VMEM((2, side, modes * side), jnp.bfloat16),
            pltpu.VMEM((2, modes * side, side), jnp.bfloat16),
            pltpu.VMEM((2, modes * side, side), jnp.float32),
            pltpu.VMEM((2, side, side), jnp.float32),
            pltpu.VMEM((total_rows, side), jnp.float32),
            pltpu.VMEM((2, side, side), jnp.float32),
            pltpu.VMEM(probe.shape, jnp.float32),
            pltpu.VMEM((4, side, side), jnp.bfloat16),
            pltpu.SemaphoreType.DMA((6,)),
            pltpu.SemaphoreType.DMA((2,)),
            pltpu.SemaphoreType.DMA((1,)),
        ],
        compiler_params=params(22),
        cost_estimate=cost(7 * 10**9, 2 * 10**7),
        name="positions",
    )(counts, spots, in_hbm(object_field), below, right, corner, *map(in_hbm, (measured, probe, tables(side))))

    chains = []
    for i, piece in enumerate(pieces):
        chains.append((halves[i], swapped(halves[len(pieces) + i], 1, 0), None if i else top))
    for i in range(plane_bits()):
        for j, (held, got, ride) in enumerate(chains):
            send, held = fold(my_plane_rank, plane_bits() - 1 - i, held, got)
            if i == plane_bits() - 1 and j == 0:
                send, g_lower = lax.optimization_barrier((send, g_lower))
            chains[j] = (held, flipped(send, i), ride)
    for i in range(col_bits()):
        for j, (held, got, ride) in enumerate(chains):
            send, held, *ride = fold(my_col_rank, col_bits() - 1 - i, held, got, ride)
            chains[j] = (held, swapped(send, 0, 1 << i), ride[0] if ride else None)
    g_up = shifted(g_lower, 1, 0)
    owns = []
    for piece, (held, got, ride) in zip(pieces, chains):
        own = held + got[:piece]
        parts = [own] + [swapped(own, 0, rank_by(e, range(col_bits()))) for e in range(1, n_col)]
        if ride is not None:
            parts.append(jnp.maximum(ride, got[piece:]))
        owns.append(jnp.concatenate(parts, axis=0))
    owns[0], g_up, g_right = lax.optimization_barrier((owns[0], g_up, g_right + g_up[:, :, cols:]))
    g_left = shifted(g_right, 0, 1)
    gathered = []
    for j, own in enumerate(owns):
        blocks = [own]
        for i in reversed(range(plane_bits())):
            blocks = blocks + [flipped(block, i) for block in blocks]
        if j == len(owns) - 1:
            blocks[-1], g_left = lax.optimization_barrier((blocks[-1], g_left))
        gathered.append(blocks + [swapped(block, 1, 0) for block in blocks])
    top = functools.reduce(jnp.maximum, [block[n_col * pieces[0]:] for block in gathered[0]])
    blocks = sum(gathered, [])
    return pl.pallas_call(
        functools.partial(finish_kernel, (pairs, n_col, pieces)),
        out_shape=(f32(*object_field.shape), f32(*probe.shape)),
        in_specs=[VM] * (7 + len(blocks)),
        out_specs=(ANY, ANY),
        scratch_shapes=[
            pltpu.VMEM(object_field.shape, jnp.float32),
            pltpu.VMEM(probe.shape, jnp.float32),
            pltpu.VMEM((total_rows, side), jnp.float32),
            pltpu.SemaphoreType.DMA((3,)),
        ],
        compiler_params=params(20),
        cost_estimate=cost(10**6, 10**7),
        name="update",
    )(object_field, light, top, g_tile, g_left, g_up, probe, *blocks)


def solution(mesh):
    in_specs = (
        P(None, "row", "col"),
        P(),
        P("row", "col", None, None, None),
        P("row", "col", None, None),
        P(),
    )
    out_specs = (P(None, "row", "col"), P())
    return jax.shard_map(body, mesh=mesh, in_specs=in_specs, out_specs=out_specs, check_vma=False)
```

```python
import functools
import math

import jax
import jax.numpy as jnp
import numpy as np
from jax import lax
from jax.experimental import pallas as pl
from jax.experimental.pallas import tpu as pltpu
from jax.sharding import PartitionSpec as P

LANES = 128
SUBLANES = 8
MIB = 1024 * 1024


def shifted(value, d_row, d_col):
    rows, cols = lax.axis_size("row"), lax.axis_size("col")
    pairs = []
    for r in range(rows):
        for c in range(cols):
            if 0 <= r + d_row < rows and 0 <= c + d_col < cols:
                pairs.append((r * cols + c, (r + d_row) * cols + c + d_col))
    return lax.ppermute(value, ("row", "col"), pairs)


def swapped(value, flip_row, flip_col):
    rows, cols = lax.axis_size("row"), lax.axis_size("col")
    pairs = [(r * cols + c, (r ^ flip_row) * cols + (c ^ flip_col)) for r in range(rows) for c in range(cols)]
    return lax.ppermute(value, ("row", "col"), pairs)


def plane_bits():
    return (lax.axis_size("row") // 2).bit_length() - 1


def col_bits():
    return lax.axis_size("col").bit_length() - 1


def plane_bit(core, step):
    return step if core == 0 else plane_bits() - 1 - step


def rank_by(index, bits):
    rank = 0
    for bit in bits:
        rank = rank * 2 + ((index >> bit) & 1)
    return rank


def plane_rank(core, pair):
    ranks = [rank_by(pair, [plane_bit(c, step) for step in range(plane_bits())]) for c in range(2)]
    return jnp.where(core == 0, ranks[0], ranks[1])


def my_plane_rank():
    my_row = lax.axis_index("row")
    return plane_rank(lax.rem(my_row, 2), my_row // 2)


def my_col_rank():
    return rank_by(lax.axis_index("col"), range(col_bits()))


def flipped(value, step):
    rows, cols = lax.axis_size("row"), lax.axis_size("col")
    pairs = [
        (r * cols + c, (r ^ (2 << plane_bit(r % 2, step))) * cols + c) for r in range(rows) for c in range(cols)
    ]
    return lax.ppermute(value, ("row", "col"), pairs)


def tables(side):
    index = np.arange(side)
    angle = (index[:, None] * index[None, :] % side) * (2.0 * math.pi / side)
    scale = 1.0 / math.sqrt(side)
    re = (np.cos(angle) * scale).astype(np.float32)
    im = (-np.sin(angle) * scale).astype(np.float32)
    blocks = []
    for first in (0, 1):
        a, b = re[first::2, :side // 2], im[first::2, :side // 2]
        blocks.append(np.block([[a, -b], [b, a]]))
    return jnp.asarray(np.stack(blocks + [block.T for block in blocks]), jnp.bfloat16)


def evens_first(amplitudes, rows):
    side = amplitudes.shape[-1]
    order = np.concatenate([np.arange(0, side, 2), np.arange(1, side, 2)])
    pick = jnp.asarray(np.eye(side)[order], jnp.float32)
    form = "ab,sbc->sac" if rows else "cb,sab->sac"
    return jnp.einsum(form, pick, amplitudes, precision=lax.Precision.HIGH)


def corner_of(row, col):
    row_base = pl.multiple_of(row // SUBLANES * SUBLANES, SUBLANES)
    col_base = pl.multiple_of(col // LANES * LANES, LANES)
    return row_base, row - row_base, col_base, col - col_base


def window_at(ref, part, row, col, side):
    row_base, down, col_base, over = corner_of(row, col)
    groups = side // SUBLANES
    lane = lax.broadcasted_iota(jnp.int32, (side, LANES), 1)
    sub = lax.broadcasted_iota(jnp.int32, (groups, SUBLANES, LANES), 1)
    turned = []
    for j in range(side // LANES + 1):
        block = ref[part, pl.ds(row_base, side + SUBLANES), pl.ds(col_base + j * LANES, LANES)]
        block = block.reshape(groups + 1, SUBLANES, LANES)
        block = pltpu.roll(block, lax.rem(SUBLANES - down, SUBLANES), 1)
        block = jnp.where(sub < SUBLANES - down, block[:groups], block[1:]).reshape(side, LANES)
        turned.append(pltpu.roll(block, lax.rem(LANES - over, LANES), 1))
    parts = [jnp.where(lane < LANES - over, turned[j], turned[j + 1]) for j in range(side // LANES)]
    return jnp.concatenate(parts, axis=1)


def add_at(ref, part, row, col, value, side):
    row_base, down, col_base, over = corner_of(row, col)
    groups = side // SUBLANES
    blocks = side // LANES
    lane = lax.broadcasted_iota(jnp.int32, (side, LANES), 1)
    sub = lax.broadcasted_iota(jnp.int32, (groups + 1, SUBLANES, LANES), 1)
    turned = [pltpu.roll(value[:, j * LANES:(j + 1) * LANES], over, 1) for j in range(blocks)]
    none = jnp.zeros((side, LANES), value.dtype)
    gap = jnp.zeros((1, SUBLANES, LANES), value.dtype)
    for j in range(blocks + 1):
        block = jnp.where(lane >= over, turned[j] if j < blocks else none, turned[j - 1] if j else none)
        block = pltpu.roll(block.reshape(groups, SUBLANES, LANES), down, 1)
        block = jnp.where(
            sub >= down, jnp.concatenate([block, gap], axis=0), jnp.concatenate([gap, block], axis=0)
        )
        place = (part, pl.ds(row_base, side + SUBLANES), pl.ds(col_base + j * LANES, LANES))
        ref[place] += block.reshape(side + SUBLANES, LANES)


def main_kernel(
    counts_ref, spots_ref, tile_hbm, below_any, right_any, corner_any, amp_hbm, probe_hbm, table_hbm,
    g_tile, g_lower, g_right, *rest
):
    chains = (len(rest) - 13) // 2
    mine_refs, other_refs = rest[:chains], rest[chains:2 * chains]
    (
        ext, gacc, stage, turned, wave, wins, sums, amp_ref, probe_ref, table_ref, in_sem, amp_sem, out_sem,
    ) = rest[2 * chains:]
    modes, side = probe_ref.shape[1], probe_ref.shape[2]
    rows, cols = tile_hbm.shape[1], tile_hbm.shape[2]
    low = side // 2
    my_row, my_col = lax.axis_index("row"), lax.axis_index("col")
    count = counts_ref[my_row, my_col]
    loads = [(probe_hbm, probe_ref), (table_hbm, table_ref)]
    for ref, r, c in ((tile_hbm, 0, 0), (below_any, rows, 0), (right_any, 0, cols), (corner_any, rows, cols)):
        loads.append((ref, ext.at[:, pl.ds(r, ref.shape[1]), pl.ds(c, ref.shape[2])]))
    loads = [pltpu.make_async_copy(a, b, in_sem.at[i]) for i, (a, b) in enumerate(loads)]

    def amp_load(p, slot):
        return pltpu.make_async_copy(amp_hbm.at[p], amp_ref.at[slot], amp_sem.at[slot])

    for load in loads:
        load.start()
    amp_load(0, 0).start()
    gacc[...] = jnp.zeros_like(gacc)
    sums[...] = jnp.zeros_like(sums)
    for load in loads:
        load.wait()

    def dot(a, b):
        return jnp.dot(a, b, preferred_element_type=jnp.float32)

    def plane(index):
        return slice(index * side, (index + 1) * side)

    def bf16(value):
        return value.astype(jnp.bfloat16)

    def step(p, carry):
        slot = lax.rem(p, 2)

        @pl.when(p + 1 < count)
        def _():
            amp_load(p + 1, 1 - slot).start()

        row, col = spots_ref[p, 0] - my_row * rows, spots_ref[p, 1] - my_col * cols
        win_re = window_at(ext, 0, row, col, side)
        win_im = window_at(ext, 1, row, col, side)
        wins[0], wins[1] = win_re, win_im
        sums[plane(2 * modes)] += win_re * win_re + win_im * win_im
        for k in range(modes):
            pr, pi = probe_ref[0, k], probe_ref[1, k]
            for i, psi in enumerate((pr * win_re - pi * win_im, pr * win_im + pi * win_re)):
                stage[0, i * low:(i + 1) * low, plane(k)] = bf16(psi[:low] + psi[low:])
                stage[1, i * low:(i + 1) * low, plane(k)] = bf16(psi[:low] - psi[low:])
        for k in range(modes):
            for parity in range(2):
                half = dot(table_ref[parity], stage[parity, :, plane(k)])
                at = k * side + parity * low
                for i in range(2):
                    left, right = half[i * low:(i + 1) * low, :low], half[i * low:(i + 1) * low, low:]
                    turned[0, at:at + low, i * low:(i + 1) * low] = bf16(left + right)
                    turned[1, at:at + low, i * low:(i + 1) * low] = bf16(left - right)
        models = [jnp.zeros((side, low), jnp.float32)] * 2
        for parity in range(2):
            for k in range(modes):
                got = dot(turned[parity, plane(k)], table_ref[2 + parity])
                wave[parity, plane(k)] = got
                models[parity] += got[:, :low] * got[:, :low] + got[:, low:] * got[:, low:]
        amp_load(p, slot).wait()
        for parity in range(2):
            model = models[parity]
            factor = amp_ref[slot, :, parity * low:(parity + 1) * low] * lax.rsqrt(jnp.maximum(model, 1.0)) - 1.0
            for k in range(modes):
                at = k * side + parity * low
                for i in range(2):
                    target = bf16(wave[parity, plane(k), i * low:(i + 1) * low] * factor)
                    stage[0, i * low:(i + 1) * low, at:at + low] = target[:low]
                    stage[1, i * low:(i + 1) * low, at:at + low] = target[low:]
        for k in range(modes):
            even = dot(table_ref[2], stage[0, :, plane(k)])
            odd = dot(table_ref[3], stage[1, :, plane(k)])
            for lower, back in enumerate((bf16(even + odd), bf16(even - odd))):
                at = k * side + lower * low
                for i in range(2):
                    for parity in range(2):
                        turned[parity, at:at + low, i * low:(i + 1) * low] = (
                            back[i * low:(i + 1) * low, parity * low:(parity + 1) * low]
                        )
        grads = [[jnp.zeros((side, low), jnp.float32)] * 2 for _ in range(2)]
        for k in range(modes):
            even = dot(turned[0, plane(k)], table_ref[0])
            odd = dot(turned[1, plane(k)], table_ref[1])
            for lower, chi in enumerate((even + odd, even - odd)):
                part = slice(lower * low, (lower + 1) * low)
                cr, ci = chi[:, :low], chi[:, low:]
                pr, pi = probe_ref[0, k, :, part], probe_ref[1, k, :, part]
                win_re, win_im = wins[0, :, part], wins[1, :, part]
                grads[lower][0] += pr * cr + pi * ci
                grads[lower][1] += pr * ci - pi * cr
                sums[plane(k), part] += win_re * cr + win_im * ci
                sums[plane(modes + k), part] += win_re * ci - win_im * cr
        for i in range(2):
            add_at(gacc, i, row, col, jnp.concatenate([grads[0][i], grads[1][i]], axis=1), side)
        return carry

    lax.fori_loop(0, count, step, 0)

    store = pltpu.make_async_copy(gacc.at[:, pl.ds(0, rows), pl.ds(0, cols)], g_tile, out_sem.at[0])
    store.start()
    core = lax.rem(my_row, 2)
    half = sums.shape[0] // 2
    for refs, at in ((other_refs, 1 - core), (mine_refs, core)):
        start = 0
        for ref in refs:
            ref[...] = sums[pl.ds(pl.multiple_of(at * half + start, SUBLANES), ref.shape[0])]
            start += ref.shape[0]
    g_lower[...] = gacc[:, rows:]
    g_right[...] = gacc[:, :rows, cols:]
    store.wait()


def light_kernel(sides, last, counts_ref, *refs):
    spot_refs, (lit_ref, *rest) = refs[:len(sides)], refs[len(sides):]
    light_ref, acc = rest[1 if last else 0], rest[-1]
    side = lit_ref.shape[0]
    rows, cols = light_ref.shape
    my_row, my_col = lax.axis_index("row"), lax.axis_index("col")
    acc[...] = jnp.zeros_like(acc)
    for ref, (d_row, d_col) in zip(spot_refs, sides):
        inside = (my_row >= d_row) & (my_col >= d_col)
        number = counts_ref[jnp.maximum(my_row - d_row, 0), jnp.maximum(my_col - d_col, 0)]

        def step(p, carry, ref=ref):
            row, col = ref[p, 0] - my_row * rows + side, ref[p, 1] - my_col * cols + side

            @pl.when((row > 0) & (col > 0))
            def _():
                add_at(acc, 0, row, col, lit_ref[...], side)

            return carry

        lax.fori_loop(0, jnp.where(inside, number, 0), step, 0)
    light = acc[0, side:side + rows, side:side + cols]
    if last:
        light += rest[0][...]
        top_ref = rest[2]
        top = jnp.max(light, axis=0, keepdims=True)
        top = jnp.max(top, axis=1, keepdims=True)
        top_ref[...] = jnp.broadcast_to(top, top_ref.shape)
    light_ref[...] = light


def add_light(sides, counts, spots, lit, shape, before=None):
    last = before is not None
    (rows, cols), side = shape, lit.shape[0]
    return pl.pallas_call(
        functools.partial(light_kernel, sides, last),
        out_shape=(f32(rows, cols), f32(SUBLANES, side)) if last else f32(rows, cols),
        in_specs=[SM] * (1 + len(sides)) + [VM] * (1 + last),
        out_specs=(VM, VM) if last else VM,
        scratch_shapes=[pltpu.VMEM((1, rows + 2 * side, cols + 2 * side), jnp.float32)],
        compiler_params=params(12),
        cost_estimate=cost(10**8, 6 * 10**6),
        name="lighting_end" if last else "lighting_start",
    )(counts, *spots, lit, *((before,) if last else ()))


def fold_kernel(rank_of, below, with_top, *refs):
    held_ref, got_ref, top_ref = refs[:2] + ((refs[2],) if with_top else (None,))
    send_ref, keep_ref, out_top = refs[2 + with_top:] if with_top else refs[2:] + (None,)
    rows, half = held_ref.shape[0], keep_ref.shape[0]
    keep = (rank_of() >> below) & 1
    for ref, at in ((send_ref, 1 - keep), (keep_ref, keep)):
        part = pl.ds(pl.multiple_of(at * half, SUBLANES), half)
        ref[:half] = held_ref[part] + got_ref[part]
    if with_top:
        top = top_ref[...]
        if got_ref.shape[0] > rows:
            top = jnp.maximum(top, got_ref[rows:])
        out_top[...] = top
        send_ref[half:] = top


def fold(rank_of, below, held, got, top=None):
    rows, side = held.shape
    half = rows // 2
    with_top = top is not None
    extra = SUBLANES if with_top else 0
    return pl.pallas_call(
        functools.partial(fold_kernel, rank_of, below, with_top),
        out_shape=(f32(half + extra, side), f32(half, side)) + ((f32(*top.shape),) if with_top else ()),
        in_specs=[VM] * (2 + with_top),
        out_specs=(VM,) * (2 + with_top),
        compiler_params=params(8),
        cost_estimate=cost(10**6, 12 * rows * side),
        name="fold",
    )(held, got, *((top,) if with_top else ()))


def finish_kernel(parts, tile_ref, light_ref, top_ref, g_tile, g_left, g_up, probe_ref, *refs):
    pairs, n_col, pieces = parts
    count = 2 * pairs * len(pieces)
    block_refs = refs[:count]
    object_out, probe_out, new_object, new_probe, sums, sem = refs[count:]
    modes, side = probe_ref.shape[1], probe_ref.shape[2]
    rows, cols = light_ref.shape
    top = top_ref[0:1, 0:1]
    for at in range(0, cols, side):
        part = slice(at, at + side)
        scale = 1.0 / (light_ref[:, part] + 0.1 * top)
        for i in range(2):
            total = g_tile[i, :, part] + g_up[i, :, part]
            if at == 0:
                total += g_left[i]
            new_object[i, :, part] = tile_ref[i, :, part] + total * scale
    stores = [pltpu.make_async_copy(new_object, object_out, sem.at[0])]
    stores[0].start()

    my_row = lax.axis_index("row")
    core, pair, col_rank = lax.rem(my_row, 2), my_row // 2, my_col_rank()
    half, start = sums.shape[0] // 2, 0
    for j, piece in enumerate(pieces):
        for i in range(2 * pairs):
            ref, flip, d = block_refs[j * 2 * pairs + i], i // pairs, i % pairs
            base = (core ^ flip) * half + start + (plane_rank(core ^ flip, pair) ^ d) * (n_col * piece)
            for e in range(n_col):
                to = pl.multiple_of(base + (col_rank ^ e) * piece, SUBLANES)
                sums[pl.ds(to, piece)] = ref[e * piece:(e + 1) * piece]
        start += pairs * n_col * piece
    den = sums[2 * modes * side:(2 * modes + 1) * side]
    top = jnp.max(jnp.max(den, axis=0, keepdims=True), axis=1, keepdims=True)
    scale = 1.0 / (den + 0.1 * top)
    for i in range(2):
        for k in range(modes):
            at = (i * modes + k) * side
            new_probe[i, k] = probe_ref[i, k] + sums[at:at + side] * scale
        stores.append(pltpu.make_async_copy(new_probe.at[i], probe_out.at[i], sem.at[1 + i]))
        stores[-1].start()
    for store in stores:
        store.wait()


def f32(*shape):
    return jax.ShapeDtypeStruct(shape, jnp.float32)


VM = pl.BlockSpec(memory_space=pltpu.VMEM)
SM = pl.BlockSpec(memory_space=pltpu.SMEM)
ANY = pl.BlockSpec(memory_space=pl.ANY)
HBM = pl.BlockSpec(memory_space=pltpu.HBM)


def params(mib):
    return pltpu.CompilerParams(vmem_limit_bytes=mib * MIB)


def hbm(*shape):
    return pltpu.HBM(shape, jnp.float32)


def vmem(*shape):
    return pltpu.VMEM(shape, jnp.float32)


def in_hbm(value):
    return pltpu.with_memory_space_constraint(value, pltpu.HBM)


def cost(flops, moved):
    return pl.CostEstimate(flops=flops, bytes_accessed=moved, transcendentals=0)


def body(object_field, probe, amplitudes, corners, counts):
    rows, cols = object_field.shape[1], object_field.shape[2]
    modes, side = probe.shape[1], probe.shape[2]
    slots = amplitudes.shape[2]
    pairs, n_col = lax.axis_size("row") // 2, lax.axis_size("col")
    step = SUBLANES * 2 * pairs * n_col
    total_rows = -(-(2 * modes + 1) * side // step) * step
    piece = total_rows // (2 * pairs * n_col)
    pieces = [piece]
    spots = corners[0, 0]

    right = shifted(object_field[:, :, :side], 0, -1)
    lit = jnp.sum(probe[0] * probe[0] + probe[1] * probe[1], axis=0)
    tile, lit, spots_now, patterns = lax.optimization_barrier((object_field, lit, spots, amplitudes[0, 0]))
    measured = evens_first(patterns, True)
    below = shifted(tile[:, :side, :], -1, 0)
    from_left = shifted(spots_now, 0, 1)
    measured = evens_first(measured, False)
    right, from_left, measured = lax.optimization_barrier((right, from_left, measured))
    corner = shifted(right[:, :side, :], -1, 0)
    from_up = shifted(jnp.concatenate([spots, from_left], axis=0), 1, 0)
    light = add_light(((0, 0), (0, 1)), counts, (spots, from_left), lit, (rows, cols))
    light, top = add_light(
        ((1, 0), (1, 1)), counts, (from_up[:slots], from_up[slots:]), lit, (rows, cols), light
    )
    corner, top, measured = lax.optimization_barrier((corner, top, measured))
    g_tile, g_lower, g_right, *halves = pl.pallas_call(
        main_kernel,
        out_shape=(
            hbm(2, rows, cols), vmem(2, side, cols + side), vmem(2, rows, side),
        ) + tuple(vmem(pairs * n_col * piece, side) for piece in pieces) * 2,
        in_specs=[SM] * 2 + [HBM] + [ANY] * 3 + [HBM] * 3,
        out_specs=(HBM,) + (VM,) * (2 + 2 * len(pieces)),
        scratch_shapes=[
            pltpu.VMEM((2, rows + side, cols + side), jnp.float32),
            pltpu.VMEM((2, rows + side, cols + side), jnp.float32),
            pltpu.VMEM((2, side, modes * side), jnp.bfloat16),
            pltpu.VMEM((2, modes * side, side), jnp.bfloat16),
            pltpu.VMEM((2, modes * side, side), jnp.float32),
            pltpu.VMEM((2, side, side), jnp.float32),
            pltpu.VMEM((total_rows, side), jnp.float32),
            pltpu.VMEM((2, side, side), jnp.float32),
            pltpu.VMEM(probe.shape, jnp.float32),
            pltpu.VMEM((4, side, side), jnp.bfloat16),
            pltpu.SemaphoreType.DMA((6,)),
            pltpu.SemaphoreType.DMA((2,)),
            pltpu.SemaphoreType.DMA((1,)),
        ],
        compiler_params=params(22),
        cost_estimate=cost(7 * 10**9, 2 * 10**7),
        name="positions",
    )(counts, spots, in_hbm(object_field), below, right, corner, *map(in_hbm, (measured, probe, tables(side))))

    chains = []
    for i, piece in enumerate(pieces):
        chains.append((halves[i], swapped(halves[len(pieces) + i], 1, 0), None if i else top))
    for i in range(plane_bits()):
        for j, (held, got, ride) in enumerate(chains):
            send, held = fold(my_plane_rank, plane_bits() - 1 - i, held, got)
            chains[j] = (held, flipped(send, i), ride)
    for i in range(col_bits()):
        for j, (held, got, ride) in enumerate(chains):
            send, held, *ride = fold(my_col_rank, col_bits() - 1 - i, held, got, ride)
            if i == 0 and j == 0:
                send, g_lower = lax.optimization_barrier((send, g_lower))
            chains[j] = (held, swapped(send, 0, 1 << i), ride[0] if ride else None)
    g_up = shifted(g_lower, 1, 0)
    owns = []
    for piece, (held, got, ride) in zip(pieces, chains):
        own = held + got[:piece]
        parts = [own] + [swapped(own, 0, rank_by(e, range(col_bits()))) for e in range(1, n_col)]
        if ride is not None:
            parts.append(jnp.maximum(ride, got[piece:]))
        owns.append(jnp.concatenate(parts, axis=0))
    owns[0], g_up, g_right = lax.optimization_barrier((owns[0], g_up, g_right + g_up[:, :, cols:]))
    g_left = shifted(g_right, 0, 1)
    gathered = []
    for j, own in enumerate(owns):
        blocks = [own]
        for i in reversed(range(plane_bits())):
            blocks = blocks + [flipped(block, i) for block in blocks]
        if j == len(owns) - 1:
            blocks[-1], g_left = lax.optimization_barrier((blocks[-1], g_left))
        gathered.append(blocks + [swapped(block, 1, 0) for block in blocks])
    top = functools.reduce(jnp.maximum, [block[n_col * pieces[0]:] for block in gathered[0]])
    blocks = sum(gathered, [])
    return pl.pallas_call(
        functools.partial(finish_kernel, (pairs, n_col, pieces)),
        out_shape=(f32(*object_field.shape), f32(*probe.shape)),
        in_specs=[VM] * (7 + len(blocks)),
        out_specs=(ANY, ANY),
        scratch_shapes=[
            pltpu.VMEM(object_field.shape, jnp.float32),
            pltpu.VMEM(probe.shape, jnp.float32),
            pltpu.VMEM((total_rows, side), jnp.float32),
            pltpu.SemaphoreType.DMA((3,)),
        ],
        compiler_params=params(20),
        cost_estimate=cost(10**6, 10**7),
        name="update",
    )(object_field, light, top, g_tile, g_left, g_up, probe, *blocks)


def solution(mesh):
    in_specs = (
        P(None, "row", "col"),
        P(),
        P("row", "col", None, None, None),
        P("row", "col", None, None),
        P(),
    )
    out_specs = (P(None, "row", "col"), P())
    return jax.shard_map(body, mesh=mesh, in_specs=in_specs, out_specs=out_specs, check_vma=False)
```
